256 devices in a mesh: slot: 32 (over z_hi, y, core), tp: 8 (over z_lo, x).
Axes of the slice: x: 4, y: 4, z: 8 (z_hi: 4, z_lo: 2; z = z_hi * 2 + z_lo), core: 2. Of those that a mesh axis runs over, the one named last changes fastest.
Arguments:
- hidden: bfloat16 [14336, 6144], P('slot', 'tp'), may hold values from -4 to 4
- queries: bfloat16 [14336, 3072], P('slot', 'tp'), may hold values from -22 to 22
- key_rows: bfloat16 [14336, 3072], P('slot', 'tp'), may hold values from -6 to 6
- values: bfloat16 [14336, 3072], P('slot', 'tp'), may hold values from -6 to 6
- out_weight: bfloat16 [3072, 6144], P('tp'), may hold values from -0.109375 to 0.109375
- level_table: float32 [64, 6144], P(None, 'tp'), may hold values from 0.3 to 3
- noise_level: int32 [32], P('slot'), may hold values from 0 to 63
- group_live: int32 [32], replicated, may hold values 0 or 1
Outputs:
- refined: bfloat16 [14336, 6144], P('slot', 'tp')
The draws below stay inside these ranges and needn't reach their ends.
All inputs are finite; a program needn't handle non-finite values.
Results may differ from the reference program's by a relative error of at most 0.014.
Values may be sent and summed in bfloat16 or wider, within the bound.
No kernel may reach another device: no remote copies, remote signals or barrier semaphores. Data moves between devices by JAX's collectives and lax.ppermute only.
A program may use at most 128 MiB of HBM per device.

```python
import math
import jax
import jax.numpy as jnp
from jax import lax

D = 6144
HEADS = 24
HD = 128
LEVELS = 64
GROUP = 448
TOKENS = 14336
N_SLOT = 32


def draw_key_rows(key, part):
    key = jax.random.fold_in(key, 1)
    drawn_draw = jnp.clip(jax.random.normal(key, (TOKENS, HEADS * HD), jnp.float32), -6.0, 6.0)
    return drawn_draw.astype(jnp.bfloat16)


def draw_queries(key, part):
    key = jax.random.fold_in(key, 2)
    drawn_draw = jnp.clip(2.5 * jax.random.normal(key, (TOKENS, HEADS * HD), jnp.float32), -15.0, 15.0)
    return drawn_draw.astype(jnp.bfloat16)


def touch_ends(result, key, smallest, largest):
    longest = result.shape.index(max(result.shape))
    spots = []
    for shift in (0, 1):
        where = [jax.random.randint(jax.random.fold_in(key, axis), (), 0, length) for axis, length in enumerate(result.shape)]
        where[longest] = (where[longest] + shift) % result.shape[longest]
        spots.append(tuple(where))
    return result.at[spots[0]].set(smallest).at[spots[1]].set(largest)


def block_levels(key, extent, cuts, low, top_value):
    gain = 1.0
    for position, parts in cuts:
        steps = jax.random.uniform(jax.random.fold_in(jax.random.fold_in(key, 6), position), (parts,), jnp.float32, low / len(cuts), top_value / len(cuts))
        gain = gain * jnp.repeat(jnp.exp(steps), extent[position] // parts).reshape((-1,) + (1,) * (len(extent) - 1 - position))
    return gain


def noise(own_key, dims, spread, limit, pieces=(), dtype=jnp.bfloat16):
    drawn = spread * jax.random.normal(own_key, dims, jnp.float32)
    if pieces:
        drawn = drawn * block_levels(own_key, dims, pieces, -0.22, 0.18)
    return jnp.clip(drawn, -limit, limit).astype(dtype)


def setup_inputs(seed: int = 0) -> dict:
    splits = jax.random.split(jax.random.key(seed), 9)
    hidden = noise(splits[0], (TOKENS, D), 0.5, 4.0, ((0, 32), (1, 8)))
    queries = draw_queries(jax.random.fold_in(splits[8], 71), 0)
    key_rows = draw_key_rows(jax.random.fold_in(splits[8], 71), 0)
    values = noise(splits[3], (TOKENS, HEADS * HD), 1.0, 6.0, ((0, 32), (1, 8)))
    out_weight = noise(splits[4], (HEADS * HD, D), (HEADS * HD) ** -0.5, 0.109375, ((0, 8),))
    level_table = jnp.clip(jnp.exp(math.log(3.0) - 2.3025851 * jax.random.uniform(splits[5], (LEVELS, D), jnp.float32) ** block_levels(splits[5], (LEVELS, D), ((1, 8),), -0.2, 0.2)), 0.3, 3.0)
    noise_level = touch_ends(jax.random.randint(splits[6], (N_SLOT,), 0, LEVELS), jax.random.fold_in(splits[6], 1), 0, LEVELS - 1).astype(jnp.int32)
    group_live = touch_ends((jax.random.randint(splits[7], (N_SLOT,), 0, 4) < 3).astype(jnp.int32), jax.random.fold_in(splits[7], 1), 0, 1)
    return {"hidden": hidden, "queries": queries, "key_rows": key_rows, "values": values, "out_weight": out_weight, "level_table": level_table, "noise_level": noise_level, "group_live": group_live}


def reference(hidden, queries, key_rows, values, out_weight, level_table, noise_level, group_live):
    score_scale = HD ** -0.5
    pieces_out = []
    for slot_index in range(N_SLOT):
        span_end = (slot_index + 1) * GROUP
        query_part = queries[slot_index * GROUP:span_end].reshape(GROUP, HEADS, HD).transpose(1, 0, 2)
        key_part = key_rows[:span_end].reshape(span_end, HEADS, HD).transpose(1, 0, 2)
        value_part = values[:span_end].reshape(span_end, HEADS, HD).transpose(1, 0, 2)
        group_of = jnp.arange(span_end) // GROUP
        allowed = (group_live[group_of] == 1) | (group_of == slot_index)

        def one_head(operands):
            query_head, key_head, value_head = operands
            scores = jnp.dot(query_head, key_head.T, preferred_element_type=jnp.float32) * score_scale
            masked = jnp.where(allowed[None, :], scores, -1e30)
            rowmax = jnp.max(masked, axis=1, keepdims=True)
            expon = jnp.where(allowed[None, :], jnp.exp(scores - rowmax), 0.0)
            rowsum = jnp.sum(expon, axis=1, keepdims=True)
            mixed_head = jnp.dot(expon.astype(jnp.bfloat16), value_head, preferred_element_type=jnp.float32) / rowsum
            return mixed_head.astype(jnp.bfloat16)

        per_head = lax.map(one_head, (query_part, key_part, value_part))
        pieces_out.append(per_head.transpose(1, 0, 2).reshape(GROUP, HEADS * HD))
    attended = jnp.concatenate(pieces_out, axis=0)
    projected = jnp.dot(attended, out_weight, preferred_element_type=jnp.float32)
    gate_row = jnp.repeat(level_table[noise_level], GROUP, axis=0)
    mixed_out = (hidden.astype(jnp.float32) + gate_row * projected).astype(jnp.bfloat16)
    return jnp.roll(mixed_out, -GROUP, axis=0)
```

```python
import math

import jax
import jax.numpy as jnp
import numpy as np
from jax import lax
from jax.experimental import pallas as pl
from jax.experimental.pallas import tpu as pltpu
from jax.sharding import Mesh
from jax.sharding import PartitionSpec as P

HD = 128
ROWS = 448
HEADS_HERE = 3
WIDTH = HEADS_HERE * HD
STAT = 32
LOWEST = -1e30
EXP2_SCALE = HD**-0.5 * math.log2(math.e)
Y_STEPS = (0, -1, 1, 2)
SLOT = ("z", "y", "c")
VMEM_LIMIT = 48 * 1024 * 1024


def score(query, key):
    return lax.dot_general(
        query, key, (((1,), (1,)), ((), ())), preferred_element_type=jnp.float32
    )


def attend_kernel(ids, live, *refs):
    query_in, pair_in, out = refs[0:4], refs[4:12], refs[12:16]
    queries, pairs, own, acc, top, done, query_sem, pair_sem, own_sem, out_sem = refs[16:]
    level, y, core = ids[0], ids[1], ids[2]
    first = level * 8
    mine = first + y * 2 + core
    groups = []
    for other in (0, 1):
        for step in Y_STEPS:
            core_there = core if other == 0 else 1 - core
            groups.append(first + lax.rem(y + step + 4, 4) * 2 + core_there)
    alive = [live[first + k] for k in range(8)]

    def live_before(group):
        count = jnp.int32(0)
        for k in range(8):
            count = count + jnp.where(first + k < group, alive[k], 0)
        return count

    n_all = live_before(first + 8)
    n_own = live_before(mine)

    def own_copy():
        return pltpu.make_async_copy(pair_in[0], own, own_sem)

    def query_copy(d):
        return pltpu.make_async_copy(query_in[d], queries.at[d], query_sem.at[d])

    def pair_copy(p):
        place = pl.multiple_of(live_before(groups[p]) * ROWS, 64)
        return pltpu.make_async_copy(pair_in[p], pairs.at[pl.ds(place, ROWS)], pair_sem.at[p])

    own_copy().start()
    for d in range(4):
        query_copy(d).start()
    for p in range(8):

        @pl.when(live[groups[p]] == 1)
        def _():
            pair_copy(p).start()

    for d in range(4):
        query_copy(d).wait()
    own_copy().wait()
    for p in range(8):

        @pl.when(live[groups[p]] == 1)
        def _():
            pair_copy(p).wait()

    def update(d, head, key, value, rows, opening):
        query = queries[d, :, head * HD : (head + 1) * HD]
        scores = score(query, key)
        highest = jnp.max(scores, axis=1, keepdims=True)
        ones = jnp.ones((rows, HD), jnp.bfloat16)
        if opening:
            new = jnp.broadcast_to(highest, (ROWS, HD))
            weights = jnp.exp2(scores * EXP2_SCALE - highest * EXP2_SCALE)
        else:
            old = top[head]
            new = jnp.maximum(old, highest)
            shift = new * EXP2_SCALE
            if rows % HD == 0:
                shift = jnp.concatenate([shift] * (rows // HD), axis=1)
            else:
                shift = shift[:, :1]
            weights = jnp.exp2(scores * EXP2_SCALE - shift)
        weighted = jnp.dot(
            weights.astype(jnp.bfloat16),
            jnp.concatenate([value, ones], axis=1),
            preferred_element_type=jnp.float32,
        )
        if opening:
            acc[head] = weighted
        else:
            shrink = jnp.exp2((old - new) * EXP2_SCALE)
            acc[head] = acc[head] * jnp.concatenate([shrink, shrink], axis=1) + weighted
        top[head] = new

    def update_heads(d, ref, at, rows, opening):
        for head in range(HEADS_HERE):
            low = head * HD
            key = ref[at, low : low + HD]
            value = ref[at, WIDTH + low : WIDTH + low + HD]
            update(d, head, key, value, rows, opening)

    def source(d, unused):
        @pl.when(d == 0)
        def _():
            update_heads(0, own, pl.ds(0, ROWS), ROWS, True)

        @pl.when(d > 0)
        def _():
            top[...] = jnp.full(top.shape, LOWEST, jnp.float32)
            acc[...] = jnp.zeros(acc.shape, jnp.float32)

        count = jnp.where(d == 0, n_own, n_all)

        def two(t, unused_too):
            at = pl.ds(pl.multiple_of(t * 2 * ROWS, HD), 2 * ROWS)
            update_heads(d, pairs, at, 2 * ROWS, False)
            return 0

        lax.fori_loop(0, count // 2, two, 0)

        @pl.when(count % 2 == 1)
        def _():
            at = pl.ds(pl.multiple_of((count - 1) * ROWS, 64), ROWS)
            update_heads(d, pairs, at, ROWS, False)

        lane = lax.broadcasted_iota(jnp.int32, (ROWS, HD), 1)
        stats = jnp.zeros((ROWS, HD), jnp.float32)
        for head in range(HEADS_HERE):
            exact = top[head]
            sent = exact.astype(jnp.bfloat16).astype(jnp.float32)
            factor = jnp.exp2((exact - sent) * EXP2_SCALE)
            both = acc[head]
            done[d, 0:ROWS, head * HD : (head + 1) * HD] = (both[:, :HD] * factor).astype(
                jnp.bfloat16
            )
            total = both[:, HD:] * factor
            high = total.astype(jnp.bfloat16).astype(jnp.float32)
            stats = jnp.where(lane == head, sent, stats)
            stats = jnp.where(lane == HEADS_HERE + head, high, stats)
            stats = jnp.where(lane == 2 * HEADS_HERE + head, total - high, stats)
        flat = jnp.transpose(stats)[:16].astype(jnp.bfloat16)
        done[d, ROWS : ROWS + 16, :] = flat[:, :WIDTH]
        rest = jnp.zeros((16, 2 * WIDTH - ROWS), jnp.bfloat16)
        done[d, ROWS + 16 : ROWS + 32, :] = jnp.concatenate([flat[:, WIDTH:], rest], axis=1)
        return 0

    lax.fori_loop(0, 4 - level, source, 0)
    for d in range(4):
        pltpu.make_async_copy(done.at[d], out[d], out_sem.at[d]).start()
    for d in range(4):
        pltpu.make_async_copy(done.at[d], out[d], out_sem.at[d]).wait()


def attend(ids, live, queries, pairs):
    smem = pl.BlockSpec(memory_space=pltpu.SMEM)
    anywhere = pl.BlockSpec(memory_space=pl.ANY)
    bf16, f32 = jnp.bfloat16, jnp.float32
    return pl.pallas_call(
        attend_kernel,
        out_shape=[jax.ShapeDtypeStruct((ROWS + STAT, WIDTH), bf16)] * 4,
        in_specs=[smem, smem] + [anywhere] * 12,
        out_specs=[anywhere] * 4,
        scratch_shapes=[
            pltpu.VMEM((4, ROWS, WIDTH), bf16),
            pltpu.VMEM((8 * ROWS, 2 * WIDTH), bf16),
            pltpu.VMEM((ROWS, 2 * WIDTH), bf16),
            pltpu.VMEM((HEADS_HERE, ROWS, 2 * HD), f32),
            pltpu.VMEM((HEADS_HERE, ROWS, HD), f32),
            pltpu.VMEM((4, ROWS + STAT, WIDTH), bf16),
            pltpu.SemaphoreType.DMA((4,)),
            pltpu.SemaphoreType.DMA((8,)),
            pltpu.SemaphoreType.DMA,
            pltpu.SemaphoreType.DMA((4,)),
        ],
        compiler_params=pltpu.CompilerParams(vmem_limit_bytes=VMEM_LIMIT),
        name="attend",
    )(ids, live, *queries, *pairs)


def combine_kernel(ids, *refs):
    parts, out = refs[0:4], refs[4]
    home = ids[3]
    maxima, sums = [], []
    for d in range(4):
        tail = parts[d][ROWS : ROWS + STAT, :].astype(jnp.float32)
        flat = jnp.concatenate([tail[0:16], tail[16:32, : ROWS - WIDTH]], axis=1)
        stats = jnp.transpose(jnp.concatenate([flat, jnp.zeros((HD - 16, ROWS), jnp.float32)]))
        present = d <= home
        row_max, row_sum = [], []
        for head in range(HEADS_HERE):
            total = (
                stats[:, HEADS_HERE + head : HEADS_HERE + head + 1]
                + stats[:, 2 * HEADS_HERE + head : 2 * HEADS_HERE + head + 1]
            )
            row_max.append(jnp.where(present, stats[:, head : head + 1], LOWEST))
            row_sum.append(total)
        maxima.append(row_max)
        sums.append(row_sum)
    for head in range(HEADS_HERE):
        at = slice(head * HD, (head + 1) * HD)
        highest = maxima[0][head]
        for d in range(1, 4):
            highest = jnp.maximum(highest, maxima[d][head])
        numerator = jnp.zeros((ROWS, HD), jnp.float32)
        denominator = jnp.zeros((ROWS, 1), jnp.float32)
        for d in range(4):
            factor = jnp.exp2((maxima[d][head] - highest) * EXP2_SCALE)
            numerator = numerator + parts[d][0:ROWS, at].astype(jnp.float32) * factor
            denominator = denominator + sums[d][head] * factor
        out[:, at] = (numerator / denominator).astype(jnp.bfloat16)


def combine(ids, parts):
    vmem = pl.BlockSpec(memory_space=pltpu.VMEM)
    return pl.pallas_call(
        combine_kernel,
        out_shape=jax.ShapeDtypeStruct((ROWS, WIDTH), jnp.bfloat16),
        in_specs=[pl.BlockSpec(memory_space=pltpu.SMEM)] + [vmem] * 4,
        out_specs=vmem,
        compiler_params=pltpu.CompilerParams(vmem_limit_bytes=VMEM_LIMIT),
        name="combine",
    )(ids, *parts)


def around(value, axis, steps):
    count = lax.axis_size(axis)
    return lax.ppermute(value, axis, [(i, (i + steps) % count) for i in range(count)])


def per_device(hidden, queries, key_rows, values, out_weight, level_table, noise_level, group_live):
    z, y, core = lax.axis_index("z"), lax.axis_index("y"), lax.axis_index("c")
    w, x = lax.axis_index("w"), lax.axis_index("x")
    slot = z * 8 + y * 2 + core
    home = lax.rem(slot + 1, 32) // 8
    ids = jnp.stack([z, y, core, home]).astype(jnp.int32)

    pair = jnp.concatenate([key_rows, values], axis=1)
    pairs = [pair] + [around(pair, "y", -step) for step in Y_STEPS[1:]]
    pairs = pairs + [around(p, "c", 1) for p in pairs]
    sources = [queries] + [
        lax.ppermute(queries, "z", [(i, i - d) for i in range(d, 4)]) for d in (1, 2, 3)
    ]

    part = out_weight.shape[1] // 8
    pieces = []
    for step in range(4):
        there = lax.rem(x + step, 4)
        near = lax.dynamic_slice_in_dim(out_weight, (w * 4 + there) * part, part, 1)
        far = lax.dynamic_slice_in_dim(out_weight, ((1 - w) * 4 + there) * part, part, 1)
        piece = jnp.concatenate([near, far], axis=1)
        pieces.append(piece if step == 0 else around(piece, "x", step))
    weight = jnp.concatenate(pieces, axis=0)

    hidden_next = around(hidden, SLOT, -1)
    level_next = around(noise_level, SLOT, -1)

    shares = attend(ids, group_live, sources, pairs)
    back = []
    for d in range(4):
        pairs_back = [
            (8 * (i - d) + j, (8 * i + j - 1) % 32) for i in range(d, 4) for j in range(8)
        ]
        back.append(lax.ppermute(shares[d], SLOT, pairs_back))
    attended = combine(ids, back)

    gathered = [attended] + [around(attended, "x", step) for step in (1, 2, 3)]
    rows = jnp.concatenate(gathered, axis=1)
    far_sum = jnp.dot(rows, weight[:, part:], preferred_element_type=jnp.float32)
    arrived = around(far_sum.astype(jnp.bfloat16), "w", 1)
    near_sum = jnp.dot(rows, weight[:, :part], preferred_element_type=jnp.float32)
    projected = near_sum + arrived.astype(jnp.float32)
    gate_row = lax.dynamic_slice_in_dim(level_table, level_next[0], 1, 0)
    return (hidden_next.astype(jnp.float32) + gate_row * projected).astype(jnp.bfloat16)


def solution(mesh):
    fine = Mesh(np.asarray(mesh.devices).reshape(4, 4, 2, 2, 4), ("z", "y", "c", "w", "x"))
    tp = ("w", "x")
    block = P(SLOT, tp)
    in_specs = (block, block, block, block, P(tp, None), P(None, tp), P(SLOT), P())
    return jax.shard_map(
        per_device, mesh=fine, in_specs=in_specs, out_specs=block, check_vma=False
    )
```

```python
import functools
import math

import jax
import jax.numpy as jnp
import numpy as np
from jax import lax
from jax.experimental import pallas as pl
from jax.experimental.pallas import tpu as pltpu
from jax.sharding import Mesh
from jax.sharding import PartitionSpec as P

HD = 128
ROWS = 448
HEADS_HERE = 3
WIDTH = HEADS_HERE * HD
STAT = 32
LOWEST = -1e30
EXP2_SCALE = HD**-0.5 * math.log2(math.e)
Y_STEPS = (0, -1, 1, 2)
SLOT = ("z", "y", "c")
VMEM_LIMIT = 48 * 1024 * 1024


def score(query, key):
    return lax.dot_general(
        query, key, (((1,), (1,)), ((), ())), preferred_element_type=jnp.float32
    )


def attend_kernel(steps, ids, live, level, *refs):
    many = len(steps)
    query_in, pair_in, out = refs[0:many], refs[many : many + 8], refs[many + 8 : 2 * many + 8]
    raw, scaled, pairs, own, acc, top, done, raw_sem, pair_sem, own_sem, out_sem = refs[2 * many + 8 :]
    here, y, core = ids[0], ids[1], ids[2]
    first = here * 8
    mine = first + y * 2 + core
    groups = []
    for other in (0, 1):
        for step in Y_STEPS:
            core_there = core if other == 0 else 1 - core
            groups.append(first + lax.rem(y + step + 4, 4) * 2 + core_there)
    alive = [live[first + k] for k in range(8)]

    def live_before(group):
        count = jnp.int32(0)
        for k in range(8):
            count = count + jnp.where(first + k < group, alive[k], 0)
        return count

    bound = mine if steps == (0,) else first + 8
    count = live_before(bound)
    active = [here + step <= 3 for step in steps]
    some = here + min(steps) <= 3

    def raw_copy(i):
        return pltpu.make_async_copy(query_in[i], raw.at[i], raw_sem.at[i])

    def own_copy():
        return pltpu.make_async_copy(pair_in[0], own, own_sem)

    def place_copy(p, place):
        at = pl.ds(pl.multiple_of(place * ROWS, 64), ROWS)
        return pltpu.make_async_copy(pair_in[p], pairs.at[at], pair_sem.at[place])

    def wait_place(place):
        place_copy(0, place).wait()

    @pl.when(some)
    def _():
        for i in range(many):
            raw_copy(i).start()
        if steps == (0,):
            own_copy().start()
        for p in range(8):

            @pl.when((live[groups[p]] == 1) & (groups[p] < bound))
            def _():
                place_copy(p, live_before(groups[p])).start()

        for i in range(many):
            raw_copy(i).wait()

    def update_heads(ref, at, rows, opening):
        ones = jnp.ones((rows, HD), jnp.bfloat16)

        def scores_of(head):
            key = ref[at, head * HD : (head + 1) * HD]
            return score(scaled[head], jnp.concatenate([key, key], axis=1))

        def absorb(head, scores):
            highest = jnp.max(scores, axis=1, keepdims=True)
            if opening:
                new = jnp.broadcast_to(highest, (ROWS, HD))
                weights = jnp.exp2(scores - highest)
            else:
                old = top[head]
                new = jnp.maximum(old, highest)
                if rows % HD == 0:
                    shift = jnp.concatenate([new] * (rows // HD), axis=1)
                else:
                    shift = new[:, :1]
                weights = jnp.exp2(scores - shift)
            value = ref[at, WIDTH + head * HD : WIDTH + (head + 1) * HD]
            weighted = jnp.dot(
                weights.astype(jnp.bfloat16),
                jnp.concatenate([value, ones], axis=1),
                preferred_element_type=jnp.float32,
            )
            if opening:
                acc[head] = weighted
            else:
                shrink = jnp.exp2(old - new)
                acc[head] = acc[head] * jnp.concatenate([shrink, shrink], axis=1) + weighted
            top[head] = new

        scores = scores_of(0)
        for head in range(HEADS_HERE):
            following = scores_of(head + 1) if head + 1 < HEADS_HERE else None
            absorb(head, scores)
            scores = following

    def sweep(fresh):
        def four(t, unused):
            @pl.when(fresh)
            def _():
                for k in range(4):
                    wait_place(t * 4 + k)

            update_heads(pairs, pl.ds(pl.multiple_of(t * 4 * ROWS, HD), 4 * ROWS), 4 * ROWS, False)
            return 0

        lax.fori_loop(0, count // 4, four, 0)
        rest = count % 4
        base = count - rest

        @pl.when(fresh)
        def _():
            for k in range(3):

                @pl.when(k < rest)
                def _():
                    wait_place(base + k)

        @pl.when(rest >= 2)
        def _():
            update_heads(pairs, pl.ds(pl.multiple_of(base * ROWS, HD), 2 * ROWS), 2 * ROWS, False)

        @pl.when(rest % 2 == 1)
        def _():
            update_heads(pairs, pl.ds(pl.multiple_of((count - 1) * ROWS, 64), ROWS), ROWS, False)

    def source(i, fresh):
        for head in range(HEADS_HERE):
            exact = raw[i, :, head * HD : (head + 1) * HD].astype(jnp.float32) * EXP2_SCALE
            high = exact.astype(jnp.bfloat16)
            scaled[head, :, :HD] = high
            scaled[head, :, HD:] = (exact - high.astype(jnp.float32)).astype(jnp.bfloat16)
        if steps == (0,):
            own_copy().wait()
            update_heads(own, pl.ds(0, ROWS), ROWS, True)
        else:
            top[...] = jnp.full(top.shape, LOWEST, jnp.float32)
            acc[...] = jnp.zeros(acc.shape, jnp.float32)
        sweep(fresh)
        lane = lax.broadcasted_iota(jnp.int32, (ROWS, HD), 1)
        stats = jnp.where(lane == 3 * HEADS_HERE, level[0].astype(jnp.float32), 0.0)
        for head in range(HEADS_HERE):
            exact = top[head]
            sent = exact.astype(jnp.bfloat16).astype(jnp.float32)
            factor = jnp.exp2(exact - sent)
            both = acc[head]
            done[i, 0:ROWS, head * HD : (head + 1) * HD] = (both[:, :HD] * factor).astype(
                jnp.bfloat16
            )
            total = both[:, HD:] * factor
            high = total.astype(jnp.bfloat16).astype(jnp.float32)
            stats = jnp.where(lane == head, sent, stats)
            stats = jnp.where(lane == HEADS_HERE + head, high, stats)
            stats = jnp.where(lane == 2 * HEADS_HERE + head, total - high, stats)
        flat = jnp.transpose(stats)[:16].astype(jnp.bfloat16)
        done[i, ROWS : ROWS + 16, :] = flat[:, :WIDTH]
        pad = jnp.zeros((16, 2 * WIDTH - ROWS), jnp.bfloat16)
        done[i, ROWS + 16 : ROWS + 32, :] = jnp.concatenate([flat[:, WIDTH:], pad], axis=1)

    if many == 1:

        @pl.when(active[0])
        def _():
            source(0, True)

    else:

        def one(i, unused):
            step = steps[0] - i
            before = here + step + 1 <= 3

            @pl.when(here + step <= 3)
            def _():
                source(i, jnp.logical_or(i == 0, jnp.logical_not(before)))

            return 0

        lax.fori_loop(0, many, one, 0)

    for i in range(many):

        @pl.when(active[i])
        def _():
            pltpu.make_async_copy(done.at[i], out[i], out_sem.at[i]).start()

    for i in range(many):

        @pl.when(active[i])
        def _():
            pltpu.make_async_copy(done.at[i], out[i], out_sem.at[i]).wait()


def attend(steps, ids, live, level, queries, pairs):
    smem = pl.BlockSpec(memory_space=pltpu.SMEM)
    anywhere = pl.BlockSpec(memory_space=pl.ANY)
    bf16, f32 = jnp.bfloat16, jnp.float32
    many = len(steps)
    return pl.pallas_call(
        functools.partial(attend_kernel, steps),
        out_shape=[jax.ShapeDtypeStruct((ROWS + STAT, WIDTH), bf16)] * many,
        in_specs=[smem] * 3 + [anywhere] * (many + 8),
        out_specs=[anywhere] * many,
        scratch_shapes=[
            pltpu.VMEM((many, ROWS, WIDTH), bf16),
            pltpu.VMEM((HEADS_HERE, ROWS, 2 * HD), bf16),
            pltpu.VMEM((8 * ROWS, 2 * WIDTH), bf16),
            pltpu.VMEM((ROWS, 2 * WIDTH), bf16),
            pltpu.VMEM((HEADS_HERE, ROWS, 2 * HD), f32),
            pltpu.VMEM((HEADS_HERE, ROWS, HD), f32),
            pltpu.VMEM((many, ROWS + STAT, WIDTH), bf16),
            pltpu.SemaphoreType.DMA((many,)),
            pltpu.SemaphoreType.DMA((8,)),
            pltpu.SemaphoreType.DMA,
            pltpu.SemaphoreType.DMA((many,)),
        ],
        compiler_params=pltpu.CompilerParams(vmem_limit_bytes=VMEM_LIMIT),
        cost_estimate=pl.CostEstimate(
            flops=many * 8 * 3 * ROWS * ROWS * HD * 16, bytes_accessed=6000000, transcendentals=0
        ),
        name="attend",
    )(ids, live, level, *queries, *pairs)


def combine_kernel(ids, table, *refs):
    parts, out, gate = refs[0:4], refs[4], refs[5]
    home = ids[3]
    maxima, sums = [], []
    for d in range(4):
        tail = parts[d][ROWS : ROWS + STAT, :].astype(jnp.float32)
        flat = jnp.concatenate([tail[0:16], tail[16:32, : ROWS - WIDTH]], axis=1)
        if d == 0:
            noise = flat[3 * HEADS_HERE : 3 * HEADS_HERE + 1, 0:1]
        stats = jnp.transpose(jnp.concatenate([flat, jnp.zeros((HD - 16, ROWS), jnp.float32)]))
        present = d <= home
        row_max, row_sum = [], []
        for head in range(HEADS_HERE):
            total = (
                stats[:, HEADS_HERE + head : HEADS_HERE + head + 1]
                + stats[:, 2 * HEADS_HERE + head : 2 * HEADS_HERE + head + 1]
            )
            row_max.append(jnp.where(present, stats[:, head : head + 1], LOWEST))
            row_sum.append(jnp.where(present, total, 0.0))
        maxima.append(row_max)
        sums.append(row_sum)
    for head in range(HEADS_HERE):
        at = slice(head * HD, (head + 1) * HD)
        highest = maxima[0][head]
        for d in range(1, 4):
            highest = jnp.maximum(highest, maxima[d][head])
        numerator = jnp.zeros((ROWS, HD), jnp.float32)
        denominator = jnp.zeros((ROWS, 1), jnp.float32)
        for d in range(4):
            factor = jnp.exp2(maxima[d][head] - highest)
            share = jnp.where(d <= home, parts[d][0:ROWS, at].astype(jnp.float32), 0.0)
            numerator = numerator + share * factor
            denominator = denominator + sums[d][head] * factor
        out[:, at] = (numerator / denominator).astype(jnp.bfloat16)
    index = lax.broadcasted_iota(jnp.int32, table.shape, 0).astype(jnp.float32)
    gate[...] = jnp.sum(jnp.where(index == noise, table[...], 0.0), axis=0, keepdims=True)


def combine(ids, table, parts):
    vmem = pl.BlockSpec(memory_space=pltpu.VMEM)
    return pl.pallas_call(
        combine_kernel,
        out_shape=[
            jax.ShapeDtypeStruct((ROWS, WIDTH), jnp.bfloat16),
            jax.ShapeDtypeStruct((1, table.shape[1]), jnp.float32),
        ],
        in_specs=[pl.BlockSpec(memory_space=pltpu.SMEM)] + [vmem] * 5,
        out_specs=[vmem] * 2,
        compiler_params=pltpu.CompilerParams(vmem_limit_bytes=VMEM_LIMIT),
        name="combine",
    )(ids, table, *parts)


def project_kernel(far, ids, *refs):
    rows, own, fetched, swapped, out, held, sem = refs[0:4], refs[4], refs[5], refs[6], refs[7], refs[8], refs[9]
    mine = ids[2] == (1 if far else 0)

    @pl.when(mine)
    def _():
        pltpu.make_async_copy(fetched, held, sem).start()

    @pl.when(jnp.logical_not(mine))
    def _():
        pltpu.make_async_copy(swapped, held, sem).start()

    total = jnp.dot(rows[0][...], own[...], preferred_element_type=jnp.float32)
    pltpu.make_async_copy(fetched, held, sem).wait()
    for k in range(3):
        total = total + jnp.dot(rows[k + 1][...], held[k], preferred_element_type=jnp.float32)
    out[...] = total.astype(out.dtype)


def project(far, ids, rows, own, fetched, swapped):
    vmem = pl.BlockSpec(memory_space=pltpu.VMEM)
    anywhere = pl.BlockSpec(memory_space=pl.ANY)
    part = own.shape[1]
    return pl.pallas_call(
        functools.partial(project_kernel, far),
        out_shape=jax.ShapeDtypeStruct((ROWS, part), jnp.bfloat16 if far else jnp.float32),
        in_specs=[pl.BlockSpec(memory_space=pltpu.SMEM)] + [vmem] * 5 + [anywhere] * 2,
        out_specs=vmem,
        scratch_shapes=[pltpu.VMEM((3, WIDTH, part), jnp.bfloat16), pltpu.SemaphoreType.DMA],
        compiler_params=pltpu.CompilerParams(vmem_limit_bytes=VMEM_LIMIT),
        cost_estimate=pl.CostEstimate(
            flops=8 * ROWS * WIDTH * part, bytes_accessed=5000000, transcendentals=0
        ),
        name="project",
    )(ids, *rows, own, fetched, swapped)


def after(value, *earlier):
    return lax.optimization_barrier((value, *earlier))[0]


def around(value, axis, steps):
    count = lax.axis_size(axis)
    return lax.ppermute(value, axis, [(i, (i + steps) % count) for i in range(count)])


def per_device(hidden, queries, key_rows, values, out_weight, level_table, noise_level, group_live):
    z, y, core = lax.axis_index("z"), lax.axis_index("y"), lax.axis_index("c")
    w, x = lax.axis_index("w"), lax.axis_index("x")
    slot = z * 8 + y * 2 + core
    home = lax.rem(slot + 1, 32) // 8
    ids = jnp.stack([z, y, core, home]).astype(jnp.int32)

    def to_level(value, d):
        return lax.ppermute(value, "z", [(i, i - d) for i in range(d, 4)])

    pair = jnp.concatenate([key_rows, values], axis=1)
    next_one, next_two = to_level(queries, 1), to_level(queries, 2)
    below, above, across = [around(pair, "y", -step) for step in Y_STEPS[1:]]
    next_three = to_level(after(queries, next_one), 3)
    pairs = [pair, below, above, across]
    pairs = pairs + [around(after(p, below), "c", 1) for p in pairs]

    part = out_weight.shape[1] // 8

    def columns(owner):
        return lax.dynamic_slice_in_dim(out_weight, owner * part, part, 1)

    weight_near, weight_far = columns(w * 4 + x), columns((1 - w) * 4 + x)
    block = jnp.where(core == 0, w, 1 - w) * 4
    fetched = []
    for step, ready in ((1, below), (2, across), (3, above)):
        piece = after(columns(block + lax.rem(x + step, 4)), ready)
        fetched.append(around(piece, "x", step))
    fetched = jnp.stack(fetched)
    swapped = around(fetched, "c", 1)

    hidden_next = around(after(hidden, across), SLOT, -1)

    def back(share, d):
        pairs_back = [
            (8 * (i - d) + j, (8 * i + j - 1) % 32) for i in range(d, 4) for j in range(8)
        ]
        return lax.ppermute(share, SLOT, pairs_back)

    two, one = attend((2, 1), ids, group_live, noise_level, [next_two, next_one], pairs)
    back_two, back_one = back(two, 2), back(one, 1)
    (three,) = attend((3,), ids, after(group_live, one), noise_level, [next_three], pairs)
    back_three = back(three, 3)
    (zero,) = attend((0,), ids, after(group_live, three), noise_level, [queries], pairs)
    back_zero = back(zero, 0)
    attended, gate_row = combine(ids, level_table, [back_zero, back_one, back_two, back_three])

    rows = [attended] + [around(attended, "x", step) for step in (1, 2, 3)]
    far_sum = project(True, ids, rows, weight_far, fetched, swapped)
    arrived = around(far_sum, "w", 1)
    near_sum = project(False, ids, rows, weight_near, fetched, swapped)
    projected = near_sum + arrived.astype(jnp.float32)
    return (hidden_next.astype(jnp.float32) + gate_row * projected).astype(jnp.bfloat16)


def solution(mesh):
    fine = Mesh(np.asarray(mesh.devices).reshape(4, 4, 2, 2, 4), ("z", "y", "c", "w", "x"))
    tp = ("w", "x")
    block = P(SLOT, tp)
    in_specs = (block, block, block, block, P(tp, None), P(None, tp), P(SLOT), P())
    return jax.shard_map(
        per_device, mesh=fine, in_specs=in_specs, out_specs=block, check_vma=False
    )
```

```python
import functools
import math

import jax
import jax.numpy as jnp
import numpy as np
from jax import lax
from jax.experimental import pallas as pl
from jax.experimental.pallas import tpu as pltpu
from jax.sharding import Mesh
from jax.sharding import PartitionSpec as P

HD = 128
ROWS = 448
HEADS_HERE = 3
WIDTH = HEADS_HERE * HD
STAT = 32
LOWEST = -1e30
EXP2_SCALE = HD**-0.5 * math.log2(math.e)
Y_STEPS = (0, -1, 1, 2)
SLOT = ("z", "y", "c")
VMEM_LIMIT = 48 * 1024 * 1024


def score(query, key):
    return lax.dot_general(
        query, key, (((1,), (1,)), ((), ())), preferred_element_type=jnp.float32
    )


def attend_kernel(steps, ids, live, level, *refs):
    many = len(steps)
    query_in, pair_in, out = refs[0:many], refs[many : many + 8], refs[many + 8 : 2 * many + 8]
    raw, scaled, pairs, own, acc, top, done, raw_sem, pair_sem, own_sem, out_sem = refs[2 * many + 8 :]
    here, y, core = ids[0], ids[1], ids[2]
    first = here * 8
    mine = first + y * 2 + core
    groups = []
    for other in (0, 1):
        for step in Y_STEPS:
            core_there = core if other == 0 else 1 - core
            groups.append(first + lax.rem(y + step + 4, 4) * 2 + core_there)
    alive = [live[first + k] for k in range(8)]

    def live_before(group):
        count = jnp.int32(0)
        for k in range(8):
            count = count + jnp.where(first + k < group, alive[k], 0)
        return count

    bound = mine if steps == (0,) else first + 8
    count = live_before(bound)
    active = [here + step <= 3 for step in steps]
    some = here + min(steps) <= 3

    def raw_copy(i):
        return pltpu.make_async_copy(query_in[i], raw.at[i], raw_sem.at[i])

    def own_copy():
        return pltpu.make_async_copy(pair_in[0], own, own_sem)

    def place_copy(p, place):
        at = pl.ds(pl.multiple_of(place * ROWS, 64), ROWS)
        return pltpu.make_async_copy(pair_in[p], pairs.at[at], pair_sem.at[place])

    def wait_place(place):
        place_copy(0, place).wait()

    @pl.when(some)
    def _():
        for i in range(many):
            raw_copy(i).start()
        if steps == (0,):
            own_copy().start()
        for p in range(8):

            @pl.when((live[groups[p]] == 1) & (groups[p] < bound))
            def _():
                place_copy(p, live_before(groups[p])).start()

        for i in range(many):
            raw_copy(i).wait()

    def update_heads(ref, at, rows, opening):
        ones = jnp.ones((rows, HD), jnp.bfloat16)

        def scores_of(head):
            key = ref[at, head * HD : (head + 1) * HD]
            return score(scaled[head], jnp.concatenate([key, key], axis=1))

        def absorb(head, scores):
            highest = jnp.max(scores, axis=1, keepdims=True)
            if opening:
                new = jnp.broadcast_to(highest, (ROWS, HD))
                weights = jnp.exp2(scores - highest)
            else:
                old = top[head]
                new = jnp.maximum(old, highest)
                if rows % HD == 0:
                    shift = jnp.concatenate([new] * (rows // HD), axis=1)
                else:
                    shift = new[:, :1]
                weights = jnp.exp2(scores - shift)
            value = ref[at, WIDTH + head * HD : WIDTH + (head + 1) * HD]
            weighted = jnp.dot(
                weights.astype(jnp.bfloat16),
                jnp.concatenate([value, ones], axis=1),
                preferred_element_type=jnp.float32,
            )
            if opening:
                acc[head] = weighted
            else:
                shrink = jnp.exp2(old - new)
                acc[head] = acc[head] * jnp.concatenate([shrink, shrink], axis=1) + weighted
            top[head] = new

        scores = scores_of(0)
        for head in range(HEADS_HERE):
            following = scores_of(head + 1) if head + 1 < HEADS_HERE else None
            absorb(head, scores)
            scores = following

    def sweep(fresh):
        def four(t, unused):
            @pl.when(fresh)
            def _():
                for k in range(4):
                    wait_place(t * 4 + k)

            update_heads(pairs, pl.ds(pl.multiple_of(t * 4 * ROWS, HD), 4 * ROWS), 4 * ROWS, False)
            return 0

        lax.fori_loop(0, count // 4, four, 0)
        rest = count % 4
        base = count - rest

        @pl.when(fresh)
        def _():
            for k in range(3):

                @pl.when(k < rest)
                def _():
                    wait_place(base + k)

        @pl.when(rest >= 2)
        def _():
            update_heads(pairs, pl.ds(pl.multiple_of(base * ROWS, HD), 2 * ROWS), 2 * ROWS, False)

        @pl.when(rest % 2 == 1)
        def _():
            update_heads(pairs, pl.ds(pl.multiple_of((count - 1) * ROWS, 64), ROWS), ROWS, False)

    def source(i, fresh):
        for head in range(HEADS_HERE):
            exact = raw[i, :, head * HD : (head + 1) * HD].astype(jnp.float32) * EXP2_SCALE
            high = exact.astype(jnp.bfloat16)
            scaled[head, :, :HD] = high
            scaled[head, :, HD:] = (exact - high.astype(jnp.float32)).astype(jnp.bfloat16)
        if steps == (0,):
            own_copy().wait()
            update_heads(own, pl.ds(0, ROWS), ROWS, True)
        else:
            top[...] = jnp.full(top.shape, LOWEST, jnp.float32)
            acc[...] = jnp.zeros(acc.shape, jnp.float32)
        sweep(fresh)
        lane = lax.broadcasted_iota(jnp.int32, (ROWS, HD), 1)
        stats = jnp.where(lane == 3 * HEADS_HERE, level[0].astype(jnp.float32), 0.0)
        for head in range(HEADS_HERE):
            exact = top[head]
            sent = exact.astype(jnp.bfloat16).astype(jnp.float32)
            factor = jnp.exp2(exact - sent)
            both = acc[head]
            done[i, 0:ROWS, head * HD : (head + 1) * HD] = (both[:, :HD] * factor).astype(
                jnp.bfloat16
            )
            total = both[:, HD:] * factor
            high = total.astype(jnp.bfloat16).astype(jnp.float32)
            stats = jnp.where(lane == head, sent, stats)
            stats = jnp.where(lane == HEADS_HERE + head, high, stats)
            stats = jnp.where(lane == 2 * HEADS_HERE + head, total - high, stats)
        flat = jnp.transpose(stats)[:16].astype(jnp.bfloat16)
        done[i, ROWS : ROWS + 16, :] = flat[:, :WIDTH]
        pad = jnp.zeros((16, 2 * WIDTH - ROWS), jnp.bfloat16)
        done[i, ROWS + 16 : ROWS + 32, :] = jnp.concatenate([flat[:, WIDTH:], pad], axis=1)

    if many == 1:

        @pl.when(active[0])
        def _():
            source(0, True)

    else:

        def one(i, unused):
            step = steps[0] - i
            before = here + step + 1 <= 3

            @pl.when(here + step <= 3)
            def _():
                source(i, jnp.logical_or(i == 0, jnp.logical_not(before)))

            return 0

        lax.fori_loop(0, many, one, 0)

    for i in range(many):

        @pl.when(active[i])
        def _():
            pltpu.make_async_copy(done.at[i], out[i], out_sem.at[i]).start()

    for i in range(many):

        @pl.when(active[i])
        def _():
            pltpu.make_async_copy(done.at[i], out[i], out_sem.at[i]).wait()


def attend(steps, ids, live, level, queries, pairs):
    smem = pl.BlockSpec(memory_space=pltpu.SMEM)
    anywhere = pl.BlockSpec(memory_space=pl.ANY)
    bf16, f32 = jnp.bfloat16, jnp.float32
    many = len(steps)
    return pl.pallas_call(
        functools.partial(attend_kernel, steps),
        out_shape=[jax.ShapeDtypeStruct((ROWS + STAT, WIDTH), bf16)] * many,
        in_specs=[smem] * 3 + [anywhere] * (many + 8),
        out_specs=[anywhere] * many,
        scratch_shapes=[
            pltpu.VMEM((many, ROWS, WIDTH), bf16),
            pltpu.VMEM((HEADS_HERE, ROWS, 2 * HD), bf16),
            pltpu.VMEM((8 * ROWS, 2 * WIDTH), bf16),
            pltpu.VMEM((ROWS, 2 * WIDTH), bf16),
            pltpu.VMEM((HEADS_HERE, ROWS, 2 * HD), f32),
            pltpu.VMEM((HEADS_HERE, ROWS, HD), f32),
            pltpu.VMEM((many, ROWS + STAT, WIDTH), bf16),
            pltpu.SemaphoreType.DMA((many,)),
            pltpu.SemaphoreType.DMA((8,)),
            pltpu.SemaphoreType.DMA,
            pltpu.SemaphoreType.DMA((many,)),
        ],
        compiler_params=pltpu.CompilerParams(vmem_limit_bytes=VMEM_LIMIT),
        cost_estimate=pl.CostEstimate(
            flops=many * 8 * 3 * ROWS * ROWS * HD * 16, bytes_accessed=6000000, transcendentals=0
        ),
        name="attend",
    )(ids, live, level, *queries, *pairs)


def combine_kernel(ids, table, *refs):
    parts, out, gate = refs[0:4], refs[4], refs[5]
    home = ids[3]
    maxima, sums = [], []
    for d in range(4):
        tail = parts[d][ROWS : ROWS + STAT, :].astype(jnp.float32)
        flat = jnp.concatenate([tail[0:16], tail[16:32, : ROWS - WIDTH]], axis=1)
        if d == 0:
            noise = flat[3 * HEADS_HERE : 3 * HEADS_HERE + 1, 0:1]
        stats = jnp.transpose(jnp.concatenate([flat, jnp.zeros((HD - 16, ROWS), jnp.float32)]))
        present = d <= home
        row_max, row_sum = [], []
        for head in range(HEADS_HERE):
            total = (
                stats[:, HEADS_HERE + head : HEADS_HERE + head + 1]
                + stats[:, 2 * HEADS_HERE + head : 2 * HEADS_HERE + head + 1]
            )
            row_max.append(jnp.where(present, stats[:, head : head + 1], LOWEST))
            row_sum.append(jnp.where(present, total, 0.0))
        maxima.append(row_max)
        sums.append(row_sum)
    for head in range(HEADS_HERE):
        at = slice(head * HD, (head + 1) * HD)
        highest = maxima[0][head]
        for d in range(1, 4):
            highest = jnp.maximum(highest, maxima[d][head])
        numerator = jnp.zeros((ROWS, HD), jnp.float32)
        denominator = jnp.zeros((ROWS, 1), jnp.float32)
        for d in range(4):
            factor = jnp.exp2(maxima[d][head] - highest)
            share = jnp.where(d <= home, parts[d][0:ROWS, at].astype(jnp.float32), 0.0)
            numerator = numerator + share * factor
            denominator = denominator + sums[d][head] * factor
        out[:, at] = (numerator / denominator).astype(jnp.bfloat16)
    index = lax.broadcasted_iota(jnp.int32, table.shape, 0).astype(jnp.float32)
    gate[...] = jnp.sum(jnp.where(index == noise, table[...], 0.0), axis=0, keepdims=True)


def combine(ids, table, parts):
    vmem = pl.BlockSpec(memory_space=pltpu.VMEM)
    return pl.pallas_call(
        combine_kernel,
        out_shape=[
            jax.ShapeDtypeStruct((ROWS, WIDTH), jnp.bfloat16),
            jax.ShapeDtypeStruct((1, table.shape[1]), jnp.float32),
        ],
        in_specs=[pl.BlockSpec(memory_space=pltpu.SMEM)] + [vmem] * 5,
        out_specs=[vmem] * 2,
        compiler_params=pltpu.CompilerParams(vmem_limit_bytes=VMEM_LIMIT),
        name="combine",
    )(ids, table, *parts)


def project_kernel(far, ids, *refs):
    rows, own, fetched, swapped, out, held, sem = refs[0:4], refs[4], refs[5], refs[6], refs[7], refs[8], refs[9]
    mine = ids[2] == (1 if far else 0)

    @pl.when(mine)
    def _():
        pltpu.make_async_copy(fetched, held, sem).start()

    @pl.when(jnp.logical_not(mine))
    def _():
        pltpu.make_async_copy(swapped, held, sem).start()

    total = jnp.dot(rows[0][...], own[...], preferred_element_type=jnp.float32)
    pltpu.make_async_copy(fetched, held, sem).wait()
    for k in range(3):
        total = total + jnp.dot(rows[k + 1][...], held[k], preferred_element_type=jnp.float32)
    out[...] = total.astype(out.dtype)


def project(far, ids, rows, own, fetched, swapped):
    vmem = pl.BlockSpec(memory_space=pltpu.VMEM)
    anywhere = pl.BlockSpec(memory_space=pl.ANY)
    part = own.shape[1]
    return pl.pallas_call(
        functools.partial(project_kernel, far),
        out_shape=jax.ShapeDtypeStruct((ROWS, part), jnp.bfloat16 if far else jnp.float32),
        in_specs=[pl.BlockSpec(memory_space=pltpu.SMEM)] + [vmem] * 5 + [anywhere] * 2,
        out_specs=vmem,
        scratch_shapes=[pltpu.VMEM((3, WIDTH, part), jnp.bfloat16), pltpu.SemaphoreType.DMA],
        compiler_params=pltpu.CompilerParams(vmem_limit_bytes=VMEM_LIMIT),
        cost_estimate=pl.CostEstimate(
            flops=8 * ROWS * WIDTH * part, bytes_accessed=5000000, transcendentals=0
        ),
        name="project",
    )(ids, *rows, own, fetched, swapped)


def around(value, axis, steps):
    count = lax.axis_size(axis)
    return lax.ppermute(value, axis, [(i, (i + steps) % count) for i in range(count)])


def together(*values):
    return lax.optimization_barrier(values)


def per_device(hidden, queries, key_rows, values, out_weight, level_table, noise_level, group_live):
    z, y, core = lax.axis_index("z"), lax.axis_index("y"), lax.axis_index("c")
    w, x = lax.axis_index("w"), lax.axis_index("x")
    slot = z * 8 + y * 2 + core
    home = lax.rem(slot + 1, 32) // 8
    ids = jnp.stack([z, y, core, home]).astype(jnp.int32)

    def to_level(value, d):
        return lax.ppermute(value, "z", [(i, i - d) for i in range(d, 4)])

    part = out_weight.shape[1] // 8

    def columns(owner):
        return lax.dynamic_slice_in_dim(out_weight, owner * part, part, 1)

    block = jnp.where(core == 0, w, 1 - w) * 4

    def fetch(value, step):
        return around(value, "x", step)

    pieces = [columns(block + lax.rem(x + step, 4)) for step in (1, 2, 3)]
    weight_near, weight_far = columns(w * 4 + x), columns((1 - w) * 4 + x)

    pair = jnp.concatenate([key_rows, values], axis=1)
    below, above, next_one, first_piece, third_piece, pair, queries, second, hidden = together(
        around(pair, "y", 1),
        around(pair, "y", -1),
        to_level(queries, 1),
        fetch(pieces[0], 1),
        fetch(pieces[2], 3),
        pair,
        queries,
        pieces[1],
        hidden,
    )
    across, next_two, next_three, second_piece, pair_there, below_there, above_there, hidden = together(
        around(pair, "y", 2),
        to_level(queries, 2),
        to_level(queries, 3),
        fetch(second, 2),
        around(pair, "c", 1),
        around(below, "c", 1),
        around(above, "c", 1),
        hidden,
    )
    across_there = around(across, "c", 1)
    pairs = [pair, below, above, across, pair_there, below_there, above_there, across_there]
    fetched = jnp.stack([first_piece, second_piece, third_piece])
    swapped = around(fetched, "c", 1)
    hidden_next = around(hidden, SLOT, -1)

    def back(share, d):
        pairs_back = [
            (8 * (i - d) + j, (8 * i + j - 1) % 32) for i in range(d, 4) for j in range(8)
        ]
        return lax.ppermute(share, SLOT, pairs_back)

    two, one = attend((2, 1), ids, group_live, noise_level, [next_two, next_one], pairs)
    back_two, back_one = back(two, 2), back(one, 1)
    live_later, one = together(group_live, one)
    (three,) = attend((3,), ids, live_later, noise_level, [next_three], pairs)
    back_three = back(three, 3)
    live_later, three, hidden_next, fetched, swapped = together(
        live_later, three, hidden_next, fetched, swapped
    )
    (zero,) = attend((0,), ids, live_later, noise_level, [queries], pairs)
    back_zero = back(zero, 0)
    attended, gate_row = combine(ids, level_table, [back_zero, back_one, back_two, back_three])

    rows = [attended] + [around(attended, "x", step) for step in (1, 2, 3)]
    far_sum = project(True, ids, rows, weight_far, fetched, swapped)
    arrived = around(far_sum, "w", 1)
    near_sum = project(False, ids, rows, weight_near, fetched, swapped)
    projected = near_sum + arrived.astype(jnp.float32)
    return (hidden_next.astype(jnp.float32) + gate_row * projected).astype(jnp.bfloat16)


def solution(mesh):
    fine = Mesh(np.asarray(mesh.devices).reshape(4, 4, 2, 2, 4), ("z", "y", "c", "w", "x"))
    tp = ("w", "x")
    block = P(SLOT, tp)
    in_specs = (block, block, block, block, P(tp, None), P(None, tp), P(SLOT), P())
    return jax.shard_map(
        per_device, mesh=fine, in_specs=in_specs, out_specs=block, check_vma=False
    )
```

```python
import functools
import math

import jax
import jax.numpy as jnp
import numpy as np
from jax import lax
from jax.experimental import pallas as pl
from jax.experimental.pallas import tpu as pltpu
from jax.sharding import Mesh
from jax.sharding import PartitionSpec as P

HD = 128
ROWS = 448
HEADS_HERE = 3
WIDTH = HEADS_HERE * HD
STAT = 32
LOWEST = -1e30
EXP2_SCALE = HD**-0.5 * math.log2(math.e)
Y_STEPS = (0, -1, 1, 2)
SLOT = ("z", "y", "c")
ATTEND_VMEM = 32 * 1024 * 1024
SMALL_VMEM = 16 * 1024 * 1024


def score(query, key):
    return lax.dot_general(
        query, key, (((1,), (1,)), ((), ())), preferred_element_type=jnp.float32
    )


def attend_kernel(steps, ids, live, level, *refs):
    many = len(steps)
    query_in, pair_in, out = refs[0:many], refs[many : many + 8], refs[many + 8 : 2 * many + 8]
    raw, scaled, pairs, own, acc, top, done, raw_sem, pair_sem, own_sem, out_sem = refs[2 * many + 8 :]
    here, y, core = ids[0], ids[1], ids[2]
    first = here * 8
    mine = first + y * 2 + core
    groups = []
    for other in (0, 1):
        for step in Y_STEPS:
            core_there = core if other == 0 else 1 - core
            groups.append(first + lax.rem(y + step + 4, 4) * 2 + core_there)
    alive = [live[first + k] for k in range(8)]

    def live_before(group):
        count = jnp.int32(0)
        for k in range(8):
            count = count + jnp.where(first + k < group, alive[k], 0)
        return count

    bound = mine if steps == (0,) else first + 8
    count = live_before(bound)
    active = [here + step <= 3 for step in steps]
    some = here + min(steps) <= 3

    def raw_copy(i):
        return pltpu.make_async_copy(query_in[i], raw.at[i], raw_sem.at[i])

    def own_copy():
        return pltpu.make_async_copy(pair_in[0], own, own_sem)

    def place_copy(p, place):
        at = pl.ds(pl.multiple_of(place * ROWS, 64), ROWS)
        return pltpu.make_async_copy(pair_in[p], pairs.at[at], pair_sem.at[place])

    def wait_place(place):
        place_copy(0, place).wait()

    @pl.when(some)
    def _():
        for i in range(many):
            raw_copy(i).start()
        if steps == (0,):
            own_copy().start()
        for p in range(8):

            @pl.when((live[groups[p]] == 1) & (groups[p] < bound))
            def _():
                place_copy(p, live_before(groups[p])).start()

        for i in range(many):
            raw_copy(i).wait()

    def update_heads(ref, at, rows, opening):
        ones = jnp.ones((rows, HD), jnp.bfloat16)

        def scores_of(head):
            key = ref[at, head * HD : (head + 1) * HD]
            return score(scaled[head], jnp.concatenate([key, key], axis=1))

        def absorb(head, scores):
            highest = jnp.max(scores, axis=1, keepdims=True)
            if opening:
                new = jnp.broadcast_to(highest, (ROWS, HD))
                weights = jnp.exp2(scores - highest)
            else:
                old = top[head]
                new = jnp.maximum(old, highest)
                if rows % HD == 0:
                    shift = jnp.concatenate([new] * (rows // HD), axis=1)
                else:
                    shift = new[:, :1]
                weights = jnp.exp2(scores - shift)
            value = ref[at, WIDTH + head * HD : WIDTH + (head + 1) * HD]
            weighted = jnp.dot(
                weights.astype(jnp.bfloat16),
                jnp.concatenate([value, ones], axis=1),
                preferred_element_type=jnp.float32,
            )
            if opening:
                acc[head] = weighted
            else:
                shrink = jnp.exp2(old - new)
                acc[head] = acc[head] * jnp.concatenate([shrink, shrink], axis=1) + weighted
            top[head] = new

        scores = scores_of(0)
        for head in range(HEADS_HERE):
            following = scores_of(head + 1) if head + 1 < HEADS_HERE else None
            absorb(head, scores)
            scores = following

    def sweep(fresh):
        def four(t, unused):
            @pl.when(fresh)
            def _():
                for k in range(4):
                    wait_place(t * 4 + k)

            update_heads(pairs, pl.ds(pl.multiple_of(t * 4 * ROWS, HD), 4 * ROWS), 4 * ROWS, False)
            return 0

        lax.fori_loop(0, count // 4, four, 0)
        rest = count % 4
        base = count - rest

        @pl.when(fresh)
        def _():
            for k in range(3):

                @pl.when(k < rest)
                def _():
                    wait_place(base + k)

        @pl.when(rest >= 2)
        def _():
            update_heads(pairs, pl.ds(pl.multiple_of(base * ROWS, HD), 2 * ROWS), 2 * ROWS, False)

        @pl.when(rest % 2 == 1)
        def _():
            update_heads(pairs, pl.ds(pl.multiple_of((count - 1) * ROWS, 64), ROWS), ROWS, False)

    def source(i, fresh):
        for head in range(HEADS_HERE):
            exact = raw[i, :, head * HD : (head + 1) * HD].astype(jnp.float32) * EXP2_SCALE
            high = exact.astype(jnp.bfloat16)
            scaled[head, :, :HD] = high
            scaled[head, :, HD:] = (exact - high.astype(jnp.float32)).astype(jnp.bfloat16)
        if steps == (0,):
            own_copy().wait()
            update_heads(own, pl.ds(0, ROWS), ROWS, True)
        else:
            top[...] = jnp.full(top.shape, LOWEST, jnp.float32)
            acc[...] = jnp.zeros(acc.shape, jnp.float32)
        sweep(fresh)
        lane = lax.broadcasted_iota(jnp.int32, (ROWS, HD), 1)
        stats = jnp.where(lane == 3 * HEADS_HERE, level[0].astype(jnp.float32), 0.0)
        for head in range(HEADS_HERE):
            exact = top[head]
            sent = exact.astype(jnp.bfloat16).astype(jnp.float32)
            factor = jnp.exp2(exact - sent)
            both = acc[head]
            done[i, 0:ROWS, head * HD : (head + 1) * HD] = (both[:, :HD] * factor).astype(
                jnp.bfloat16
            )
            total = both[:, HD:] * factor
            high = total.astype(jnp.bfloat16).astype(jnp.float32)
            stats = jnp.where(lane == head, sent, stats)
            stats = jnp.where(lane == HEADS_HERE + head, high, stats)
            stats = jnp.where(lane == 2 * HEADS_HERE + head, total - high, stats)
        flat = jnp.transpose(stats)[:16].astype(jnp.bfloat16)
        done[i, ROWS : ROWS + 16, :] = flat[:, :WIDTH]
        pad = jnp.zeros((16, 2 * WIDTH - ROWS), jnp.bfloat16)
        done[i, ROWS + 16 : ROWS + 32, :] = jnp.concatenate([flat[:, WIDTH:], pad], axis=1)

    if many == 1:

        @pl.when(active[0])
        def _():
            source(0, True)

    else:

        def one(i, unused):
            step = steps[0] - i
            before = here + step + 1 <= 3

            @pl.when(here + step <= 3)
            def _():
                source(i, jnp.logical_or(i == 0, jnp.logical_not(before)))

            return 0

        lax.fori_loop(0, many, one, 0)

    for i in range(many):

        @pl.when(active[i])
        def _():
            pltpu.make_async_copy(done.at[i], out[i], out_sem.at[i]).start()

    for i in range(many):

        @pl.when(active[i])
        def _():
            pltpu.make_async_copy(done.at[i], out[i], out_sem.at[i]).wait()


def attend(steps, ids, live, level, queries, pairs):
    smem = pl.BlockSpec(memory_space=pltpu.SMEM)
    anywhere = pl.BlockSpec(memory_space=pl.ANY)
    bf16, f32 = jnp.bfloat16, jnp.float32
    many = len(steps)
    return pl.pallas_call(
        functools.partial(attend_kernel, steps),
        out_shape=[jax.ShapeDtypeStruct((ROWS + STAT, WIDTH), bf16)] * many,
        in_specs=[smem] * 3 + [anywhere] * (many + 8),
        out_specs=[anywhere] * many,
        scratch_shapes=[
            pltpu.VMEM((many, ROWS, WIDTH), bf16),
            pltpu.VMEM((HEADS_HERE, ROWS, 2 * HD), bf16),
            pltpu.VMEM((8 * ROWS, 2 * WIDTH), bf16),
            pltpu.VMEM((ROWS, 2 * WIDTH), bf16),
            pltpu.VMEM((HEADS_HERE, ROWS, 2 * HD), f32),
            pltpu.VMEM((HEADS_HERE, ROWS, HD), f32),
            pltpu.VMEM((many, ROWS + STAT, WIDTH), bf16),
            pltpu.SemaphoreType.DMA((many,)),
            pltpu.SemaphoreType.DMA((8,)),
            pltpu.SemaphoreType.DMA,
            pltpu.SemaphoreType.DMA((many,)),
        ],
        compiler_params=pltpu.CompilerParams(vmem_limit_bytes=ATTEND_VMEM),
        cost_estimate=pl.CostEstimate(
            flops=many * 8 * 3 * ROWS * ROWS * HD * 16, bytes_accessed=6000000, transcendentals=0
        ),
        name="attend",
    )(ids, live, level, *queries, *pairs)


def combine_kernel(ids, table, *refs):
    parts, out, gate = refs[0:4], refs[4], refs[5]
    home = ids[3]
    maxima, sums = [], []
    for d in range(4):
        tail = parts[d][ROWS : ROWS + STAT, :].astype(jnp.float32)
        flat = jnp.concatenate([tail[0:16], tail[16:32, : ROWS - WIDTH]], axis=1)
        if d == 0:
            noise = flat[3 * HEADS_HERE : 3 * HEADS_HERE + 1, 0:1]
        stats = jnp.transpose(jnp.concatenate([flat, jnp.zeros((HD - 16, ROWS), jnp.float32)]))
        present = d <= home
        row_max, row_sum = [], []
        for head in range(HEADS_HERE):
            total = (
                stats[:, HEADS_HERE + head : HEADS_HERE + head + 1]
                + stats[:, 2 * HEADS_HERE + head : 2 * HEADS_HERE + head + 1]
            )
            row_max.append(jnp.where(present, stats[:, head : head + 1], LOWEST))
            row_sum.append(jnp.where(present, total, 0.0))
        maxima.append(row_max)
        sums.append(row_sum)
    for head in range(HEADS_HERE):
        at = slice(head * HD, (head + 1) * HD)
        highest = maxima[0][head]
        for d in range(1, 4):
            highest = jnp.maximum(highest, maxima[d][head])
        numerator = jnp.zeros((ROWS, HD), jnp.float32)
        denominator = jnp.zeros((ROWS, 1), jnp.float32)
        for d in range(4):
            factor = jnp.exp2(maxima[d][head] - highest)
            share = jnp.where(d <= home, parts[d][0:ROWS, at].astype(jnp.float32), 0.0)
            numerator = numerator + share * factor
            denominator = denominator + sums[d][head] * factor
        out[:, at] = (numerator / denominator).astype(jnp.bfloat16)
    index = lax.broadcasted_iota(jnp.int32, table.shape, 0).astype(jnp.float32)
    gate[...] = jnp.sum(jnp.where(index == noise, table[...], 0.0), axis=0, keepdims=True)


def combine(ids, table, parts):
    vmem = pl.BlockSpec(memory_space=pltpu.VMEM)
    return pl.pallas_call(
        combine_kernel,
        out_shape=[
            jax.ShapeDtypeStruct((ROWS, WIDTH), jnp.bfloat16),
            jax.ShapeDtypeStruct((1, table.shape[1]), jnp.float32),
        ],
        in_specs=[pl.BlockSpec(memory_space=pltpu.SMEM)] + [vmem] * 5,
        out_specs=[vmem] * 2,
        compiler_params=pltpu.CompilerParams(vmem_limit_bytes=SMALL_VMEM),
        name="combine",
    )(ids, table, *parts)


def project_kernel(far, ids, *refs):
    rows, own, fetched, swapped, out, held, sem = refs[0:4], refs[4], refs[5], refs[6], refs[7], refs[8], refs[9]
    mine = ids[2] == (1 if far else 0)

    @pl.when(mine)
    def _():
        pltpu.make_async_copy(fetched, held, sem).start()

    @pl.when(jnp.logical_not(mine))
    def _():
        pltpu.make_async_copy(swapped, held, sem).start()

    total = jnp.dot(rows[0][...], own[...], preferred_element_type=jnp.float32)
    pltpu.make_async_copy(fetched, held, sem).wait()
    for k in range(3):
        total = total + jnp.dot(rows[k + 1][...], held[k], preferred_element_type=jnp.float32)
    out[...] = total.astype(out.dtype)


def project(far, ids, rows, own, fetched, swapped):
    vmem = pl.BlockSpec(memory_space=pltpu.VMEM)
    anywhere = pl.BlockSpec(memory_space=pl.ANY)
    part = own.shape[1]
    return pl.pallas_call(
        functools.partial(project_kernel, far),
        out_shape=jax.ShapeDtypeStruct((ROWS, part), jnp.bfloat16 if far else jnp.float32),
        in_specs=[pl.BlockSpec(memory_space=pltpu.SMEM)] + [vmem] * 5 + [anywhere] * 2,
        out_specs=vmem,
        scratch_shapes=[pltpu.VMEM((3, WIDTH, part), jnp.bfloat16), pltpu.SemaphoreType.DMA],
        compiler_params=pltpu.CompilerParams(vmem_limit_bytes=SMALL_VMEM),
        cost_estimate=pl.CostEstimate(
            flops=8 * ROWS * WIDTH * part, bytes_accessed=5000000, transcendentals=0
        ),
        name="project",
    )(ids, *rows, own, fetched, swapped)


def around(value, axis, steps):
    count = lax.axis_size(axis)
    return lax.ppermute(value, axis, [(i, (i + steps) % count) for i in range(count)])


def together(*values):
    return lax.optimization_barrier(values)


def per_device(hidden, queries, key_rows, values, out_weight, level_table, noise_level, group_live):
    z, y, core = lax.axis_index("z"), lax.axis_index("y"), lax.axis_index("c")
    w, x = lax.axis_index("w"), lax.axis_index("x")
    slot = z * 8 + y * 2 + core
    home = lax.rem(slot + 1, 32) // 8
    ids = jnp.stack([z, y, core, home]).astype(jnp.int32)

    def to_level(value, d):
        return lax.ppermute(value, "z", [(i, i - d) for i in range(d, 4)])

    part = out_weight.shape[1] // 8

    def columns(owner):
        return lax.dynamic_slice_in_dim(out_weight, owner * part, part, 1)

    block = jnp.where(core == 0, w, 1 - w) * 4

    def fetch(step):
        return around(columns(block + lax.rem(x + step, 4)), "x", step)

    pair = jnp.concatenate([key_rows, values], axis=1)
    below, above, next_one, next_three, piece_one, pair, queries, hidden, out_weight = together(
        around(pair, "y", 1),
        around(pair, "y", -1),
        to_level(queries, 1),
        to_level(queries, 3),
        fetch(1),
        pair,
        queries,
        hidden,
        out_weight,
    )
    across, next_two, pair_there, piece_two, piece_three, below, above, hidden, out_weight = together(
        around(pair, "y", 2),
        to_level(queries, 2),
        around(pair, "c", 1),
        fetch(2),
        fetch(3),
        below,
        above,
        hidden,
        out_weight,
    )
    below_there, above_there, across_there, fetched, hidden, out_weight = together(
        around(below, "c", 1),
        around(above, "c", 1),
        around(across, "c", 1),
        jnp.stack([piece_one, piece_two, piece_three]),
        hidden,
        out_weight,
    )
    pairs = [pair, below, above, across, pair_there, below_there, above_there, across_there]
    weight_near, weight_far = columns(w * 4 + x), columns((1 - w) * 4 + x)
    swapped = around(fetched, "c", 1)
    hidden_next = around(hidden, SLOT, -1)

    def back(share, d):
        pairs_back = [
            (8 * (i - d) + j, (8 * i + j - 1) % 32) for i in range(d, 4) for j in range(8)
        ]
        return lax.ppermute(share, SLOT, pairs_back)

    two, one = attend((2, 1), ids, group_live, noise_level, [next_two, next_one], pairs)
    back_two, back_one = back(two, 2), back(one, 1)
    live_later, one = together(group_live, one)
    (three,) = attend((3,), ids, live_later, noise_level, [next_three], pairs)
    back_three = back(three, 3)
    live_later, three, hidden_next, swapped = together(live_later, three, hidden_next, swapped)
    (zero,) = attend((0,), ids, live_later, noise_level, [queries], pairs)
    back_zero = back(zero, 0)
    attended, gate_row = combine(ids, level_table, [back_zero, back_one, back_two, back_three])

    rows = [attended] + [around(attended, "x", step) for step in (1, 2, 3)]
    far_sum = project(True, ids, rows, weight_far, fetched, swapped)
    arrived = around(far_sum, "w", 1)
    near_sum = project(False, ids, rows, weight_near, fetched, swapped)
    projected = near_sum + arrived.astype(jnp.float32)
    return (hidden_next.astype(jnp.float32) + gate_row * projected).astype(jnp.bfloat16)


def solution(mesh):
    fine = Mesh(np.asarray(mesh.devices).reshape(4, 4, 2, 2, 4), ("z", "y", "c", "w", "x"))
    tp = ("w", "x")
    block = P(SLOT, tp)
    in_specs = (block, block, block, block, P(tp, None), P(None, tp), P(SLOT), P())
    return jax.shard_map(
        per_device, mesh=fine, in_specs=in_specs, out_specs=block, check_vma=False
    )
```

```python
import functools
import math

import jax
import jax.numpy as jnp
import numpy as np
from jax import lax
from jax.experimental import pallas as pl
from jax.experimental.pallas import tpu as pltpu
from jax.sharding import Mesh
from jax.sharding import PartitionSpec as P

HD = 128
ROWS = 448
HEADS_HERE = 3
WIDTH = HEADS_HERE * HD
STAT = 32
LOWEST = -(2.0**100)
EXP2_SCALE = HD**-0.5 * math.log2(math.e)
Y_STEPS = (0, -1, 1, 2)
SLOT = ("z", "y", "c")
ATTEND_VMEM = 32 * 1024 * 1024
SMALL_VMEM = 16 * 1024 * 1024


def score(query, key):
    return lax.dot_general(
        query, key, (((1,), (1,)), ((), ())), preferred_element_type=jnp.float32
    )


def attend_kernel(ids, live, level, *refs):
    query_in, pair_in, out = refs[0:4], refs[4:12], refs[12:16]
    raw, scaled, pairs, held, acc, top, done, raw_sem, pair_sem, out_sem = refs[16:]
    here, y, core = ids[0], ids[1], ids[2]
    first = here * 8
    mine = first + y * 2 + core
    groups = []
    for other in (0, 1):
        for step in Y_STEPS:
            core_there = core if other == 0 else 1 - core
            groups.append(first + lax.rem(y + step + 4, 4) * 2 + core_there)
    alive = [live[first + k] for k in range(8)]

    def live_before(group):
        count = jnp.int32(0)
        for k in range(8):
            count = count + jnp.where(first + k < group, alive[k], 0)
        return count

    n_all, n_own = live_before(first + 8), live_before(mine)
    last = here == 3
    own_place = jnp.where((live[mine] == 1) | last, n_own, n_all)

    def raw_copy(d):
        return pltpu.make_async_copy(query_in[d], raw.at[d], raw_sem.at[d])

    def place_copy(p, place):
        at = pl.ds(pl.multiple_of(place * ROWS, 64), ROWS)
        return pltpu.make_async_copy(pair_in[p], pairs.at[at], pair_sem.at[place])

    def wait_place(place):
        place_copy(0, place).wait()

    raw_copy(0).start()
    place_copy(0, own_place).start()
    for p in range(1, 8):

        @pl.when((live[groups[p]] == 1) & ((groups[p] < mine) | jnp.logical_not(last)))
        def _():
            place_copy(p, live_before(groups[p])).start()

    for d in range(1, 4):

        @pl.when(here + d <= 3)
        def _():
            raw_copy(d).start()

    raw_copy(0).wait()
    wait_place(own_place)
    for k in range(8):

        @pl.when(k < n_own)
        def _():
            wait_place(k)

    def source(d, unused):
        @pl.when(d == 1)
        def _():
            for k in range(8):

                @pl.when((k >= n_own) & (k < n_all) & (k != own_place))
                def _():
                    wait_place(k)

            for e in range(1, 4):

                @pl.when(here + e <= 3)
                def _():
                    raw_copy(e).wait()

        count = jnp.where(d == 0, n_own + 1, n_all)
        chunks = (count + 1) // 2

        def place(i):
            i = jnp.maximum(jnp.minimum(i, count - 1), 0)
            return jnp.where((d == 0) & (i == n_own), own_place, i)

        def at(i):
            return pl.ds(pl.multiple_of(place(i) * ROWS, 64), ROWS)

        for head in range(HEADS_HERE):
            exact = raw[d, :, head * HD : (head + 1) * HD].astype(jnp.float32) * EXP2_SCALE
            high = exact.astype(jnp.bfloat16)
            scaled[head, :, :HD] = high
            scaled[head, :, HD:] = (exact - high.astype(jnp.float32)).astype(jnp.bfloat16)
        top[...] = jnp.full(top.shape, LOWEST, jnp.float32)
        acc[...] = jnp.zeros(acc.shape, jnp.float32)

        def scores_of(t, head):
            cols = slice(head * HD, (head + 1) * HD)
            key = jnp.concatenate([pairs[at(2 * t), cols], pairs[at(2 * t + 1), cols]], axis=0)
            return score(scaled[head], jnp.concatenate([key, key], axis=1))

        def absorb(t, head, scores):
            old = top[head]
            new = jnp.maximum(old, jnp.max(scores, axis=1, keepdims=True))
            weights = jnp.exp2(scores - jnp.concatenate([new] * (2 * ROWS // HD), axis=1))
            cols = slice(WIDTH + head * HD, WIDTH + (head + 1) * HD)
            there = jnp.where(2 * t + 1 < count, 1.0, 0.0).astype(jnp.bfloat16)
            ones = jnp.ones((ROWS, HD), jnp.bfloat16)
            value = jnp.concatenate(
                [
                    jnp.concatenate([pairs[at(2 * t), cols], ones], axis=1),
                    jnp.concatenate([pairs[at(2 * t + 1), cols], ones], axis=1) * there,
                ],
                axis=0,
            )
            weighted = jnp.dot(
                weights.astype(jnp.bfloat16), value, preferred_element_type=jnp.float32
            )
            shrink = jnp.exp2(old - new)
            acc[head] = acc[head] * jnp.concatenate([shrink, shrink], axis=1) + weighted
            top[head] = new

        held[...] = scores_of(0, 0)

        def chunk(t, unused_too):
            scores = held[...]
            following = scores_of(t, 1)
            absorb(t, 0, scores)
            scores = scores_of(t, 2)
            absorb(t, 1, following)
            held[...] = scores_of(t + 1, 0)
            absorb(t, 2, scores)
            return 0

        lax.fori_loop(0, chunks, chunk, 0)

        lane = lax.broadcasted_iota(jnp.int32, (ROWS, HD), 1)
        stats = jnp.where(lane == 3 * HEADS_HERE, level[0].astype(jnp.float32), 0.0)
        for head in range(HEADS_HERE):
            exact = top[head]
            sent = exact.astype(jnp.bfloat16).astype(jnp.float32)
            factor = jnp.exp2(exact - sent)
            both = acc[head]
            done[d, 0:ROWS, head * HD : (head + 1) * HD] = (both[:, :HD] * factor).astype(
                jnp.bfloat16
            )
            total = both[:, HD:] * factor
            high = total.astype(jnp.bfloat16).astype(jnp.float32)
            stats = jnp.where(lane == head, sent, stats)
            stats = jnp.where(lane == HEADS_HERE + head, high, stats)
            stats = jnp.where(lane == 2 * HEADS_HERE + head, total - high, stats)
        flat = jnp.transpose(stats)[:16].astype(jnp.bfloat16)
        done[d, ROWS : ROWS + 16, :] = flat[:, :WIDTH]
        pad = jnp.zeros((16, 2 * WIDTH - ROWS), jnp.bfloat16)
        done[d, ROWS + 16 : ROWS + 32, :] = jnp.concatenate([flat[:, WIDTH:], pad], axis=1)
        for k in range(4):

            @pl.when(d == k)
            def _():
                pltpu.make_async_copy(done.at[k], out[k], out_sem.at[k]).start()

        return 0

    lax.fori_loop(0, 4 - here, source, 0)
    for k in range(4):

        @pl.when(here + k <= 3)
        def _():
            pltpu.make_async_copy(done.at[k], out[k], out_sem.at[k]).wait()


def attend(ids, live, level, queries, pairs):
    smem = pl.BlockSpec(memory_space=pltpu.SMEM)
    anywhere = pl.BlockSpec(memory_space=pl.ANY)
    bf16, f32 = jnp.bfloat16, jnp.float32
    return pl.pallas_call(
        attend_kernel,
        out_shape=[jax.ShapeDtypeStruct((ROWS + STAT, WIDTH), bf16)] * 4,
        in_specs=[smem] * 3 + [anywhere] * 12,
        out_specs=[anywhere] * 4,
        scratch_shapes=[
            pltpu.VMEM((4, ROWS, WIDTH), bf16),
            pltpu.VMEM((HEADS_HERE, ROWS, 2 * HD), bf16),
            pltpu.VMEM((8 * ROWS, 2 * WIDTH), bf16),
            pltpu.VMEM((ROWS, 2 * ROWS), f32),
            pltpu.VMEM((HEADS_HERE, ROWS, 2 * HD), f32),
            pltpu.VMEM((HEADS_HERE, ROWS, HD), f32),
            pltpu.VMEM((4, ROWS + STAT, WIDTH), bf16),
            pltpu.SemaphoreType.DMA((4,)),
            pltpu.SemaphoreType.DMA((8,)),
            pltpu.SemaphoreType.DMA((4,)),
        ],
        compiler_params=pltpu.CompilerParams(vmem_limit_bytes=ATTEND_VMEM),
        cost_estimate=pl.CostEstimate(
            flops=32 * HEADS_HERE * ROWS * ROWS * HD * 8, bytes_accessed=8000000, transcendentals=0
        ),
        name="attend",
    )(ids, live, level, *queries, *pairs)


def combine_kernel(ids, table, *refs):
    parts, out, gate = refs[0:4], refs[4], refs[5]
    home = ids[3]
    maxima, sums = [], []
    for d in range(4):
        tail = parts[d][ROWS : ROWS + STAT, :].astype(jnp.float32)
        flat = jnp.concatenate([tail[0:16], tail[16:32, : ROWS - WIDTH]], axis=1)
        if d == 0:
            noise = flat[3 * HEADS_HERE : 3 * HEADS_HERE + 1, 0:1]
        stats = jnp.transpose(jnp.concatenate([flat, jnp.zeros((HD - 16, ROWS), jnp.float32)]))
        present = d <= home
        row_max, row_sum = [], []
        for head in range(HEADS_HERE):
            total = (
                stats[:, HEADS_HERE + head : HEADS_HERE + head + 1]
                + stats[:, 2 * HEADS_HERE + head : 2 * HEADS_HERE + head + 1]
            )
            row_max.append(jnp.where(present, stats[:, head : head + 1], LOWEST))
            row_sum.append(jnp.where(present, total, 0.0))
        maxima.append(row_max)
        sums.append(row_sum)
    for head in range(HEADS_HERE):
        at = slice(head * HD, (head + 1) * HD)
        highest = maxima[0][head]
        for d in range(1, 4):
            highest = jnp.maximum(highest, maxima[d][head])
        numerator = jnp.zeros((ROWS, HD), jnp.float32)
        denominator = jnp.zeros((ROWS, 1), jnp.float32)
        for d in range(4):
            factor = jnp.exp2(maxima[d][head] - highest)
            share = jnp.where(d <= home, parts[d][0:ROWS, at].astype(jnp.float32), 0.0)
            numerator = numerator + share * factor
            denominator = denominator + sums[d][head] * factor
        out[:, at] = (numerator / denominator).astype(jnp.bfloat16)
    index = lax.broadcasted_iota(jnp.int32, table.shape, 0).astype(jnp.float32)
    gate[...] = jnp.sum(jnp.where(index == noise, table[...], 0.0), axis=0, keepdims=True)


def combine(ids, table, parts):
    vmem = pl.BlockSpec(memory_space=pltpu.VMEM)
    return pl.pallas_call(
        combine_kernel,
        out_shape=[
            jax.ShapeDtypeStruct((ROWS, WIDTH), jnp.bfloat16),
            jax.ShapeDtypeStruct((1, table.shape[1]), jnp.float32),
        ],
        in_specs=[pl.BlockSpec(memory_space=pltpu.SMEM)] + [vmem] * 5,
        out_specs=[vmem] * 2,
        compiler_params=pltpu.CompilerParams(vmem_limit_bytes=SMALL_VMEM),
        name="combine",
    )(ids, table, *parts)


def project_kernel(far, ids, *refs):
    rows, own, fetched, swapped, out, held, sem = refs[0:4], refs[4], refs[5], refs[6], refs[7], refs[8], refs[9]
    mine = ids[2] == (1 if far else 0)

    @pl.when(mine)
    def _():
        pltpu.make_async_copy(fetched, held, sem).start()

    @pl.when(jnp.logical_not(mine))
    def _():
        pltpu.make_async_copy(swapped, held, sem).start()

    pltpu.make_async_copy(fetched, held, sem).wait()
    block = out.shape[1] // 3

    def columns(n, unused):
        at = pl.ds(pl.multiple_of(n * block, block), block)
        total = jnp.dot(rows[0][...], own[:, at], preferred_element_type=jnp.float32)
        for k in range(3):
            total = total + jnp.dot(
                rows[k + 1][...], held[k, :, at], preferred_element_type=jnp.float32
            )
        out[:, at] = total.astype(out.dtype)
        return 0

    lax.fori_loop(0, 3, columns, 0)


def project(far, ids, rows, own, fetched, swapped):
    vmem = pl.BlockSpec(memory_space=pltpu.VMEM)
    anywhere = pl.BlockSpec(memory_space=pl.ANY)
    part = own.shape[1]
    return pl.pallas_call(
        functools.partial(project_kernel, far),
        out_shape=jax.ShapeDtypeStruct((ROWS, part), jnp.bfloat16 if far else jnp.float32),
        in_specs=[pl.BlockSpec(memory_space=pltpu.SMEM)] + [vmem] * 5 + [anywhere] * 2,
        out_specs=vmem,
        scratch_shapes=[pltpu.VMEM((3, WIDTH, part), jnp.bfloat16), pltpu.SemaphoreType.DMA],
        compiler_params=pltpu.CompilerParams(vmem_limit_bytes=SMALL_VMEM),
        cost_estimate=pl.CostEstimate(
            flops=8 * ROWS * WIDTH * part, bytes_accessed=5000000, transcendentals=0
        ),
        name="project",
    )(ids, *rows, own, fetched, swapped)


def around(value, axis, steps):
    count = lax.axis_size(axis)
    return lax.ppermute(value, axis, [(i, (i + steps) % count) for i in range(count)])


def together(*values):
    return lax.optimization_barrier(values)


def per_device(hidden, queries, key_rows, values, out_weight, level_table, noise_level, group_live):
    z, y, core = lax.axis_index("z"), lax.axis_index("y"), lax.axis_index("c")
    w, x = lax.axis_index("w"), lax.axis_index("x")
    slot = z * 8 + y * 2 + core
    home = lax.rem(slot + 1, 32) // 8
    ids = jnp.stack([z, y, core, home]).astype(jnp.int32)

    def to_level(value, d):
        return lax.ppermute(value, "z", [(i, i - d) for i in range(d, 4)])

    part = out_weight.shape[1] // 8

    def columns(owner):
        return lax.dynamic_slice_in_dim(out_weight, owner * part, part, 1)

    block = jnp.where(core == 0, w, 1 - w) * 4

    def fetch(step):
        return around(columns(block + lax.rem(x + step, 4)), "x", step)

    pair = jnp.concatenate([key_rows, values], axis=1)
    next_one, next_three, below, above, piece_one, pair, queries, hidden, out_weight = together(
        to_level(queries, 1),
        to_level(queries, 3),
        around(pair, "y", 1),
        around(pair, "y", -1),
        fetch(1),
        pair,
        queries,
        hidden,
        out_weight,
    )
    next_two, across, pair_there, piece_two, below, above, hidden, out_weight = together(
        to_level(queries, 2),
        around(pair, "y", 2),
        around(pair, "c", 1),
        fetch(2),
        below,
        above,
        hidden,
        out_weight,
    )
    below_there, above_there, across_there, hidden, out_weight = together(
        around(below, "c", 1),
        around(above, "c", 1),
        around(across, "c", 1),
        hidden,
        out_weight,
    )
    pairs = [pair, below, above, across, pair_there, below_there, above_there, across_there]
    weight_near, weight_far = columns(w * 4 + x), columns((1 - w) * 4 + x)
    piece_three = fetch(3)
    hidden_next = around(hidden, SLOT, -1)

    def back(share, d):
        pairs_back = [
            (8 * (i - d) + j, (8 * i + j - 1) % 32) for i in range(d, 4) for j in range(8)
        ]
        return lax.ppermute(share, SLOT, pairs_back)

    shares = attend(
        ids, group_live, noise_level, [queries, next_one, next_two, next_three], pairs
    )
    *shares, hidden_next, piece_three, weight_near, weight_far = together(
        *shares, hidden_next, piece_three, weight_near, weight_far
    )
    fetched = jnp.stack([piece_one, piece_two, piece_three])
    swapped = around(fetched, "c", 1)
    returned = [back(shares[d], d) for d in range(4)]
    attended, gate_row = combine(ids, level_table, returned)

    rows = [attended] + [around(attended, "x", step) for step in (1, 2, 3)]
    far_sum = project(True, ids, rows, weight_far, fetched, swapped)
    arrived = around(far_sum, "w", 1)
    near_sum = project(False, ids, rows, weight_near, fetched, swapped)
    projected = near_sum + arrived.astype(jnp.float32)
    return (hidden_next.astype(jnp.float32) + gate_row * projected).astype(jnp.bfloat16)


def solution(mesh):
    fine = Mesh(np.asarray(mesh.devices).reshape(4, 4, 2, 2, 4), ("z", "y", "c", "w", "x"))
    tp = ("w", "x")
    block = P(SLOT, tp)
    in_specs = (block, block, block, block, P(tp, None), P(None, tp), P(SLOT), P())
    return jax.shard_map(
        per_device, mesh=fine, in_specs=in_specs, out_specs=block, check_vma=False
    )
```

```python
import functools
import math

import jax
import jax.numpy as jnp
import numpy as np
from jax import lax
from jax.experimental import pallas as pl
from jax.experimental.pallas import tpu as pltpu
from jax.sharding import Mesh
from jax.sharding import PartitionSpec as P

HD = 128
ROWS = 448
HEADS_HERE = 3
WIDTH = HEADS_HERE * HD
STAT = 32
LOWEST = -(2.0**100)
EXP2_SCALE = HD**-0.5 * math.log2(math.e)
Y_STEPS = (0, -1, 1, 2)
SLOT = ("z", "y", "c")
ATTEND_VMEM = 32 * 1024 * 1024
SMALL_VMEM = 16 * 1024 * 1024


def score(query, key):
    return lax.dot_general(
        query, key, (((1,), (1,)), ((), ())), preferred_element_type=jnp.float32
    )


CALLS = {"early": (1, 3, 0), "middle": (2, 1), "late": (3, 0)}
EARLY, LATER = (0, 1, 2, 4), (3, 5, 6, 7)


def attend_kernel(call, ids, live, level, *refs):
    steps = CALLS[call]
    many = len(steps)
    early, middle = call == "early", call == "middle"
    members = EARLY if early else EARLY + LATER if middle else LATER
    resumed = () if early else (1,) if middle else (0, 1)
    kept = many if early else len(resumed)
    refs = list(refs)

    def take(count):
        taken = refs[:count]
        del refs[:count]
        return taken

    query_in, pair_in = take(many), take(len(members))
    state_in = [] if early else take(2 * kept)
    out = take(2 * many if early else many)
    raw, scaled, pairs, held, acc, top, done, raw_sem, pair_sem, state_sem, out_sem = refs
    here, y, core = ids[0], ids[1], ids[2]
    first = here * 8
    mine = first + y * 2 + core
    groups = {}
    for p in members:
        core_there = core if p < 4 else 1 - core
        groups[p] = first + lax.rem(y + Y_STEPS[p % 4] + 4, 4) * 2 + core_there

    def live_before(group, part):
        count = jnp.int32(0)
        for p in part:
            if p in groups:
                count = count + jnp.where(groups[p] < group, live[groups[p]], 0)
        return count

    everything = first + 8
    n_early, n_later = live_before(everything, EARLY), live_before(everything, LATER)
    n_own = live_before(mine, EARLY if early else LATER)
    own_place = jnp.where(live[mine] == 1, n_own, n_early)

    def raw_copy(i):
        return pltpu.make_async_copy(query_in[i], raw.at[i], raw_sem.at[i])

    def place_copy(j, place):
        at = pl.ds(pl.multiple_of(place * ROWS, 64), ROWS)
        return pltpu.make_async_copy(pair_in[j], pairs.at[at], pair_sem.at[place])

    def state_copies(k):
        i = resumed[k]
        return (
            pltpu.make_async_copy(state_in[2 * k], acc.at[i], state_sem.at[2 * k]),
            pltpu.make_async_copy(state_in[2 * k + 1], top.at[i], state_sem.at[2 * k + 1]),
        )

    def out_copies(i):
        if early:
            return (
                pltpu.make_async_copy(acc.at[i], out[2 * i], out_sem.at[2 * i]),
                pltpu.make_async_copy(top.at[i], out[2 * i + 1], out_sem.at[2 * i + 1]),
            )
        return (pltpu.make_async_copy(done.at[i], out[i], out_sem.at[i]),)

    def active(i):
        return here + steps[i] <= 3

    def step_of(i):
        step = jnp.int32(steps[-1])
        for k in range(many - 1):
            step = jnp.where(i == k, steps[k], step)
        return step

    def run():
        for j, p in enumerate(members):
            part = EARLY if p in EARLY else LATER
            base = 0 if p in EARLY else 4
            if early and p == 0:
                place_copy(j, own_place).start()
            else:

                @pl.when(live[groups[p]] == 1)
                def _():
                    place_copy(j, base + live_before(groups[p], part)).start()

        for i in range(many):

            @pl.when(active(i))
            def _():
                raw_copy(i).start()

        for k in range(len(resumed)):

            @pl.when(active(resumed[k]))
            def _():
                for copy in state_copies(k):
                    copy.start()

        if early:
            place_copy(0, own_place).wait()
        for k in range(8):
            if k < 4 and call != "late":
                there = k < n_early
                if early:
                    there = there & (k != own_place)
            elif k >= 4 and not early:
                there = k - 4 < n_later
            else:
                continue

            @pl.when(there)
            def _():
                place_copy(0, k).wait()

        for i in range(many):

            @pl.when(active(i))
            def _():
                raw_copy(i).wait()

        for k in range(len(resumed)):

            @pl.when(active(resumed[k]))
            def _():
                for copy in state_copies(k):
                    copy.wait()

        def one(i, unused):
            @pl.when(here + step_of(i) <= 3)
            def _():
                source(i)

            return 0

        lax.fori_loop(0, many, one, 0)
        for i in range(many):

            @pl.when(active(i))
            def _():
                for copy in out_copies(i):
                    copy.wait()

    def source(i):
        own = step_of(i) == 0
        if early:
            count = jnp.where(own, n_own + 1, n_early)
            split, base = jnp.where(own, n_own, n_early), own_place
        elif middle:
            count = jnp.where(i == 0, n_early + n_later, n_later)
            split, base = jnp.where(i == 0, n_early, 0), 4
        else:
            count = jnp.where(own, n_own, n_later)
            split, base = jnp.int32(0), 4
        chunks = (count + 1) // 2

        def at(k):
            k = jnp.maximum(jnp.minimum(k, count - 1), 0)
            place = jnp.where(k < split, k, base + k - split)
            return pl.ds(pl.multiple_of(place * ROWS, 64), ROWS)

        for head in range(HEADS_HERE):
            exact = raw[i, :, head * HD : (head + 1) * HD].astype(jnp.float32) * EXP2_SCALE
            high = exact.astype(jnp.bfloat16)
            scaled[head, :, :HD] = high
            scaled[head, :, HD:] = (exact - high.astype(jnp.float32)).astype(jnp.bfloat16)

        def fresh():
            top[i] = jnp.full(top.shape[1:], LOWEST, jnp.float32)
            acc[i] = jnp.zeros(acc.shape[1:], jnp.float32)

        if early:
            fresh()
        elif middle:
            pl.when(i == 0)(fresh)

        def scores_of(t, head):
            cols = slice(head * HD, (head + 1) * HD)
            key = jnp.concatenate([pairs[at(2 * t), cols], pairs[at(2 * t + 1), cols]], axis=0)
            return score(scaled[head], jnp.concatenate([key, key], axis=1))

        def absorb(t, head, scores):
            old = top[i, head]
            new = jnp.maximum(old, jnp.max(scores, axis=1, keepdims=True))
            weights = jnp.exp2(scores - jnp.concatenate([new] * (2 * ROWS // HD), axis=1))
            cols = slice(WIDTH + head * HD, WIDTH + (head + 1) * HD)
            there = jnp.where(2 * t + 1 < count, 1.0, 0.0).astype(jnp.bfloat16)
            ones = jnp.ones((ROWS, HD), jnp.bfloat16)
            value = jnp.concatenate(
                [
                    jnp.concatenate([pairs[at(2 * t), cols], ones], axis=1),
                    jnp.concatenate([pairs[at(2 * t + 1), cols], ones], axis=1) * there,
                ],
                axis=0,
            )
            weighted = jnp.dot(
                weights.astype(jnp.bfloat16), value, preferred_element_type=jnp.float32
            )
            shrink = jnp.exp2(old - new)
            acc[i, head] = acc[i, head] * jnp.concatenate([shrink, shrink], axis=1) + weighted
            top[i, head] = new

        @pl.when(chunks > 0)
        def _():
            held[...] = scores_of(0, 0)

        def chunk(t, unused):
            scores = held[...]
            following = scores_of(t, 1)
            absorb(t, 0, scores)
            scores = scores_of(t, 2)
            absorb(t, 1, following)
            held[...] = scores_of(t + 1, 0)
            absorb(t, 2, scores)
            return 0

        lax.fori_loop(0, chunks, chunk, 0)
        if not early:
            finish(i)
        for k in range(many):

            @pl.when(i == k)
            def _():
                for copy in out_copies(k):
                    copy.start()

    def finish(i):
        lane = lax.broadcasted_iota(jnp.int32, (ROWS, HD), 1)
        stats = jnp.where(lane == 3 * HEADS_HERE, level[0].astype(jnp.float32), 0.0)
        for head in range(HEADS_HERE):
            exact = top[i, head]
            sent = exact.astype(jnp.bfloat16).astype(jnp.float32)
            factor = jnp.exp2(exact - sent)
            both = acc[i, head]
            done[i, 0:ROWS, head * HD : (head + 1) * HD] = (both[:, :HD] * factor).astype(
                jnp.bfloat16
            )
            total = both[:, HD:] * factor
            high = total.astype(jnp.bfloat16).astype(jnp.float32)
            stats = jnp.where(lane == head, sent, stats)
            stats = jnp.where(lane == HEADS_HERE + head, high, stats)
            stats = jnp.where(lane == 2 * HEADS_HERE + head, total - high, stats)
        flat = jnp.transpose(stats)[:16].astype(jnp.bfloat16)
        done[i, ROWS : ROWS + 16, :] = flat[:, :WIDTH]
        pad = jnp.zeros((16, 2 * WIDTH - ROWS), jnp.bfloat16)
        done[i, ROWS + 16 : ROWS + 32, :] = jnp.concatenate([flat[:, WIDTH:], pad], axis=1)

    if middle:
        pl.when(active(1))(run)
    else:
        run()


def attend(call, ids, live, level, queries, pairs, states=()):
    smem = pl.BlockSpec(memory_space=pltpu.SMEM)
    anywhere = pl.BlockSpec(memory_space=pl.ANY)
    bf16, f32 = jnp.bfloat16, jnp.float32
    many = len(CALLS[call])
    early = call == "early"
    members = EARLY if early else EARLY + LATER if call == "middle" else LATER
    state = [(HEADS_HERE, ROWS, 2 * HD), (HEADS_HERE, ROWS, HD)]
    if early:
        out_shape = [jax.ShapeDtypeStruct(shape, f32) for shape in state * many]
    else:
        out_shape = [jax.ShapeDtypeStruct((ROWS + STAT, WIDTH), bf16)] * many
    operands = [*queries, *[pairs[p] for p in members], *states]
    return pl.pallas_call(
        functools.partial(attend_kernel, call),
        out_shape=out_shape,
        in_specs=[smem] * 3 + [anywhere] * len(operands),
        out_specs=[anywhere] * len(out_shape),
        scratch_shapes=[
            pltpu.VMEM((many, ROWS, WIDTH), bf16),
            pltpu.VMEM((HEADS_HERE, ROWS, 2 * HD), bf16),
            pltpu.VMEM((8 * ROWS, 2 * WIDTH), bf16),
            pltpu.VMEM((ROWS, 2 * ROWS), f32),
            pltpu.VMEM((many, *state[0]), f32),
            pltpu.VMEM((many, *state[1]), f32),
            pltpu.VMEM((many, ROWS + STAT, WIDTH), bf16),
            pltpu.SemaphoreType.DMA((many,)),
            pltpu.SemaphoreType.DMA((8,)),
            pltpu.SemaphoreType.DMA((4,)),
            pltpu.SemaphoreType.DMA((2 * many,)),
        ],
        compiler_params=pltpu.CompilerParams(vmem_limit_bytes=ATTEND_VMEM),
        cost_estimate=pl.CostEstimate(
            flops=12 * HEADS_HERE * ROWS * ROWS * HD * 12, bytes_accessed=8000000, transcendentals=0
        ),
        name="attend_" + call,
    )(ids, live, level, *operands)


def combine_kernel(ids, table, *refs):
    parts, out, gate = refs[0:4], refs[4], refs[5]
    home = ids[3]
    maxima, sums = [], []
    for d in range(4):
        tail = parts[d][ROWS : ROWS + STAT, :].astype(jnp.float32)
        flat = jnp.concatenate([tail[0:16], tail[16:32, : ROWS - WIDTH]], axis=1)
        if d == 0:
            noise = flat[3 * HEADS_HERE : 3 * HEADS_HERE + 1, 0:1]
        stats = jnp.transpose(jnp.concatenate([flat, jnp.zeros((HD - 16, ROWS), jnp.float32)]))
        present = d <= home
        row_max, row_sum = [], []
        for head in range(HEADS_HERE):
            total = (
                stats[:, HEADS_HERE + head : HEADS_HERE + head + 1]
                + stats[:, 2 * HEADS_HERE + head : 2 * HEADS_HERE + head + 1]
            )
            row_max.append(jnp.where(present, stats[:, head : head + 1], LOWEST))
            row_sum.append(jnp.where(present, total, 0.0))
        maxima.append(row_max)
        sums.append(row_sum)
    for head in range(HEADS_HERE):
        at = slice(head * HD, (head + 1) * HD)
        highest = maxima[0][head]
        for d in range(1, 4):
            highest = jnp.maximum(highest, maxima[d][head])
        numerator = jnp.zeros((ROWS, HD), jnp.float32)
        denominator = jnp.zeros((ROWS, 1), jnp.float32)
        for d in range(4):
            factor = jnp.exp2(maxima[d][head] - highest)
            share = jnp.where(d <= home, parts[d][0:ROWS, at].astype(jnp.float32), 0.0)
            numerator = numerator + share * factor
            denominator = denominator + sums[d][head] * factor
        out[:, at] = (numerator / denominator).astype(jnp.bfloat16)
    index = lax.broadcasted_iota(jnp.int32, table.shape, 0).astype(jnp.float32)
    gate[...] = jnp.sum(jnp.where(index == noise, table[...], 0.0), axis=0, keepdims=True)


def combine(ids, table, parts):
    vmem = pl.BlockSpec(memory_space=pltpu.VMEM)
    return pl.pallas_call(
        combine_kernel,
        out_shape=[
            jax.ShapeDtypeStruct((ROWS, WIDTH), jnp.bfloat16),
            jax.ShapeDtypeStruct((1, table.shape[1]), jnp.float32),
        ],
        in_specs=[pl.BlockSpec(memory_space=pltpu.SMEM)] + [vmem] * 5,
        out_specs=[vmem] * 2,
        compiler_params=pltpu.CompilerParams(vmem_limit_bytes=SMALL_VMEM),
        name="combine",
    )(ids, table, *parts)


def project_kernel(far, ids, *refs):
    rows, own, fetched, swapped, out, held, sem = refs[0:4], refs[4], refs[5], refs[6], refs[7], refs[8], refs[9]
    mine = ids[2] == (1 if far else 0)

    @pl.when(mine)
    def _():
        pltpu.make_async_copy(fetched, held, sem).start()

    @pl.when(jnp.logical_not(mine))
    def _():
        pltpu.make_async_copy(swapped, held, sem).start()

    pltpu.make_async_copy(fetched, held, sem).wait()
    block = out.shape[1] // 3

    def columns(n, unused):
        at = pl.ds(pl.multiple_of(n * block, block), block)
        total = jnp.dot(rows[0][...], own[:, at], preferred_element_type=jnp.float32)
        for k in range(3):
            total = total + jnp.dot(
                rows[k + 1][...], held[k, :, at], preferred_element_type=jnp.float32
            )
        out[:, at] = total.astype(out.dtype)
        return 0

    lax.fori_loop(0, 3, columns, 0)


def project(far, ids, rows, own, fetched, swapped):
    vmem = pl.BlockSpec(memory_space=pltpu.VMEM)
    anywhere = pl.BlockSpec(memory_space=pl.ANY)
    part = own.shape[1]
    return pl.pallas_call(
        functools.partial(project_kernel, far),
        out_shape=jax.ShapeDtypeStruct((ROWS, part), jnp.bfloat16 if far else jnp.float32),
        in_specs=[pl.BlockSpec(memory_space=pltpu.SMEM)] + [vmem] * 5 + [anywhere] * 2,
        out_specs=vmem,
        scratch_shapes=[pltpu.VMEM((3, WIDTH, part), jnp.bfloat16), pltpu.SemaphoreType.DMA],
        compiler_params=pltpu.CompilerParams(vmem_limit_bytes=SMALL_VMEM),
        cost_estimate=pl.CostEstimate(
            flops=8 * ROWS * WIDTH * part, bytes_accessed=5000000, transcendentals=0
        ),
        name="project",
    )(ids, *rows, own, fetched, swapped)


def around(value, axis, steps):
    count = lax.axis_size(axis)
    return lax.ppermute(value, axis, [(i, (i + steps) % count) for i in range(count)])


def together(*values):
    return lax.optimization_barrier(values)


def per_device(hidden, queries, key_rows, values, out_weight, level_table, noise_level, group_live):
    z, y, core = lax.axis_index("z"), lax.axis_index("y"), lax.axis_index("c")
    w, x = lax.axis_index("w"), lax.axis_index("x")
    slot = z * 8 + y * 2 + core
    home = lax.rem(slot + 1, 32) // 8
    ids = jnp.stack([z, y, core, home]).astype(jnp.int32)

    def to_level(value, d):
        return lax.ppermute(value, "z", [(i, i - d) for i in range(d, 4)])

    part = out_weight.shape[1] // 8

    def columns(owner):
        return lax.dynamic_slice_in_dim(out_weight, owner * part, part, 1)

    block = jnp.where(core == 0, w, 1 - w) * 4

    def fetch(step):
        return around(columns(block + lax.rem(x + step, 4)), "x", step)

    pair = jnp.concatenate([key_rows, values], axis=1)
    next_one, next_three, below, above, pair_there, pair, queries, hidden, out_weight = together(
        to_level(queries, 1),
        to_level(queries, 3),
        around(pair, "y", 1),
        around(pair, "y", -1),
        around(pair, "c", 1),
        pair,
        queries,
        hidden,
        out_weight,
    )
    pairs = [pair, below, above, None, pair_there, None, None, None]
    states = attend(
        "early", ids, group_live, noise_level, [next_one, next_three, queries], pairs
    )
    next_two, across, below_there, above_there, piece_one, hidden, out_weight, *states = together(
        to_level(queries, 2),
        around(pair, "y", 2),
        around(below, "c", 1),
        around(above, "c", 1),
        fetch(1),
        hidden,
        out_weight,
        *states,
    )
    pairs = [pair, below, above, across, pair_there, below_there, above_there, around(across, "c", 1)]
    piece_two, piece_three = fetch(2), fetch(3)
    hidden_next = around(hidden, SLOT, -1)

    def back(share, d):
        pairs_back = [
            (8 * (i - d) + j, (8 * i + j - 1) % 32) for i in range(d, 4) for j in range(8)
        ]
        return lax.ppermute(share, SLOT, pairs_back)

    state_one, state_three, state_own = states[0:2], states[2:4], states[4:6]
    two, one = attend(
        "middle", ids, group_live, noise_level, [next_two, next_one], pairs, state_one
    )
    back_two, back_one = back(two, 2), back(one, 1)
    live_later, one = together(group_live, one)
    three, zero = attend(
        "late", ids, live_later, noise_level, [next_three, queries], pairs, state_three + state_own
    )
    three, zero, hidden_next, piece_two, piece_three, out_weight = together(
        three, zero, hidden_next, piece_two, piece_three, out_weight
    )
    back_three, back_zero = back(three, 3), back(zero, 0)
    fetched = jnp.stack([piece_one, piece_two, piece_three])
    swapped = around(fetched, "c", 1)
    weight_near, weight_far = columns(w * 4 + x), columns((1 - w) * 4 + x)
    attended, gate_row = combine(ids, level_table, [back_zero, back_one, back_two, back_three])

    rows = [attended] + [around(attended, "x", step) for step in (1, 2, 3)]
    far_sum = project(True, ids, rows, weight_far, fetched, swapped)
    arrived = around(far_sum, "w", 1)
    near_sum = project(False, ids, rows, weight_near, fetched, swapped)
    projected = near_sum + arrived.astype(jnp.float32)
    return (hidden_next.astype(jnp.float32) + gate_row * projected).astype(jnp.bfloat16)


def solution(mesh):
    fine = Mesh(np.asarray(mesh.devices).reshape(4, 4, 2, 2, 4), ("z", "y", "c", "w", "x"))
    tp = ("w", "x")
    block = P(SLOT, tp)
    in_specs = (block, block, block, block, P(tp, None), P(None, tp), P(SLOT), P())
    return jax.shard_map(
        per_device, mesh=fine, in_specs=in_specs, out_specs=block, check_vma=False
    )
```

```python
import functools
import math

import jax
import jax.numpy as jnp
import numpy as np
from jax import lax
from jax.experimental import pallas as pl
from jax.experimental.pallas import tpu as pltpu
from jax.sharding import Mesh
from jax.sharding import PartitionSpec as P

HD = 128
ROWS = 448
HEADS_HERE = 3
WIDTH = HEADS_HERE * HD
STAT = 32
LOWEST = -(2.0**100)
EXP2_SCALE = HD**-0.5 * math.log2(math.e)
Y_STEPS = (0, -1, 1, 2)
SLOT = ("z", "y", "c")
ATTEND_VMEM = 22 * 1024 * 1024
SMALL_VMEM = 8 * 1024 * 1024
WHOLE_VMEM = 60 * 1024 * 1024


def score(query, key):
    return lax.dot_general(
        query, key, (((1,), (1,)), ((), ())), preferred_element_type=jnp.float32
    )


CALLS = {"early": (1, 3, 0), "middle": (2, 1), "late": (3, 0)}
EARLY, LATER = (0, 1, 2), (3, 4, 5, 6, 7)


def attend_kernel(call, ids, live, level, *refs):
    steps = CALLS[call]
    many = len(steps)
    early, middle = call == "early", call == "middle"
    members = EARLY if early else EARLY + LATER if middle else LATER
    resumed = () if early else (1,) if middle else (0, 1)
    kept = many if early else len(resumed)
    refs = list(refs)

    def take(count):
        taken = refs[:count]
        del refs[:count]
        return taken

    query_in, pair_in = take(many), take(len(members))
    state_in = [] if early else take(2 * kept)
    out = take(2 * many if early else many)
    raw, scaled, pairs, held, acc, top, done, raw_sem, pair_sem, state_sem, out_sem = refs
    here, y, core = ids[0], ids[1], ids[2]
    first = here * 8
    mine = first + y * 2 + core
    groups = {}
    for p in members:
        core_there = core if p < 4 else 1 - core
        groups[p] = first + lax.rem(y + Y_STEPS[p % 4] + 4, 4) * 2 + core_there

    def live_before(group, part):
        count = jnp.int32(0)
        for p in part:
            if p in groups:
                count = count + jnp.where(groups[p] < group, live[groups[p]], 0)
        return count

    everything = first + 8
    n_early, n_later = live_before(everything, EARLY), live_before(everything, LATER)
    n_own = live_before(mine, EARLY if early else LATER)
    own_place = jnp.where(live[mine] == 1, n_own, n_early)

    def raw_copy(i):
        return pltpu.make_async_copy(query_in[i], raw.at[i], raw_sem.at[i])

    def place_copy(j, place):
        at = pl.ds(pl.multiple_of(place * ROWS, 64), ROWS)
        return pltpu.make_async_copy(pair_in[j], pairs.at[at], pair_sem.at[place])

    def state_copies(k):
        i = resumed[k]
        return (
            pltpu.make_async_copy(state_in[2 * k], acc.at[i], state_sem.at[2 * k]),
            pltpu.make_async_copy(state_in[2 * k + 1], top.at[i], state_sem.at[2 * k + 1]),
        )

    def out_copies(i):
        if early:
            return (
                pltpu.make_async_copy(acc.at[i], out[2 * i], out_sem.at[2 * i]),
                pltpu.make_async_copy(top.at[i], out[2 * i + 1], out_sem.at[2 * i + 1]),
            )
        return (pltpu.make_async_copy(done.at[i], out[i], out_sem.at[i]),)

    def active(i):
        return here + steps[i] <= 3

    def step_of(i):
        step = jnp.int32(steps[-1])
        for k in range(many - 1):
            step = jnp.where(i == k, steps[k], step)
        return step

    def run():
        for j, p in enumerate(members):
            part = EARLY if p in EARLY else LATER
            base = 0 if p in EARLY else 3
            if early and p == 0:
                place_copy(j, own_place).start()
            else:

                @pl.when(live[groups[p]] == 1)
                def _():
                    place_copy(j, base + live_before(groups[p], part)).start()

        for i in range(many):

            @pl.when(active(i))
            def _():
                raw_copy(i).start()

        for k in range(len(resumed)):

            @pl.when(active(resumed[k]))
            def _():
                for copy in state_copies(k):
                    copy.start()

        if early:
            place_copy(0, own_place).wait()
        for k in range(8):
            if k < 3 and call != "late":
                there = k < n_early
                if early:
                    there = there & (k != own_place)
            elif k >= 3 and not early:
                there = k - 3 < n_later
            else:
                continue

            @pl.when(there)
            def _():
                place_copy(0, k).wait()

        for i in range(many):

            @pl.when(active(i))
            def _():
                raw_copy(i).wait()

        for k in range(len(resumed)):

            @pl.when(active(resumed[k]))
            def _():
                for copy in state_copies(k):
                    copy.wait()

        def one(i, unused):
            @pl.when(here + step_of(i) <= 3)
            def _():
                source(i)

            return 0

        lax.fori_loop(0, many, one, 0)
        for i in range(many):

            @pl.when(active(i))
            def _():
                for copy in out_copies(i):
                    copy.wait()

    def source(i):
        own = step_of(i) == 0
        if early:
            count = jnp.where(own, n_own + 1, n_early)
            split, base = jnp.where(own, n_own, n_early), own_place
        elif middle:
            count = jnp.where(i == 0, n_early + n_later, n_later)
            split, base = jnp.where(i == 0, n_early, 0), 3
        else:
            count = jnp.where(own, n_own, n_later)
            split, base = jnp.int32(0), 3
        chunks = (count + 1) // 2

        def at(k):
            k = jnp.maximum(jnp.minimum(k, count - 1), 0)
            place = jnp.where(k < split, k, base + k - split)
            return pl.ds(pl.multiple_of(place * ROWS, 64), ROWS)

        for head in range(HEADS_HERE):
            exact = raw[i, :, head * HD : (head + 1) * HD].astype(jnp.float32) * EXP2_SCALE
            high = exact.astype(jnp.bfloat16)
            scaled[head, :, :HD] = high
            scaled[head, :, HD:] = (exact - high.astype(jnp.float32)).astype(jnp.bfloat16)

        def fresh():
            top[i] = jnp.full(top.shape[1:], LOWEST, jnp.float32)
            acc[i] = jnp.zeros(acc.shape[1:], jnp.float32)

        if early:
            fresh()
        elif middle:
            pl.when(i == 0)(fresh)

        def scores_of(t, head):
            cols = slice(head * HD, (head + 1) * HD)
            key = jnp.concatenate([pairs[at(2 * t), cols], pairs[at(2 * t + 1), cols]], axis=0)
            return score(scaled[head], jnp.concatenate([key, key], axis=1))

        def absorb(t, head, scores):
            old = top[i, head]
            new = jnp.maximum(old, jnp.max(scores, axis=1, keepdims=True))
            weights = jnp.exp2(scores - jnp.concatenate([new] * (2 * ROWS // HD), axis=1))
            cols = slice(WIDTH + head * HD, WIDTH + (head + 1) * HD)
            there = jnp.where(2 * t + 1 < count, 1.0, 0.0).astype(jnp.bfloat16)
            ones = jnp.ones((ROWS, HD), jnp.bfloat16)
            value = jnp.concatenate(
                [
                    jnp.concatenate([pairs[at(2 * t), cols], ones], axis=1),
                    jnp.concatenate([pairs[at(2 * t + 1), cols], ones], axis=1) * there,
                ],
                axis=0,
            )
            weighted = jnp.dot(
                weights.astype(jnp.bfloat16), value, preferred_element_type=jnp.float32
            )
            shrink = jnp.exp2(old - new)
            acc[i, head] = acc[i, head] * jnp.concatenate([shrink, shrink], axis=1) + weighted
            top[i, head] = new

        @pl.when(chunks > 0)
        def _():
            held[...] = scores_of(0, 0)

        def chunk(t, unused):
            scores = held[...]
            following = scores_of(t, 1)
            absorb(t, 0, scores)
            scores = scores_of(t, 2)
            absorb(t, 1, following)
            held[...] = scores_of(t + 1, 0)
            absorb(t, 2, scores)
            return 0

        lax.fori_loop(0, chunks, chunk, 0)
        if not early:
            finish(i)
        for k in range(many):

            @pl.when(i == k)
            def _():
                for copy in out_copies(k):
                    copy.start()

    def finish(i):
        lane = lax.broadcasted_iota(jnp.int32, (ROWS, HD), 1)
        stats = jnp.where(lane == 3 * HEADS_HERE, level[0].astype(jnp.float32), 0.0)
        for head in range(HEADS_HERE):
            exact = top[i, head]
            sent = exact.astype(jnp.bfloat16).astype(jnp.float32)
            factor = jnp.exp2(exact - sent)
            both = acc[i, head]
            done[i, 0:ROWS, head * HD : (head + 1) * HD] = (both[:, :HD] * factor).astype(
                jnp.bfloat16
            )
            total = both[:, HD:] * factor
            high = total.astype(jnp.bfloat16).astype(jnp.float32)
            stats = jnp.where(lane == head, sent, stats)
            stats = jnp.where(lane == HEADS_HERE + head, high, stats)
            stats = jnp.where(lane == 2 * HEADS_HERE + head, total - high, stats)
        flat = jnp.transpose(stats)[:16].astype(jnp.bfloat16)
        done[i, ROWS : ROWS + 16, :] = flat[:, :WIDTH]
        pad = jnp.zeros((16, 2 * WIDTH - ROWS), jnp.bfloat16)
        done[i, ROWS + 16 : ROWS + 32, :] = jnp.concatenate([flat[:, WIDTH:], pad], axis=1)

    if middle:
        pl.when(active(1))(run)
    else:
        run()


def attend(call, ids, live, level, queries, pairs, states=()):
    smem = pl.BlockSpec(memory_space=pltpu.SMEM)
    anywhere = pl.BlockSpec(memory_space=pl.ANY)
    bf16, f32 = jnp.bfloat16, jnp.float32
    many = len(CALLS[call])
    early = call == "early"
    members = EARLY if early else EARLY + LATER if call == "middle" else LATER
    state = [(HEADS_HERE, ROWS, 2 * HD), (HEADS_HERE, ROWS, HD)]
    if early:
        out_shape = [jax.ShapeDtypeStruct(shape, f32) for shape in state * many]
    else:
        out_shape = [jax.ShapeDtypeStruct((ROWS + STAT, WIDTH), bf16)] * many
    operands = [*queries, *[pairs[p] for p in members], *states]
    return pl.pallas_call(
        functools.partial(attend_kernel, call),
        out_shape=out_shape,
        in_specs=[smem] * 3 + [anywhere] * len(operands),
        out_specs=[anywhere] * len(out_shape),
        scratch_shapes=[
            pltpu.VMEM((many, ROWS, WIDTH), bf16),
            pltpu.VMEM((HEADS_HERE, ROWS, 2 * HD), bf16),
            pltpu.VMEM((8 * ROWS, 2 * WIDTH), bf16),
            pltpu.VMEM((ROWS, 2 * ROWS), f32),
            pltpu.VMEM((many, *state[0]), f32),
            pltpu.VMEM((many, *state[1]), f32),
            pltpu.VMEM((many, ROWS + STAT, WIDTH), bf16),
            pltpu.SemaphoreType.DMA((many,)),
            pltpu.SemaphoreType.DMA((8,)),
            pltpu.SemaphoreType.DMA((4,)),
            pltpu.SemaphoreType.DMA((2 * many,)),
        ],
        compiler_params=pltpu.CompilerParams(vmem_limit_bytes=ATTEND_VMEM),
        cost_estimate=pl.CostEstimate(
            flops=12 * HEADS_HERE * ROWS * ROWS * HD * 12, bytes_accessed=8000000, transcendentals=0
        ),
        name="attend_" + call,
    )(ids, live, level, *operands)


def stats_of(tail):
    tail = tail.astype(jnp.float32)
    flat = jnp.concatenate([tail[0:16], tail[16:32, : ROWS - WIDTH]], axis=1)
    noise = flat[3 * HEADS_HERE : 3 * HEADS_HERE + 1, 0:1]
    padded = jnp.concatenate([flat, jnp.zeros((HD - 16, ROWS), jnp.float32)])
    return jnp.transpose(padded), noise


def merged(parts):
    highest = parts[0][1]
    for part in parts[1:]:
        highest = jnp.maximum(highest, part[1])
    values = total = None
    for value, row_max, row_sum in parts:
        factor = jnp.exp2(row_max - highest)
        values = value * factor if values is None else values + value * factor
        total = row_sum * factor if total is None else total + row_sum * factor
    return values, highest, total


def share_of(ref, stats, head, present):
    value = ref[0:ROWS, head * HD : (head + 1) * HD].astype(jnp.float32)
    row_max = stats[:, head : head + 1]
    row_sum = (
        stats[:, HEADS_HERE + head : HEADS_HERE + head + 1]
        + stats[:, 2 * HEADS_HERE + head : 2 * HEADS_HERE + head + 1]
    )
    return (
        jnp.where(present, value, 0.0),
        jnp.where(present, row_max, LOWEST),
        jnp.where(present, row_sum, 0.0),
    )


def combine_two_kernel(ids, one, two, values, sides):
    home = ids[3]
    stats = [stats_of(ref[ROWS : ROWS + STAT, :])[0] for ref in (one, two)]
    lane = lax.broadcasted_iota(jnp.int32, (ROWS, HD), 1)
    side = jnp.zeros((ROWS, HD), jnp.float32)
    for head in range(HEADS_HERE):
        value, row_max, row_sum = merged(
            [
                share_of(one, stats[0], head, home >= 1),
                share_of(two, stats[1], head, home >= 2),
            ]
        )
        values[:, head * HD : (head + 1) * HD] = value
        side = jnp.where(lane == head, row_max, side)
        side = jnp.where(lane == HEADS_HERE + head, row_sum, side)
    sides[...] = side


def combine_two(ids, one, two):
    vmem = pl.BlockSpec(memory_space=pltpu.VMEM)
    return pl.pallas_call(
        combine_two_kernel,
        out_shape=[
            jax.ShapeDtypeStruct((ROWS, WIDTH), jnp.float32),
            jax.ShapeDtypeStruct((ROWS, HD), jnp.float32),
        ],
        in_specs=[pl.BlockSpec(memory_space=pltpu.SMEM)] + [vmem] * 2,
        out_specs=[vmem] * 2,
        compiler_params=pltpu.CompilerParams(vmem_limit_bytes=SMALL_VMEM),
        cost_estimate=pl.CostEstimate(
            flops=10**11, bytes_accessed=2 * 10**8, transcendentals=0
        ),
        name="combine_two",
    )(ids, one, two)


def combine_kernel(ids, table, zero, three, values, sides, out, gate):
    home = ids[3]
    own, noise = stats_of(zero[ROWS : ROWS + STAT, :])
    far = stats_of(three[ROWS : ROWS + STAT, :])[0]
    for head in range(HEADS_HERE):
        at = slice(head * HD, (head + 1) * HD)
        value, unused, row_sum = merged(
            [
                share_of(zero, own, head, home >= 0),
                share_of(three, far, head, home >= 3),
                (
                    values[:, at],
                    sides[:, head : head + 1],
                    sides[:, HEADS_HERE + head : HEADS_HERE + head + 1],
                ),
            ]
        )
        out[:, at] = (value / row_sum).astype(jnp.bfloat16)
    index = lax.broadcasted_iota(jnp.int32, table.shape, 0).astype(jnp.float32)
    gate[...] = jnp.sum(jnp.where(index == noise, table[...], 0.0), axis=0, keepdims=True)


def combine(ids, table, zero, three, values, sides):
    vmem = pl.BlockSpec(memory_space=pltpu.VMEM)
    return pl.pallas_call(
        combine_kernel,
        out_shape=[
            jax.ShapeDtypeStruct((ROWS, WIDTH), jnp.bfloat16),
            jax.ShapeDtypeStruct((1, table.shape[1]), jnp.float32),
        ],
        in_specs=[pl.BlockSpec(memory_space=pltpu.SMEM)] + [vmem] * 5,
        out_specs=[vmem] * 2,
        compiler_params=pltpu.CompilerParams(vmem_limit_bytes=SMALL_VMEM),
        name="combine",
    )(ids, table, zero, three, values, sides)


def finish_kernel(hidden, near, arrived, gate, out):
    projected = near[...] + arrived[...].astype(jnp.float32)
    out[...] = (hidden[...].astype(jnp.float32) + gate[...] * projected).astype(jnp.bfloat16)


def finish(hidden, near, arrived, gate):
    part = hidden.shape[1]
    rows = pl.BlockSpec((ROWS // 4, part), lambda i: (i, 0))
    return pl.pallas_call(
        finish_kernel,
        grid=(4,),
        out_shape=jax.ShapeDtypeStruct(hidden.shape, jnp.bfloat16),
        in_specs=[rows, rows, rows, pl.BlockSpec((1, part), lambda i: (0, 0))],
        out_specs=rows,
        compiler_params=pltpu.CompilerParams(vmem_limit_bytes=SMALL_VMEM),
        name="finish",
    )(hidden, near, arrived, gate)


def copies_kernel(plan, ids, *refs):
    inputs, outs, sem = refs[: plan[0]], refs[plan[0] : -1], refs[-1]
    copies = []
    for n, (kind, source, target, number) in enumerate(plan[1]):
        src, dst = inputs[source], outs[target]
        if kind == "beside":
            dst = dst.at[:, pl.ds(number * src.shape[1], src.shape[1])]
        elif kind == "columns":
            width = dst.shape[1]
            src = src.at[:, pl.ds(pl.multiple_of(ids[number] * width, width), width)]
        else:
            dst = dst.at[number]
        copies.append(pltpu.make_async_copy(src, dst, sem.at[n]))
    for copy in copies:
        copy.start()
    for copy in copies:
        copy.wait()


def copied(name, ids, inputs, shapes, plan, vmem):
    anywhere = pl.BlockSpec(memory_space=pl.ANY)
    return pl.pallas_call(
        functools.partial(copies_kernel, (len(inputs), plan)),
        out_shape=[jax.ShapeDtypeStruct(shape, jnp.bfloat16) for shape in shapes],
        in_specs=[pl.BlockSpec(memory_space=pltpu.SMEM)] + [anywhere] * len(inputs),
        out_specs=[anywhere] * len(shapes),
        scratch_shapes=[pltpu.SemaphoreType.DMA((len(plan),))],
        compiler_params=pltpu.CompilerParams(vmem_limit_bytes=vmem),
        name=name,
    )(ids, *inputs)


def project_kernel(far, ids, *refs):
    rows, own, fetched, swapped, out, held, sem = refs[0:4], refs[4], refs[5], refs[6], refs[7], refs[8], refs[9]
    mine = ids[2] == (1 if far else 0)

    @pl.when(mine)
    def _():
        pltpu.make_async_copy(fetched, held, sem).start()

    @pl.when(jnp.logical_not(mine))
    def _():
        pltpu.make_async_copy(swapped, held, sem).start()

    pltpu.make_async_copy(fetched, held, sem).wait()
    block = out.shape[1] // 3

    def columns(n, unused):
        at = pl.ds(pl.multiple_of(n * block, block), block)
        total = jnp.dot(rows[0][...], own[:, at], preferred_element_type=jnp.float32)
        for k in range(3):
            total = total + jnp.dot(
                rows[k + 1][...], held[k, :, at], preferred_element_type=jnp.float32
            )
        out[:, at] = total.astype(out.dtype)
        return 0

    lax.fori_loop(0, 3, columns, 0)


def project(far, ids, rows, own, fetched, swapped):
    vmem = pl.BlockSpec(memory_space=pltpu.VMEM)
    anywhere = pl.BlockSpec(memory_space=pl.ANY)
    part = own.shape[1]
    return pl.pallas_call(
        functools.partial(project_kernel, far),
        out_shape=jax.ShapeDtypeStruct((ROWS, part), jnp.bfloat16 if far else jnp.float32),
        in_specs=[pl.BlockSpec(memory_space=pltpu.SMEM)] + [vmem] * 5 + [anywhere] * 2,
        out_specs=vmem,
        scratch_shapes=[pltpu.VMEM((3, WIDTH, part), jnp.bfloat16), pltpu.SemaphoreType.DMA],
        compiler_params=pltpu.CompilerParams(vmem_limit_bytes=SMALL_VMEM),
        cost_estimate=pl.CostEstimate(
            flops=8 * ROWS * WIDTH * part, bytes_accessed=5 * 10**6, transcendentals=0
        ),
        name="project",
    )(ids, *rows, own, fetched, swapped)


def around(value, axis, steps):
    count = lax.axis_size(axis)
    return lax.ppermute(value, axis, [(i, (i + steps) % count) for i in range(count)])


def together(*values):
    return lax.optimization_barrier(values)


def per_device(hidden, queries, key_rows, values, out_weight, level_table, noise_level, group_live):
    z, y, core = lax.axis_index("z"), lax.axis_index("y"), lax.axis_index("c")
    w, x = lax.axis_index("w"), lax.axis_index("x")
    slot = z * 8 + y * 2 + core
    home = lax.rem(slot + 1, 32) // 8
    block = jnp.where(core == 0, w, 1 - w) * 4
    owners = [block + lax.rem(x + step, 4) for step in (1, 2, 3)] + [w * 4 + x, (1 - w) * 4 + x]
    ids = jnp.stack([z, y, core, home, *owners]).astype(jnp.int32)
    column_block = (out_weight.shape[0], out_weight.shape[1] // 8)

    def to_level(value, d):
        return lax.ppermute(value, "z", [(i, i - d) for i in range(d, 4)])

    pair, piece_one = copied(
        "pack",
        ids,
        [key_rows, values, out_weight],
        [(ROWS, 2 * WIDTH), column_block],
        (("beside", 0, 0, 0), ("beside", 1, 0, 1), ("columns", 2, 1, 4)),
        WHOLE_VMEM,
    )
    piece_two, piece_three, weight_near, weight_far = copied(
        "columns",
        ids,
        [out_weight],
        [column_block] * 4,
        tuple(("columns", 0, k, 5 + k) for k in range(4)),
        SMALL_VMEM,
    )
    (
        next_one,
        next_three,
        below,
        above,
        piece_one,
        pair,
        queries,
        hidden,
        piece_two,
        piece_three,
        weight_near,
        weight_far,
    ) = together(
        to_level(queries, 1),
        to_level(queries, 3),
        around(pair, "y", 1),
        around(pair, "y", -1),
        around(piece_one, "x", 1),
        pair,
        queries,
        hidden,
        piece_two,
        piece_three,
        weight_near,
        weight_far,
    )
    states = attend(
        "early",
        ids,
        group_live,
        noise_level,
        [next_one, next_three, queries],
        [pair, below, above],
    )
    (
        next_two,
        across,
        piece_three,
        below_there,
        above_there,
        hidden,
        piece_two,
        pair,
        *states,
    ) = together(
        to_level(queries, 2),
        around(pair, "y", 2),
        around(piece_three, "x", 3),
        around(below, "c", 1),
        around(above, "c", 1),
        hidden,
        piece_two,
        pair,
        *states,
    )
    across_there, pair_there = around(across, "c", 1), around(pair, "c", 1)
    pairs = [pair, below, above, across, pair_there, below_there, above_there, across_there]
    piece_two = around(piece_two, "x", 2)
    hidden_next = around(hidden, SLOT, -1)

    def back(share, d):
        pairs_back = [
            (8 * (i - d) + j, (8 * i + j - 1) % 32) for i in range(d, 4) for j in range(8)
        ]
        return lax.ppermute(share, SLOT, pairs_back)

    state_one, state_three, state_own = states[0:2], states[2:4], states[4:6]
    two, one = attend(
        "middle", ids, group_live, noise_level, [next_two, next_one], pairs, state_one
    )
    values_two, sides_two = combine_two(ids, back(one, 1), back(two, 2))
    live_later, one = together(group_live, one)
    three, zero = attend(
        "late", ids, live_later, noise_level, [next_three, queries], pairs, state_three + state_own
    )
    three, zero, hidden_next, piece_two = together(three, zero, hidden_next, piece_two)
    (fetched,) = copied(
        "stack",
        ids,
        [piece_one, piece_two, piece_three],
        [(3, *column_block)],
        tuple(("stack", k, 0, k) for k in range(3)),
        SMALL_VMEM,
    )
    swapped = around(fetched, "c", 1)
    attended, gate_row = combine(
        ids, level_table, back(zero, 0), back(three, 3), values_two, sides_two
    )

    rows = [attended] + [around(attended, "x", step) for step in (1, 2, 3)]
    far_sum = project(True, ids, rows, weight_far, fetched, swapped)
    arrived = around(far_sum, "w", 1)
    near_sum = project(False, ids, rows, weight_near, fetched, swapped)
    return finish(hidden_next, near_sum, arrived, gate_row)


def solution(mesh):
    fine = Mesh(np.asarray(mesh.devices).reshape(4, 4, 2, 2, 4), ("z", "y", "c", "w", "x"))
    tp = ("w", "x")
    block = P(SLOT, tp)
    in_specs = (block, block, block, block, P(tp, None), P(None, tp), P(SLOT), P())
    return jax.shard_map(
        per_device, mesh=fine, in_specs=in_specs, out_specs=block, check_vma=False
    )
```

```python
import functools
import math

import jax
import jax.numpy as jnp
import numpy as np
from jax import lax
from jax.experimental import pallas as pl
from jax.experimental.pallas import tpu as pltpu
from jax.sharding import Mesh
from jax.sharding import PartitionSpec as P

HD = 128
ROWS = 448
HEADS_HERE = 3
WIDTH = HEADS_HERE * HD
STAT = 32
LOWEST = -(2.0**100)
EXP2_SCALE = HD**-0.5 * math.log2(math.e)
Y_STEPS = (0, -1, 1, 2)
SLOT = ("z", "y", "c")
ATTEND_VMEM = 22 * 1024 * 1024
SMALL_VMEM = 8 * 1024 * 1024
WHOLE_VMEM = 60 * 1024 * 1024


def score(query, key):
    return lax.dot_general(
        query, key, (((1,), (1,)), ((), ())), preferred_element_type=jnp.float32
    )


CALLS = {"early": (1, 3, 0), "middle": (2, 1), "late": (3, 0)}
EARLY, LATER = (0, 1, 2), (3, 4, 5, 6, 7)


def attend_kernel(call, ids, live, level, *refs):
    steps = CALLS[call]
    many = len(steps)
    early, middle = call == "early", call == "middle"
    members = EARLY if early else EARLY + LATER if middle else LATER
    resumed = () if early else (1,) if middle else (0, 1)
    kept = many if early else len(resumed)
    refs = list(refs)

    def take(count):
        taken = refs[:count]
        del refs[:count]
        return taken

    query_in, pair_in = take(many), take(len(members))
    state_in = [] if early else take(2 * kept)
    out = take(2 * many if early else many)
    raw, scaled, pairs, held, acc, top, done, raw_sem, pair_sem, state_sem, out_sem = refs
    here, y, core = ids[0], ids[1], ids[2]
    first = here * 8
    mine = first + y * 2 + core
    groups = {}
    for p in members:
        core_there = core if p < 4 else 1 - core
        groups[p] = first + lax.rem(y + Y_STEPS[p % 4] + 4, 4) * 2 + core_there

    def live_before(group, part):
        count = jnp.int32(0)
        for p in part:
            if p in groups:
                count = count + jnp.where(groups[p] < group, live[groups[p]], 0)
        return count

    everything = first + 8
    n_early, n_later = live_before(everything, EARLY), live_before(everything, LATER)
    n_own = live_before(mine, EARLY if early else LATER)
    own_place = jnp.where(live[mine] == 1, n_own, n_early)

    def raw_copy(i):
        return pltpu.make_async_copy(query_in[i], raw.at[i], raw_sem.at[i])

    def place_copy(j, place):
        at = pl.ds(pl.multiple_of(place * ROWS, 64), ROWS)
        return pltpu.make_async_copy(pair_in[j], pairs.at[at], pair_sem.at[place])

    def state_copies(k):
        i = resumed[k]
        return (
            pltpu.make_async_copy(state_in[2 * k], acc.at[i], state_sem.at[2 * k]),
            pltpu.make_async_copy(state_in[2 * k + 1], top.at[i], state_sem.at[2 * k + 1]),
        )

    def out_copies(i):
        if early:
            return (
                pltpu.make_async_copy(acc.at[i], out[2 * i], out_sem.at[2 * i]),
                pltpu.make_async_copy(top.at[i], out[2 * i + 1], out_sem.at[2 * i + 1]),
            )
        return (pltpu.make_async_copy(done.at[i], out[i], out_sem.at[i]),)

    def active(i):
        return here + steps[i] <= 3

    def step_of(i):
        step = jnp.int32(steps[-1])
        for k in range(many - 1):
            step = jnp.where(i == k, steps[k], step)
        return step

    def run():
        for j, p in enumerate(members):
            part = EARLY if p in EARLY else LATER
            base = 0 if p in EARLY else 3
            if early and p == 0:
                place_copy(j, own_place).start()
            else:

                wanted = live[groups[p]] == 1
                if middle and p in EARLY:
                    wanted = wanted & active(0)
                if call == "late":
                    wanted = wanted & (active(0) | (groups[p] < mine))

                @pl.when(wanted)
                def _():
                    place_copy(j, base + live_before(groups[p], part)).start()

        for i in range(many):

            @pl.when(active(i))
            def _():
                raw_copy(i).start()

        for k in range(len(resumed)):

            @pl.when(active(resumed[k]))
            def _():
                for copy in state_copies(k):
                    copy.start()

        if early:
            place_copy(0, own_place).wait()
            for k in range(len(EARLY)):

                @pl.when((k < n_early) & (k != own_place))
                def _():
                    place_copy(0, k).wait()

        for i in range(many):

            @pl.when(active(i))
            def _():
                raw_copy(i).wait()

        def one(i, unused):
            @pl.when(here + step_of(i) <= 3)
            def _():
                source(i)

            return 0

        lax.fori_loop(0, many, one, 0)
        for i in range(many):

            @pl.when(active(i))
            def _():
                for copy in out_copies(i):
                    copy.wait()

    def source(i):
        own = step_of(i) == 0
        if early:
            count = jnp.where(own, n_own + 1, n_early)
            split, base = jnp.where(own, n_own, n_early), own_place
        elif middle:
            count = jnp.where(i == 0, n_early + n_later, n_later)
            split, base = jnp.where(i == 0, n_early, 0), 3
        else:
            count = jnp.where(own, n_own, n_later)
            split, base = jnp.int32(0), 3
        chunks = (count + 1) // 2

        waits = (i == 0) | jnp.logical_not(active(0))

        def place_of(k):
            return jnp.where(k < split, k, base + k - split)

        def arrive(t):
            if not early:
                for k in (2 * t, 2 * t + 1):

                    @pl.when(waits & (k < count))
                    def _():
                        place_copy(0, place_of(k)).wait()

        def at(k):
            place = place_of(jnp.maximum(jnp.minimum(k, count - 1), 0))
            return pl.ds(pl.multiple_of(place * ROWS, 64), ROWS)

        for head in range(HEADS_HERE):
            exact = raw[i, :, head * HD : (head + 1) * HD].astype(jnp.float32) * EXP2_SCALE
            high = exact.astype(jnp.bfloat16)
            scaled[head, :, :HD] = high
            scaled[head, :, HD:] = (exact - high.astype(jnp.float32)).astype(jnp.bfloat16)

        def fresh():
            top[i] = jnp.full(top.shape[1:], LOWEST, jnp.float32)
            acc[i] = jnp.zeros(acc.shape[1:], jnp.float32)

        if early:
            fresh()
        elif middle:
            pl.when(i == 0)(fresh)

        def scores_of(t, head):
            cols = slice(head * HD, (head + 1) * HD)
            key = jnp.concatenate([pairs[at(2 * t), cols], pairs[at(2 * t + 1), cols]], axis=0)
            return score(scaled[head], jnp.concatenate([key, key], axis=1))

        def absorb(t, head, scores):
            old = top[i, head]
            new = jnp.maximum(old, jnp.max(scores, axis=1, keepdims=True))
            weights = jnp.exp2(scores - jnp.concatenate([new] * (2 * ROWS // HD), axis=1))
            cols = slice(WIDTH + head * HD, WIDTH + (head + 1) * HD)
            there = jnp.where(2 * t + 1 < count, 1.0, 0.0).astype(jnp.bfloat16)
            ones = jnp.ones((ROWS, HD), jnp.bfloat16)
            value = jnp.concatenate(
                [
                    jnp.concatenate([pairs[at(2 * t), cols], ones], axis=1),
                    jnp.concatenate([pairs[at(2 * t + 1), cols], ones], axis=1) * there,
                ],
                axis=0,
            )
            weighted = jnp.dot(
                weights.astype(jnp.bfloat16), value, preferred_element_type=jnp.float32
            )
            shrink = jnp.exp2(old - new)
            acc[i, head] = acc[i, head] * jnp.concatenate([shrink, shrink], axis=1) + weighted
            top[i, head] = new

        arrive(0)

        @pl.when(chunks > 0)
        def _():
            held[...] = scores_of(0, 0)

        for k in range(len(resumed)):

            @pl.when(i == resumed[k])
            def _():
                for copy in state_copies(k):
                    copy.wait()

        def chunk(t, unused):
            scores = held[...]
            following = scores_of(t, 1)
            absorb(t, 0, scores)
            scores = scores_of(t, 2)
            absorb(t, 1, following)
            arrive(t + 1)
            held[...] = scores_of(t + 1, 0)
            absorb(t, 2, scores)
            return 0

        lax.fori_loop(0, chunks, chunk, 0)
        if not early:
            finish(i)
        for k in range(many):

            @pl.when(i == k)
            def _():
                for copy in out_copies(k):
                    copy.start()

    def finish(i):
        lane = lax.broadcasted_iota(jnp.int32, (ROWS, HD), 1)
        stats = jnp.where(lane == 3 * HEADS_HERE, level[0].astype(jnp.float32), 0.0)
        for head in range(HEADS_HERE):
            exact = top[i, head]
            sent = exact.astype(jnp.bfloat16).astype(jnp.float32)
            factor = jnp.exp2(exact - sent)
            both = acc[i, head]
            done[i, 0:ROWS, head * HD : (head + 1) * HD] = (both[:, :HD] * factor).astype(
                jnp.bfloat16
            )
            total = both[:, HD:] * factor
            high = total.astype(jnp.bfloat16).astype(jnp.float32)
            stats = jnp.where(lane == head, sent, stats)
            stats = jnp.where(lane == HEADS_HERE + head, high, stats)
            stats = jnp.where(lane == 2 * HEADS_HERE + head, total - high, stats)
        flat = jnp.transpose(stats)[:16].astype(jnp.bfloat16)
        done[i, ROWS : ROWS + 16, :] = flat[:, :WIDTH]
        pad = jnp.zeros((16, 2 * WIDTH - ROWS), jnp.bfloat16)
        done[i, ROWS + 16 : ROWS + 32, :] = jnp.concatenate([flat[:, WIDTH:], pad], axis=1)

    if middle:
        pl.when(active(1))(run)
    else:
        run()


def attend(call, ids, live, level, queries, pairs, states=()):
    smem = pl.BlockSpec(memory_space=pltpu.SMEM)
    anywhere = pl.BlockSpec(memory_space=pl.ANY)
    bf16, f32 = jnp.bfloat16, jnp.float32
    many = len(CALLS[call])
    early = call == "early"
    members = EARLY if early else EARLY + LATER if call == "middle" else LATER
    state = [(HEADS_HERE, ROWS, 2 * HD), (HEADS_HERE, ROWS, HD)]
    if early:
        out_shape = [jax.ShapeDtypeStruct(shape, f32) for shape in state * many]
    else:
        out_shape = [jax.ShapeDtypeStruct((ROWS + STAT, WIDTH), bf16)] * many
    operands = [*queries, *[pairs[p] for p in members], *states]
    return pl.pallas_call(
        functools.partial(attend_kernel, call),
        out_shape=out_shape,
        in_specs=[smem] * 3 + [anywhere] * len(operands),
        out_specs=[anywhere] * len(out_shape),
        scratch_shapes=[
            pltpu.VMEM((many, ROWS, WIDTH), bf16),
            pltpu.VMEM((HEADS_HERE, ROWS, 2 * HD), bf16),
            pltpu.VMEM((8 * ROWS, 2 * WIDTH), bf16),
            pltpu.VMEM((ROWS, 2 * ROWS), f32),
            pltpu.VMEM((many, *state[0]), f32),
            pltpu.VMEM((many, *state[1]), f32),
            pltpu.VMEM((many, ROWS + STAT, WIDTH), bf16),
            pltpu.SemaphoreType.DMA((many,)),
            pltpu.SemaphoreType.DMA((8,)),
            pltpu.SemaphoreType.DMA((4,)),
            pltpu.SemaphoreType.DMA((2 * many,)),
        ],
        compiler_params=pltpu.CompilerParams(vmem_limit_bytes=ATTEND_VMEM),
        cost_estimate=pl.CostEstimate(
            flops=12 * HEADS_HERE * ROWS * ROWS * HD * 12, bytes_accessed=8000000, transcendentals=0
        ),
        name="attend_" + call,
    )(ids, live, level, *operands)


def stats_of(tail):
    tail = tail.astype(jnp.float32)
    flat = jnp.concatenate([tail[0:16], tail[16:32, : ROWS - WIDTH]], axis=1)
    noise = flat[3 * HEADS_HERE : 3 * HEADS_HERE + 1, 0:1]
    padded = jnp.concatenate([flat, jnp.zeros((HD - 16, ROWS), jnp.float32)])
    return jnp.transpose(padded), noise


def merged(parts):
    highest = parts[0][1]
    for part in parts[1:]:
        highest = jnp.maximum(highest, part[1])
    values = total = None
    for value, row_max, row_sum in parts:
        factor = jnp.exp2(row_max - highest)
        values = value * factor if values is None else values + value * factor
        total = row_sum * factor if total is None else total + row_sum * factor
    return values, highest, total


def share_of(ref, stats, head, present):
    value = ref[0:ROWS, head * HD : (head + 1) * HD].astype(jnp.float32)
    row_max = stats[:, head : head + 1]
    row_sum = (
        stats[:, HEADS_HERE + head : HEADS_HERE + head + 1]
        + stats[:, 2 * HEADS_HERE + head : 2 * HEADS_HERE + head + 1]
    )
    return (
        jnp.where(present, value, 0.0),
        jnp.where(present, row_max, LOWEST),
        jnp.where(present, row_sum, 0.0),
    )


def combine_two_kernel(ids, one, two, values, sides):
    home = ids[3]
    stats = [stats_of(ref[ROWS : ROWS + STAT, :])[0] for ref in (one, two)]
    lane = lax.broadcasted_iota(jnp.int32, (ROWS, HD), 1)
    side = jnp.zeros((ROWS, HD), jnp.float32)
    for head in range(HEADS_HERE):
        value, row_max, row_sum = merged(
            [
                share_of(one, stats[0], head, home >= 1),
                share_of(two, stats[1], head, home >= 2),
            ]
        )
        values[:, head * HD : (head + 1) * HD] = value
        side = jnp.where(lane == head, row_max, side)
        side = jnp.where(lane == HEADS_HERE + head, row_sum, side)
    sides[...] = side


def combine_two(ids, one, two):
    vmem = pl.BlockSpec(memory_space=pltpu.VMEM)
    return pl.pallas_call(
        combine_two_kernel,
        out_shape=[
            jax.ShapeDtypeStruct((ROWS, WIDTH), jnp.float32),
            jax.ShapeDtypeStruct((ROWS, HD), jnp.float32),
        ],
        in_specs=[pl.BlockSpec(memory_space=pltpu.SMEM)] + [vmem] * 2,
        out_specs=[vmem] * 2,
        compiler_params=pltpu.CompilerParams(vmem_limit_bytes=SMALL_VMEM),
        cost_estimate=pl.CostEstimate(
            flops=10**11, bytes_accessed=2 * 10**8, transcendentals=0
        ),
        name="combine_two",
    )(ids, one, two)


def combine_kernel(ids, table, zero, three, values, sides, out, gate):
    home = ids[3]
    own, noise = stats_of(zero[ROWS : ROWS + STAT, :])
    far = stats_of(three[ROWS : ROWS + STAT, :])[0]
    for head in range(HEADS_HERE):
        at = slice(head * HD, (head + 1) * HD)
        value, unused, row_sum = merged(
            [
                share_of(zero, own, head, home >= 0),
                share_of(three, far, head, home >= 3),
                (
                    values[:, at],
                    sides[:, head : head + 1],
                    sides[:, HEADS_HERE + head : HEADS_HERE + head + 1],
                ),
            ]
        )
        out[:, at] = (value / row_sum).astype(jnp.bfloat16)
    index = lax.broadcasted_iota(jnp.int32, table.shape, 0).astype(jnp.float32)
    gate[...] = jnp.sum(jnp.where(index == noise, table[...], 0.0), axis=0, keepdims=True)


def combine(ids, table, zero, three, values, sides):
    vmem = pl.BlockSpec(memory_space=pltpu.VMEM)
    return pl.pallas_call(
        combine_kernel,
        out_shape=[
            jax.ShapeDtypeStruct((ROWS, WIDTH), jnp.bfloat16),
            jax.ShapeDtypeStruct((1, table.shape[1]), jnp.float32),
        ],
        in_specs=[pl.BlockSpec(memory_space=pltpu.SMEM)] + [vmem] * 5,
        out_specs=[vmem] * 2,
        compiler_params=pltpu.CompilerParams(vmem_limit_bytes=SMALL_VMEM),
        name="combine",
    )(ids, table, zero, three, values, sides)


def finish_kernel(hidden, near, arrived, gate, out):
    projected = near[...] + arrived[...].astype(jnp.float32)
    out[...] = (hidden[...].astype(jnp.float32) + gate[...] * projected).astype(jnp.bfloat16)


def finish(hidden, near, arrived, gate):
    part = hidden.shape[1]
    rows = pl.BlockSpec((ROWS // 4, part), lambda i: (i, 0))
    return pl.pallas_call(
        finish_kernel,
        grid=(4,),
        out_shape=jax.ShapeDtypeStruct(hidden.shape, jnp.bfloat16),
        in_specs=[rows, rows, rows, pl.BlockSpec((1, part), lambda i: (0, 0))],
        out_specs=rows,
        compiler_params=pltpu.CompilerParams(vmem_limit_bytes=SMALL_VMEM),
        name="finish",
    )(hidden, near, arrived, gate)


def pack_kernel(ids, keys, values, weight, pair, piece, sem):
    width = piece.shape[1]
    at = pl.ds(pl.multiple_of(ids[4] * width, width), width)
    copy = pltpu.make_async_copy(weight.at[:, at], piece, sem)
    copy.start()
    pair[:, :WIDTH] = keys[...]
    pair[:, WIDTH:] = values[...]
    copy.wait()


def pack(ids, keys, values, weight):
    vmem = pl.BlockSpec(memory_space=pltpu.VMEM)
    return pl.pallas_call(
        pack_kernel,
        out_shape=[
            jax.ShapeDtypeStruct((ROWS, 2 * WIDTH), jnp.bfloat16),
            jax.ShapeDtypeStruct((weight.shape[0], weight.shape[1] // 8), jnp.bfloat16),
        ],
        in_specs=[
            pl.BlockSpec(memory_space=pltpu.SMEM),
            vmem,
            vmem,
            pl.BlockSpec(memory_space=pl.ANY),
        ],
        out_specs=[vmem] * 2,
        scratch_shapes=[pltpu.SemaphoreType.DMA],
        compiler_params=pltpu.CompilerParams(vmem_limit_bytes=WHOLE_VMEM),
        name="pack",
    )(ids, keys, values, weight)


def copies_kernel(plan, ids, *refs):
    inputs, outs, sem = refs[: plan[0]], refs[plan[0] : -1], refs[-1]
    copies = []
    for n, (kind, source, target, number) in enumerate(plan[1]):
        src, dst = inputs[source], outs[target]
        if kind == "columns":
            width = dst.shape[1]
            src = src.at[:, pl.ds(pl.multiple_of(ids[number] * width, width), width)]
        else:
            dst = dst.at[number]
        copies.append(pltpu.make_async_copy(src, dst, sem.at[n]))
    for copy in copies:
        copy.start()
    for copy in copies:
        copy.wait()


def copied(name, ids, inputs, shapes, plan):
    anywhere = pl.BlockSpec(memory_space=pl.ANY)
    return pl.pallas_call(
        functools.partial(copies_kernel, (len(inputs), plan)),
        out_shape=[jax.ShapeDtypeStruct(shape, jnp.bfloat16) for shape in shapes],
        in_specs=[pl.BlockSpec(memory_space=pltpu.SMEM)] + [anywhere] * len(inputs),
        out_specs=[anywhere] * len(shapes),
        scratch_shapes=[pltpu.SemaphoreType.DMA((len(plan),))],
        compiler_params=pltpu.CompilerParams(vmem_limit_bytes=SMALL_VMEM),
        name=name,
    )(ids, *inputs)


def project_kernel(far, ids, *refs):
    rows, own, fetched, swapped, out, held, sem = refs[0:4], refs[4], refs[5], refs[6], refs[7], refs[8], refs[9]
    mine = ids[2] == (1 if far else 0)

    @pl.when(mine)
    def _():
        pltpu.make_async_copy(fetched, held, sem).start()

    @pl.when(jnp.logical_not(mine))
    def _():
        pltpu.make_async_copy(swapped, held, sem).start()

    pltpu.make_async_copy(fetched, held, sem).wait()
    block = out.shape[1] // 3

    def columns(n, unused):
        at = pl.ds(pl.multiple_of(n * block, block), block)
        total = jnp.dot(rows[0][...], own[:, at], preferred_element_type=jnp.float32)
        for k in range(3):
            total = total + jnp.dot(
                rows[k + 1][...], held[k, :, at], preferred_element_type=jnp.float32
            )
        out[:, at] = total.astype(out.dtype)
        return 0

    lax.fori_loop(0, 3, columns, 0)


def project(far, ids, rows, own, fetched, swapped):
    vmem = pl.BlockSpec(memory_space=pltpu.VMEM)
    anywhere = pl.BlockSpec(memory_space=pl.ANY)
    part = own.shape[1]
    return pl.pallas_call(
        functools.partial(project_kernel, far),
        out_shape=jax.ShapeDtypeStruct((ROWS, part), jnp.bfloat16 if far else jnp.float32),
        in_specs=[pl.BlockSpec(memory_space=pltpu.SMEM)] + [vmem] * 5 + [anywhere] * 2,
        out_specs=vmem,
        scratch_shapes=[pltpu.VMEM((3, WIDTH, part), jnp.bfloat16), pltpu.SemaphoreType.DMA],
        compiler_params=pltpu.CompilerParams(vmem_limit_bytes=SMALL_VMEM),
        cost_estimate=pl.CostEstimate(
            flops=8 * ROWS * WIDTH * part, bytes_accessed=5 * 10**6, transcendentals=0
        ),
        name="project",
    )(ids, *rows, own, fetched, swapped)


def around(value, axis, steps):
    count = lax.axis_size(axis)
    return lax.ppermute(value, axis, [(i, (i + steps) % count) for i in range(count)])


def together(*values):
    return lax.optimization_barrier(values)


def per_device(hidden, queries, key_rows, values, out_weight, level_table, noise_level, group_live):
    z, y, core = lax.axis_index("z"), lax.axis_index("y"), lax.axis_index("c")
    w, x = lax.axis_index("w"), lax.axis_index("x")
    slot = z * 8 + y * 2 + core
    home = lax.rem(slot + 1, 32) // 8
    block = jnp.where(core == 0, w, 1 - w) * 4
    owners = [block + lax.rem(x + step, 4) for step in (1, 2, 3)] + [w * 4 + x, (1 - w) * 4 + x]
    ids = jnp.stack([z, y, core, home, *owners]).astype(jnp.int32)
    column_block = (out_weight.shape[0], out_weight.shape[1] // 8)

    def to_level(value, d):
        return lax.ppermute(value, "z", [(i, i - d) for i in range(d, 4)])

    pair, piece_one = pack(ids, key_rows, values, out_weight)
    piece_two, piece_three, weight_near, weight_far = copied(
        "columns",
        ids,
        [out_weight],
        [column_block] * 4,
        tuple(("columns", 0, k, 5 + k) for k in range(4)),
    )
    (
        next_one,
        next_three,
        below,
        above,
        piece_one,
        pair,
        queries,
        hidden,
        piece_two,
        piece_three,
        weight_near,
        weight_far,
    ) = together(
        to_level(queries, 1),
        to_level(queries, 3),
        around(pair, "y", 1),
        around(pair, "y", -1),
        around(piece_one, "x", 1),
        pair,
        queries,
        hidden,
        piece_two,
        piece_three,
        weight_near,
        weight_far,
    )
    states = attend(
        "early",
        ids,
        group_live,
        noise_level,
        [next_one, next_three, queries],
        [pair, below, above],
    )
    (
        next_two,
        across,
        piece_three,
        below_there,
        above_there,
        hidden,
        piece_two,
        pair,
        *states,
    ) = together(
        to_level(queries, 2),
        around(pair, "y", 2),
        around(piece_three, "x", 3),
        around(below, "c", 1),
        around(above, "c", 1),
        hidden,
        piece_two,
        pair,
        *states,
    )
    across_there, pair_there = around(across, "c", 1), around(pair, "c", 1)
    pairs = [pair, below, above, across, pair_there, below_there, above_there, across_there]
    piece_two = around(piece_two, "x", 2)

    def back(share, d):
        pairs_back = [
            (8 * (i - d) + j, (8 * i + j - 1) % 32) for i in range(d, 4) for j in range(8)
        ]
        return lax.ppermute(share, SLOT, pairs_back)

    state_one, state_three, state_own = states[0:2], states[2:4], states[4:6]
    two, one = attend(
        "middle", ids, group_live, noise_level, [next_two, next_one], pairs, state_one
    )
    values_two, sides_two = combine_two(ids, back(one, 1), back(two, 2))
    live_later, one = together(group_live, one)
    three, zero = attend(
        "late", ids, live_later, noise_level, [next_three, queries], pairs, state_three + state_own
    )
    three, zero, piece_two = together(three, zero, piece_two)
    (fetched,) = copied(
        "stack",
        ids,
        [piece_one, piece_two, piece_three],
        [(3, *column_block)],
        tuple(("stack", k, 0, k) for k in range(3)),
    )
    swapped = around(fetched, "c", 1)
    attended, gate_row = combine(
        ids, level_table, back(zero, 0), back(three, 3), values_two, sides_two
    )

    attended, hidden = together(attended, hidden)
    hidden_next = around(hidden, SLOT, -1)
    rows = [attended] + [around(attended, "x", step) for step in (1, 2, 3)]
    far_sum = project(True, ids, rows, weight_far, fetched, swapped)
    arrived = around(far_sum, "w", 1)
    near_sum = project(False, ids, rows, weight_near, fetched, swapped)
    return finish(hidden_next, near_sum, arrived, gate_row)


def solution(mesh):
    fine = Mesh(np.asarray(mesh.devices).reshape(4, 4, 2, 2, 4), ("z", "y", "c", "w", "x"))
    tp = ("w", "x")
    block = P(SLOT, tp)
    in_specs = (block, block, block, block, P(tp, None), P(None, tp), P(SLOT), P())
    return jax.shard_map(
        per_device, mesh=fine, in_specs=in_specs, out_specs=block, check_vma=False
    )
```

```python
import functools
import math

import jax
import jax.numpy as jnp
import numpy as np
from jax import lax
from jax.experimental import pallas as pl
from jax.experimental.pallas import tpu as pltpu
from jax.sharding import Mesh
from jax.sharding import PartitionSpec as P

HD = 128
ROWS = 448
HEADS_HERE = 3
WIDTH = HEADS_HERE * HD
STAT = 32
LOWEST = -(2.0**100)
EXP2_SCALE = HD**-0.5 * math.log2(math.e)
Y_STEPS = (0, -1, 1, 2)
SLOT = ("z", "y", "c")
ATTEND_VMEM = 22 * 1024 * 1024
SMALL_VMEM = 8 * 1024 * 1024
WHOLE_VMEM = 60 * 1024 * 1024


def score(query, key):
    return lax.dot_general(
        query, key, (((1,), (1,)), ((), ())), preferred_element_type=jnp.float32
    )


CALLS = {"early": (1, 3), "middle": (2, 1, 3), "late": (0,)}
EARLY, LATER = (0, 1, 2, 4), (3, 5, 6, 7)


def attend_kernel(call, ids, live, level, *refs):
    steps = CALLS[call]
    many = len(steps)
    early, middle, late = call == "early", call == "middle", call == "late"
    members = EARLY if early else tuple(range(8))
    resumed = (1, 2) if middle else ()
    kept = many if early else len(resumed)
    refs = list(refs)

    def take(count):
        taken = refs[:count]
        del refs[:count]
        return taken

    query_in, pair_in = take(many), take(len(members))
    state_in = [] if early else take(2 * kept)
    out = take(2 * many if early else many)
    raw, scaled, pairs, held, acc, top, done, raw_sem, pair_sem, state_sem, out_sem = refs
    here, y, core = ids[0], ids[1], ids[2]
    first = here * 8
    mine = first + y * 2 + core
    groups = {}
    for p in members:
        core_there = core if p < 4 else 1 - core
        groups[p] = first + lax.rem(y + Y_STEPS[p % 4] + 4, 4) * 2 + core_there

    def live_before(group, part):
        count = jnp.int32(0)
        for p in part:
            if p in groups:
                count = count + jnp.where(groups[p] < group, live[groups[p]], 0)
        return count

    everything = first + 8
    if late:
        n_own = live_before(mine, members)
    else:
        n_early, n_later = live_before(everything, EARLY), live_before(everything, LATER)

    def raw_copy(i):
        return pltpu.make_async_copy(query_in[i], raw.at[i], raw_sem.at[i])

    def place_copy(j, place):
        at = pl.ds(pl.multiple_of(place * ROWS, 64), ROWS)
        return pltpu.make_async_copy(pair_in[j], pairs.at[at], pair_sem.at[place])

    def state_copies(k):
        i = resumed[k]
        return (
            pltpu.make_async_copy(state_in[2 * k], acc.at[i], state_sem.at[2 * k]),
            pltpu.make_async_copy(state_in[2 * k + 1], top.at[i], state_sem.at[2 * k + 1]),
        )

    def out_copies(i):
        if early:
            return (
                pltpu.make_async_copy(acc.at[i], out[2 * i], out_sem.at[2 * i]),
                pltpu.make_async_copy(top.at[i], out[2 * i + 1], out_sem.at[2 * i + 1]),
            )
        return (pltpu.make_async_copy(done.at[i], out[i], out_sem.at[i]),)

    def active(i):
        return here + steps[i] <= 3

    def step_of(i):
        step = jnp.int32(steps[-1])
        for k in range(many - 1):
            step = jnp.where(i == k, steps[k], step)
        return step

    def run():
        for j, p in enumerate(members):
            if late and p == 0:
                place_copy(j, n_own).start()
                continue
            wanted = live[groups[p]] == 1
            if late:
                wanted = wanted & (groups[p] < mine)
                place = live_before(groups[p], members)
            elif p in EARLY:
                wanted = wanted & active(0) if middle else wanted
                place = live_before(groups[p], EARLY)
            else:
                place = 4 + live_before(groups[p], LATER)

            @pl.when(wanted)
            def _():
                place_copy(j, place).start()

        for i in range(many):

            @pl.when(active(i))
            def _():
                raw_copy(i).start()

        for k in range(len(resumed)):

            @pl.when(active(resumed[k]))
            def _():
                for copy in state_copies(k):
                    copy.start()

        for i in range(many):

            @pl.when(active(i))
            def _():
                raw_copy(i).wait()

        def one(i, unused):
            @pl.when(here + step_of(i) <= 3)
            def _():
                source(i)

            return 0

        lax.fori_loop(0, many, one, 0)
        for i in range(many):

            @pl.when(active(i))
            def _():
                for copy in out_copies(i):
                    copy.wait()

    def source(i):
        if early:
            count, split, base = n_early, n_early, 4
        elif middle:
            count = jnp.where(i == 0, n_early + n_later, n_later)
            split, base = jnp.where(i == 0, n_early, 0), 4
        else:
            count = n_own + 1
            split, base = count, 4
        chunks = (count + 1) // 2

        waits = (i == 0) | jnp.logical_not(active(0))

        def place_of(k):
            return jnp.where(k < split, k, base + k - split)

        def arrive(t):
            for k in (2 * t, 2 * t + 1):

                @pl.when(waits & (k < count))
                def _():
                    place_copy(0, place_of(k)).wait()

        def at(k):
            place = place_of(jnp.maximum(jnp.minimum(k, count - 1), 0))
            return pl.ds(pl.multiple_of(place * ROWS, 64), ROWS)

        for head in range(HEADS_HERE):
            exact = raw[i, :, head * HD : (head + 1) * HD].astype(jnp.float32) * EXP2_SCALE
            high = exact.astype(jnp.bfloat16)
            scaled[head, :, :HD] = high
            scaled[head, :, HD:] = (exact - high.astype(jnp.float32)).astype(jnp.bfloat16)

        def fresh():
            top[i] = jnp.full(top.shape[1:], LOWEST, jnp.float32)
            acc[i] = jnp.zeros(acc.shape[1:], jnp.float32)

        if middle:
            pl.when(i == 0)(fresh)
        else:
            fresh()

        def scores_of(t, head):
            cols = slice(head * HD, (head + 1) * HD)
            key = jnp.concatenate([pairs[at(2 * t), cols], pairs[at(2 * t + 1), cols]], axis=0)
            return score(scaled[head], jnp.concatenate([key, key], axis=1))

        def absorb(t, head, scores):
            old = top[i, head]
            new = jnp.maximum(old, jnp.max(scores, axis=1, keepdims=True))
            weights = jnp.exp2(scores - jnp.concatenate([new] * (2 * ROWS // HD), axis=1))
            cols = slice(WIDTH + head * HD, WIDTH + (head + 1) * HD)
            there = jnp.where(2 * t + 1 < count, 1.0, 0.0).astype(jnp.bfloat16)
            ones = jnp.ones((ROWS, HD), jnp.bfloat16)
            value = jnp.concatenate(
                [
                    jnp.concatenate([pairs[at(2 * t), cols], ones], axis=1),
                    jnp.concatenate([pairs[at(2 * t + 1), cols], ones], axis=1) * there,
                ],
                axis=0,
            )
            weighted = jnp.dot(
                weights.astype(jnp.bfloat16), value, preferred_element_type=jnp.float32
            )
            shrink = jnp.exp2(old - new)
            acc[i, head] = acc[i, head] * jnp.concatenate([shrink, shrink], axis=1) + weighted
            top[i, head] = new

        arrive(0)

        @pl.when(chunks > 0)
        def _():
            held[...] = scores_of(0, 0)

        for k in range(len(resumed)):

            @pl.when(i == resumed[k])
            def _():
                for copy in state_copies(k):
                    copy.wait()

        def chunk(t, unused):
            scores = held[...]
            following = scores_of(t, 1)
            absorb(t, 0, scores)
            scores = scores_of(t, 2)
            absorb(t, 1, following)
            arrive(t + 1)
            held[...] = scores_of(t + 1, 0)
            absorb(t, 2, scores)
            return 0

        lax.fori_loop(0, chunks, chunk, 0)
        if not early:
            finish(i)
        for k in range(many):

            @pl.when(i == k)
            def _():
                for copy in out_copies(k):
                    copy.start()

    def finish(i):
        lane = lax.broadcasted_iota(jnp.int32, (ROWS, HD), 1)
        stats = jnp.where(lane == 3 * HEADS_HERE, level[0].astype(jnp.float32), 0.0)
        for head in range(HEADS_HERE):
            exact = top[i, head]
            sent = exact.astype(jnp.bfloat16).astype(jnp.float32)
            factor = jnp.exp2(exact - sent)
            both = acc[i, head]
            done[i, 0:ROWS, head * HD : (head + 1) * HD] = (both[:, :HD] * factor).astype(
                jnp.bfloat16
            )
            total = both[:, HD:] * factor
            high = total.astype(jnp.bfloat16).astype(jnp.float32)
            stats = jnp.where(lane == head, sent, stats)
            stats = jnp.where(lane == HEADS_HERE + head, high, stats)
            stats = jnp.where(lane == 2 * HEADS_HERE + head, total - high, stats)
        flat = jnp.transpose(stats)[:16].astype(jnp.bfloat16)
        done[i, ROWS : ROWS + 16, :] = flat[:, :WIDTH]
        pad = jnp.zeros((16, 2 * WIDTH - ROWS), jnp.bfloat16)
        done[i, ROWS + 16 : ROWS + 32, :] = jnp.concatenate([flat[:, WIDTH:], pad], axis=1)

    if late:
        run()
    else:
        pl.when(active(steps.index(1)))(run)


def attend(call, ids, live, level, queries, pairs, states=()):
    smem = pl.BlockSpec(memory_space=pltpu.SMEM)
    anywhere = pl.BlockSpec(memory_space=pl.ANY)
    bf16, f32 = jnp.bfloat16, jnp.float32
    many = len(CALLS[call])
    early = call == "early"
    members = EARLY if early else tuple(range(8))
    state = [(HEADS_HERE, ROWS, 2 * HD), (HEADS_HERE, ROWS, HD)]
    if early:
        out_shape = [jax.ShapeDtypeStruct(shape, f32) for shape in state * many]
    else:
        out_shape = [jax.ShapeDtypeStruct((ROWS + STAT, WIDTH), bf16)] * many
    operands = [*queries, *[pairs[p] for p in members], *states]
    return pl.pallas_call(
        functools.partial(attend_kernel, call),
        out_shape=out_shape,
        in_specs=[smem] * 3 + [anywhere] * len(operands),
        out_specs=[anywhere] * len(out_shape),
        scratch_shapes=[
            pltpu.VMEM((many, ROWS, WIDTH), bf16),
            pltpu.VMEM((HEADS_HERE, ROWS, 2 * HD), bf16),
            pltpu.VMEM((8 * ROWS, 2 * WIDTH), bf16),
            pltpu.VMEM((ROWS, 2 * ROWS), f32),
            pltpu.VMEM((many, *state[0]), f32),
            pltpu.VMEM((many, *state[1]), f32),
            pltpu.VMEM((many, ROWS + STAT, WIDTH), bf16),
            pltpu.SemaphoreType.DMA((many,)),
            pltpu.SemaphoreType.DMA((8,)),
            pltpu.SemaphoreType.DMA((4,)),
            pltpu.SemaphoreType.DMA((2 * many,)),
        ],
        compiler_params=pltpu.CompilerParams(vmem_limit_bytes=ATTEND_VMEM),
        cost_estimate=pl.CostEstimate(
            flops=12 * HEADS_HERE * ROWS * ROWS * HD * 12, bytes_accessed=8000000, transcendentals=0
        ),
        name="attend_" + call,
    )(ids, live, level, *operands)


def stats_of(tail):
    tail = tail.astype(jnp.float32)
    flat = jnp.concatenate([tail[0:16], tail[16:32, : ROWS - WIDTH]], axis=1)
    noise = flat[3 * HEADS_HERE : 3 * HEADS_HERE + 1, 0:1]
    padded = jnp.concatenate([flat, jnp.zeros((HD - 16, ROWS), jnp.float32)])
    return jnp.transpose(padded), noise


def merged(parts):
    highest = parts[0][1]
    for part in parts[1:]:
        highest = jnp.maximum(highest, part[1])
    values = total = None
    for value, row_max, row_sum in parts:
        factor = jnp.exp2(row_max - highest)
        values = value * factor if values is None else values + value * factor
        total = row_sum * factor if total is None else total + row_sum * factor
    return values, highest, total


def share_of(ref, stats, head, present):
    value = ref[0:ROWS, head * HD : (head + 1) * HD].astype(jnp.float32)
    row_max = stats[:, head : head + 1]
    row_sum = (
        stats[:, HEADS_HERE + head : HEADS_HERE + head + 1]
        + stats[:, 2 * HEADS_HERE + head : 2 * HEADS_HERE + head + 1]
    )
    return (
        jnp.where(present, value, 0.0),
        jnp.where(present, row_max, LOWEST),
        jnp.where(present, row_sum, 0.0),
    )


def combine_later_kernel(ids, one, two, three, values, sides):
    home = ids[3]
    stats = [stats_of(ref[ROWS : ROWS + STAT, :])[0] for ref in (one, two, three)]
    lane = lax.broadcasted_iota(jnp.int32, (ROWS, HD), 1)
    side = jnp.zeros((ROWS, HD), jnp.float32)
    for head in range(HEADS_HERE):
        value, row_max, row_sum = merged(
            [
                share_of(one, stats[0], head, home >= 1),
                share_of(two, stats[1], head, home >= 2),
                share_of(three, stats[2], head, home >= 3),
            ]
        )
        values[:, head * HD : (head + 1) * HD] = value
        side = jnp.where(lane == head, row_max, side)
        side = jnp.where(lane == HEADS_HERE + head, row_sum, side)
    sides[...] = side


def combine_later(ids, one, two, three):
    vmem = pl.BlockSpec(memory_space=pltpu.VMEM)
    return pl.pallas_call(
        combine_later_kernel,
        out_shape=[
            jax.ShapeDtypeStruct((ROWS, WIDTH), jnp.float32),
            jax.ShapeDtypeStruct((ROWS, HD), jnp.float32),
        ],
        in_specs=[pl.BlockSpec(memory_space=pltpu.SMEM)] + [vmem] * 3,
        out_specs=[vmem] * 2,
        compiler_params=pltpu.CompilerParams(vmem_limit_bytes=SMALL_VMEM),
        cost_estimate=pl.CostEstimate(
            flops=10**11, bytes_accessed=2 * 10**8, transcendentals=0
        ),
        name="combine_later",
    )(ids, one, two, three)


def combine_kernel(table, zero, values, sides, out, gate):
    own, noise = stats_of(zero[ROWS : ROWS + STAT, :])
    for head in range(HEADS_HERE):
        at = slice(head * HD, (head + 1) * HD)
        value, unused, row_sum = merged(
            [
                share_of(zero, own, head, True),
                (
                    values[:, at],
                    sides[:, head : head + 1],
                    sides[:, HEADS_HERE + head : HEADS_HERE + head + 1],
                ),
            ]
        )
        out[:, at] = (value / row_sum).astype(jnp.bfloat16)
    index = lax.broadcasted_iota(jnp.int32, table.shape, 0).astype(jnp.float32)
    gate[...] = jnp.sum(jnp.where(index == noise, table[...], 0.0), axis=0, keepdims=True)


def combine(table, zero, values, sides):
    vmem = pl.BlockSpec(memory_space=pltpu.VMEM)
    return pl.pallas_call(
        combine_kernel,
        out_shape=[
            jax.ShapeDtypeStruct((ROWS, WIDTH), jnp.bfloat16),
            jax.ShapeDtypeStruct((1, table.shape[1]), jnp.float32),
        ],
        in_specs=[vmem] * 4,
        out_specs=[vmem] * 2,
        compiler_params=pltpu.CompilerParams(vmem_limit_bytes=SMALL_VMEM),
        name="combine",
    )(table, zero, values, sides)


def finish_kernel(hidden, near, arrived, gate, out):
    projected = near[...] + arrived[...].astype(jnp.float32)
    out[...] = (hidden[...].astype(jnp.float32) + gate[...] * projected).astype(jnp.bfloat16)


def finish(hidden, near, arrived, gate):
    part = hidden.shape[1]
    rows = pl.BlockSpec((ROWS // 4, part), lambda i: (i, 0))
    return pl.pallas_call(
        finish_kernel,
        grid=(4,),
        out_shape=jax.ShapeDtypeStruct(hidden.shape, jnp.bfloat16),
        in_specs=[rows, rows, rows, pl.BlockSpec((1, part), lambda i: (0, 0))],
        out_specs=rows,
        compiler_params=pltpu.CompilerParams(vmem_limit_bytes=SMALL_VMEM),
        name="finish",
    )(hidden, near, arrived, gate)


def pack_kernel(keys, values, pair):
    pair[:, :WIDTH] = keys[...]
    pair[:, WIDTH:] = values[...]


def pack(keys, values):
    vmem = pl.BlockSpec(memory_space=pltpu.VMEM)
    return pl.pallas_call(
        pack_kernel,
        out_shape=jax.ShapeDtypeStruct((ROWS, 2 * WIDTH), jnp.bfloat16),
        in_specs=[vmem] * 2,
        out_specs=vmem,
        compiler_params=pltpu.CompilerParams(vmem_limit_bytes=WHOLE_VMEM),
        name="pack",
    )(keys, values)


def copies_kernel(plan, ids, *refs):
    inputs, outs, sem = refs[: plan[0]], refs[plan[0] : -1], refs[-1]
    copies = []
    for n, (kind, source, target, number) in enumerate(plan[1]):
        src, dst = inputs[source], outs[target]
        if kind == "columns":
            width = dst.shape[1]
            src = src.at[:, pl.ds(pl.multiple_of(ids[number] * width, width), width)]
        else:
            dst = dst.at[number]
        copies.append(pltpu.make_async_copy(src, dst, sem.at[n]))
    for copy in copies:
        copy.start()
    for copy in copies:
        copy.wait()


def copied(name, ids, inputs, shapes, plan):
    anywhere = pl.BlockSpec(memory_space=pl.ANY)
    return pl.pallas_call(
        functools.partial(copies_kernel, (len(inputs), plan)),
        out_shape=[jax.ShapeDtypeStruct(shape, jnp.bfloat16) for shape in shapes],
        in_specs=[pl.BlockSpec(memory_space=pltpu.SMEM)] + [anywhere] * len(inputs),
        out_specs=[anywhere] * len(shapes),
        scratch_shapes=[pltpu.SemaphoreType.DMA((len(plan),))],
        compiler_params=pltpu.CompilerParams(vmem_limit_bytes=SMALL_VMEM),
        name=name,
    )(ids, *inputs)


def project_kernel(far, ids, *refs):
    rows, own, fetched, swapped, out, held, sem = refs[0:4], refs[4], refs[5], refs[6], refs[7], refs[8], refs[9]
    mine = ids[2] == (1 if far else 0)

    @pl.when(mine)
    def _():
        pltpu.make_async_copy(fetched, held, sem).start()

    @pl.when(jnp.logical_not(mine))
    def _():
        pltpu.make_async_copy(swapped, held, sem).start()

    pltpu.make_async_copy(fetched, held, sem).wait()
    block = out.shape[1] // 3

    def columns(n, unused):
        at = pl.ds(pl.multiple_of(n * block, block), block)
        total = jnp.dot(rows[0][...], own[:, at], preferred_element_type=jnp.float32)
        for k in range(3):
            total = total + jnp.dot(
                rows[k + 1][...], held[k, :, at], preferred_element_type=jnp.float32
            )
        out[:, at] = total.astype(out.dtype)
        return 0

    lax.fori_loop(0, 3, columns, 0)


def project(far, ids, rows, own, fetched, swapped):
    vmem = pl.BlockSpec(memory_space=pltpu.VMEM)
    anywhere = pl.BlockSpec(memory_space=pl.ANY)
    part = own.shape[1]
    return pl.pallas_call(
        functools.partial(project_kernel, far),
        out_shape=jax.ShapeDtypeStruct((ROWS, part), jnp.bfloat16 if far else jnp.float32),
        in_specs=[pl.BlockSpec(memory_space=pltpu.SMEM)] + [vmem] * 5 + [anywhere] * 2,
        out_specs=vmem,
        scratch_shapes=[pltpu.VMEM((3, WIDTH, part), jnp.bfloat16), pltpu.SemaphoreType.DMA],
        compiler_params=pltpu.CompilerParams(vmem_limit_bytes=SMALL_VMEM),
        cost_estimate=pl.CostEstimate(
            flops=8 * ROWS * WIDTH * part, bytes_accessed=5 * 10**6, transcendentals=0
        ),
        name="project",
    )(ids, *rows, own, fetched, swapped)


def around(value, axis, steps):
    count = lax.axis_size(axis)
    return lax.ppermute(value, axis, [(i, (i + steps) % count) for i in range(count)])


def together(*values):
    return lax.optimization_barrier(values)


def per_device(hidden, queries, key_rows, values, out_weight, level_table, noise_level, group_live):
    z, y, core = lax.axis_index("z"), lax.axis_index("y"), lax.axis_index("c")
    w, x = lax.axis_index("w"), lax.axis_index("x")
    slot = z * 8 + y * 2 + core
    home = lax.rem(slot + 1, 32) // 8
    block = jnp.where(core == 0, w, 1 - w) * 4
    owners = [block + lax.rem(x + step, 4) for step in (1, 2, 3)] + [w * 4 + x, (1 - w) * 4 + x]
    ids = jnp.stack([z, y, core, home, *owners]).astype(jnp.int32)
    column_block = (out_weight.shape[0], out_weight.shape[1] // 8)

    def to_level(value, d):
        return lax.ppermute(value, "z", [(i, i - d) for i in range(d, 4)])

    pair = pack(key_rows, values)
    *pieces, weight_near, weight_far = copied(
        "columns",
        ids,
        [out_weight],
        [column_block] * 5,
        tuple(("columns", 0, k, 4 + k) for k in range(5)),
    )
    next_one, next_three, below, above, pair_there, pair, queries, hidden, *pieces = together(
        to_level(queries, 1),
        to_level(queries, 3),
        around(pair, "y", 1),
        around(pair, "y", -1),
        around(pair, "c", 1),
        pair,
        queries,
        hidden,
        *pieces,
    )
    states = attend(
        "early",
        ids,
        group_live,
        noise_level,
        [next_one, next_three],
        [pair, below, above, None, pair_there],
    )
    next_two, across, piece_three, below_there, above_there, piece_one, piece_two, *states = together(
        to_level(queries, 2),
        around(pair, "y", 2),
        around(pieces[2], "x", 3),
        around(below, "c", 1),
        around(above, "c", 1),
        pieces[0],
        pieces[1],
        *states,
    )
    across_there = around(across, "c", 1)
    pairs = [pair, below, above, across, pair_there, below_there, above_there, across_there]
    piece_one, piece_two = around(piece_one, "x", 1), around(piece_two, "x", 2)

    def back(share, d):
        pairs_back = [
            (8 * (i - d) + j, (8 * i + j - 1) % 32) for i in range(d, 4) for j in range(8)
        ]
        return lax.ppermute(share, SLOT, pairs_back)

    two, one, three = attend(
        "middle", ids, group_live, noise_level, [next_two, next_one, next_three], pairs, states
    )
    values_later, sides_later = combine_later(ids, back(one, 1), back(two, 2), back(three, 3))
    live_later, one = together(group_live, one)
    (zero,) = attend("late", ids, live_later, noise_level, [queries], pairs)
    zero, piece_one, piece_two = together(zero, piece_one, piece_two)
    (fetched,) = copied(
        "stack",
        ids,
        [piece_one, piece_two, piece_three],
        [(3, *column_block)],
        tuple(("stack", k, 0, k) for k in range(3)),
    )
    swapped = around(fetched, "c", 1)
    attended, gate_row = combine(level_table, back(zero, 0), values_later, sides_later)

    attended, hidden = together(attended, hidden)
    hidden_next = around(hidden, SLOT, -1)
    rows = [attended] + [around(attended, "x", step) for step in (1, 2, 3)]
    far_sum = project(True, ids, rows, weight_far, fetched, swapped)
    arrived = around(far_sum, "w", 1)
    near_sum = project(False, ids, rows, weight_near, fetched, swapped)
    return finish(hidden_next, near_sum, arrived, gate_row)


def solution(mesh):
    fine = Mesh(np.asarray(mesh.devices).reshape(4, 4, 2, 2, 4), ("z", "y", "c", "w", "x"))
    tp = ("w", "x")
    block = P(SLOT, tp)
    in_specs = (block, block, block, block, P(tp, None), P(None, tp), P(SLOT), P())
    return jax.shard_map(
        per_device, mesh=fine, in_specs=in_specs, out_specs=block, check_vma=False
    )
```

```python
import functools
import math

import jax
import jax.numpy as jnp
import numpy as np
from jax import lax
from jax.experimental import pallas as pl
from jax.experimental.pallas import tpu as pltpu
from jax.sharding import Mesh
from jax.sharding import PartitionSpec as P

HD = 128
ROWS = 448
HEADS_HERE = 3
WIDTH = HEADS_HERE * HD
STAT = 32
LOWEST = -(2.0**100)
EXP2_SCALE = HD**-0.5 * math.log2(math.e)
Y_STEPS = (0, -1, 1, 2)
SLOT = ("z", "y", "c")
ATTEND_VMEM = 22 * 1024 * 1024
SMALL_VMEM = 8 * 1024 * 1024
WHOLE_VMEM = 60 * 1024 * 1024


def score(query, key):
    return lax.dot_general(
        query, key, (((1,), (1,)), ((), ())), preferred_element_type=jnp.float32
    )


CALLS = {"early": (1, 3), "middle": (2, 1, 3), "late": (0,)}
EARLY, LATER = (0, 1, 2, 4), (3, 5, 6, 7)


def attend_kernel(call, ids, live, level, *refs):
    steps = CALLS[call]
    many = len(steps)
    early, middle, late = call == "early", call == "middle", call == "late"
    members = EARLY if early else tuple(range(8))
    resumed = (1, 2) if middle else ()
    kept = many if early else len(resumed)
    refs = list(refs)

    def take(count):
        taken = refs[:count]
        del refs[:count]
        return taken

    query_in, pair_in = take(many), take(len(members))
    state_in = [] if early else take(2 * kept)
    out = take(2 * many if early else many)
    raw, scaled, pairs, held, acc, top, done, raw_sem, pair_sem, state_sem, out_sem = refs
    here, y, core = ids[0], ids[1], ids[2]
    first = here * 8
    mine = first + y * 2 + core
    groups = {}
    for p in members:
        core_there = core if p < 4 else 1 - core
        groups[p] = first + lax.rem(y + Y_STEPS[p % 4] + 4, 4) * 2 + core_there

    def live_before(group, part):
        count = jnp.int32(0)
        for p in part:
            if p in groups:
                count = count + jnp.where(groups[p] < group, live[groups[p]], 0)
        return count

    everything = first + 8
    if late:
        n_own = live_before(mine, members)
    else:
        n_early, n_later = live_before(everything, EARLY), live_before(everything, LATER)

    def raw_copy(i):
        return pltpu.make_async_copy(query_in[i], raw.at[i], raw_sem.at[i])

    def place_copy(j, place):
        at = pl.ds(pl.multiple_of(place * ROWS, 64), ROWS)
        return pltpu.make_async_copy(pair_in[j], pairs.at[at], pair_sem.at[place])

    def state_copies(k):
        i = resumed[k]
        return (
            pltpu.make_async_copy(state_in[2 * k], acc.at[i], state_sem.at[2 * k]),
            pltpu.make_async_copy(state_in[2 * k + 1], top.at[i], state_sem.at[2 * k + 1]),
        )

    def out_copies(i):
        if early:
            return (
                pltpu.make_async_copy(acc.at[i], out[2 * i], out_sem.at[2 * i]),
                pltpu.make_async_copy(top.at[i], out[2 * i + 1], out_sem.at[2 * i + 1]),
            )
        return (pltpu.make_async_copy(done.at[i], out[i], out_sem.at[i]),)

    def active(i):
        return here + steps[i] <= 3

    def step_of(i):
        step = jnp.int32(steps[-1])
        for k in range(many - 1):
            step = jnp.where(i == k, steps[k], step)
        return step

    def run():
        for j, p in enumerate(members):
            if late and p == 0:
                place_copy(j, n_own).start()
                continue
            wanted = live[groups[p]] == 1
            if late:
                wanted = wanted & (groups[p] < mine)
                place = live_before(groups[p], members)
            elif p in EARLY:
                wanted = wanted & active(0) if middle else wanted
                place = live_before(groups[p], EARLY)
            else:
                place = 4 + live_before(groups[p], LATER)

            @pl.when(wanted)
            def _():
                place_copy(j, place).start()

        for i in range(many):

            @pl.when(active(i))
            def _():
                raw_copy(i).start()

        for k in range(len(resumed)):

            @pl.when(active(resumed[k]))
            def _():
                for copy in state_copies(k):
                    copy.start()

        for i in range(many):

            @pl.when(active(i))
            def _():
                raw_copy(i).wait()

        def one(i, unused):
            @pl.when(here + step_of(i) <= 3)
            def _():
                source(i)

            return 0

        lax.fori_loop(0, many, one, 0)
        for i in range(many):

            @pl.when(active(i))
            def _():
                for copy in out_copies(i):
                    copy.wait()

    def source(i):
        if early:
            count, split, base = n_early, n_early, 4
        elif middle:
            count = jnp.where(i == 0, n_early + n_later, n_later)
            split, base = jnp.where(i == 0, n_early, 0), 4
        else:
            count = n_own + 1
            split, base = count, 4
        chunks = (count + 1) // 2

        waits = (i == 0) | jnp.logical_not(active(0))

        def place_of(k):
            return jnp.where(k < split, k, base + k - split)

        def arrive(t):
            for k in (2 * t, 2 * t + 1):

                @pl.when(waits & (k < count))
                def _():
                    place_copy(0, place_of(k)).wait()

        def at(k):
            place = place_of(jnp.maximum(jnp.minimum(k, count - 1), 0))
            return pl.ds(pl.multiple_of(place * ROWS, 64), ROWS)

        for head in range(HEADS_HERE):
            exact = raw[i, :, head * HD : (head + 1) * HD].astype(jnp.float32) * EXP2_SCALE
            high = exact.astype(jnp.bfloat16)
            scaled[head, :, :HD] = high
            scaled[head, :, HD:] = (exact - high.astype(jnp.float32)).astype(jnp.bfloat16)

        def fresh():
            top[i] = jnp.full(top.shape[1:], LOWEST, jnp.float32)
            acc[i] = jnp.zeros(acc.shape[1:], jnp.float32)

        if middle:
            pl.when(i == 0)(fresh)
        else:
            fresh()

        def scores_of(t, head):
            cols = slice(head * HD, (head + 1) * HD)
            key = jnp.concatenate([pairs[at(2 * t), cols], pairs[at(2 * t + 1), cols]], axis=0)
            return score(scaled[head], jnp.concatenate([key, key], axis=1))

        def absorb(t, head, scores):
            old = top[i, head]
            new = jnp.maximum(old, jnp.max(scores, axis=1, keepdims=True))
            weights = jnp.exp2(scores - jnp.concatenate([new] * (2 * ROWS // HD), axis=1))
            cols = slice(WIDTH + head * HD, WIDTH + (head + 1) * HD)
            there = jnp.where(2 * t + 1 < count, 1.0, 0.0).astype(jnp.bfloat16)
            ones = jnp.ones((ROWS, HD), jnp.bfloat16)
            value = jnp.concatenate(
                [
                    jnp.concatenate([pairs[at(2 * t), cols], ones], axis=1),
                    jnp.concatenate([pairs[at(2 * t + 1), cols], ones], axis=1) * there,
                ],
                axis=0,
            )
            weighted = jnp.dot(
                weights.astype(jnp.bfloat16), value, preferred_element_type=jnp.float32
            )
            shrink = jnp.exp2(old - new)
            acc[i, head] = acc[i, head] * jnp.concatenate([shrink, shrink], axis=1) + weighted
            top[i, head] = new

        arrive(0)

        @pl.when(chunks > 0)
        def _():
            held[...] = scores_of(0, 0)

        for k in range(len(resumed)):

            @pl.when(i == resumed[k])
            def _():
                for copy in state_copies(k):
                    copy.wait()

        def chunk(t, unused):
            scores = held[...]
            following = scores_of(t, 1)
            absorb(t, 0, scores)
            scores = scores_of(t, 2)
            absorb(t, 1, following)
            arrive(t + 1)
            held[...] = scores_of(t + 1, 0)
            absorb(t, 2, scores)
            return 0

        lax.fori_loop(0, chunks, chunk, 0)
        if not early:
            finish(i)
        for k in range(many):

            @pl.when(i == k)
            def _():
                for copy in out_copies(k):
                    copy.start()

    def finish(i):
        lane = lax.broadcasted_iota(jnp.int32, (ROWS, HD), 1)
        stats = jnp.where(lane == 3 * HEADS_HERE, level[0].astype(jnp.float32), 0.0)
        for head in range(HEADS_HERE):
            exact = top[i, head]
            sent = exact.astype(jnp.bfloat16).astype(jnp.float32)
            factor = jnp.exp2(exact - sent)
            both = acc[i, head]
            done[i, 0:ROWS, head * HD : (head + 1) * HD] = (both[:, :HD] * factor).astype(
                jnp.bfloat16
            )
            total = both[:, HD:] * factor
            high = total.astype(jnp.bfloat16).astype(jnp.float32)
            stats = jnp.where(lane == head, sent, stats)
            stats = jnp.where(lane == HEADS_HERE + head, high, stats)
            stats = jnp.where(lane == 2 * HEADS_HERE + head, total - high, stats)
        flat = jnp.transpose(stats)[:16].astype(jnp.bfloat16)
        done[i, ROWS : ROWS + 16, :] = flat[:, :WIDTH]
        pad = jnp.zeros((16, 2 * WIDTH - ROWS), jnp.bfloat16)
        done[i, ROWS + 16 : ROWS + 32, :] = jnp.concatenate([flat[:, WIDTH:], pad], axis=1)

    if late:
        run()
    else:
        pl.when(active(steps.index(1)))(run)


def attend(call, ids, live, level, queries, pairs, states=()):
    smem = pl.BlockSpec(memory_space=pltpu.SMEM)
    anywhere = pl.BlockSpec(memory_space=pl.ANY)
    bf16, f32 = jnp.bfloat16, jnp.float32
    many = len(CALLS[call])
    early = call == "early"
    members = EARLY if early else tuple(range(8))
    state = [(HEADS_HERE, ROWS, 2 * HD), (HEADS_HERE, ROWS, HD)]
    if early:
        out_shape = [jax.ShapeDtypeStruct(shape, f32) for shape in state * many]
    else:
        out_shape = [jax.ShapeDtypeStruct((ROWS + STAT, WIDTH), bf16)] * many
    operands = [*queries, *[pairs[p] for p in members], *states]
    return pl.pallas_call(
        functools.partial(attend_kernel, call),
        out_shape=out_shape,
        in_specs=[smem] * 3 + [anywhere] * len(operands),
        out_specs=[anywhere] * len(out_shape),
        scratch_shapes=[
            pltpu.VMEM((many, ROWS, WIDTH), bf16),
            pltpu.VMEM((HEADS_HERE, ROWS, 2 * HD), bf16),
            pltpu.VMEM((8 * ROWS, 2 * WIDTH), bf16),
            pltpu.VMEM((ROWS, 2 * ROWS), f32),
            pltpu.VMEM((many, *state[0]), f32),
            pltpu.VMEM((many, *state[1]), f32),
            pltpu.VMEM((many, ROWS + STAT, WIDTH), bf16),
            pltpu.SemaphoreType.DMA((many,)),
            pltpu.SemaphoreType.DMA((8,)),
            pltpu.SemaphoreType.DMA((4,)),
            pltpu.SemaphoreType.DMA((2 * many,)),
        ],
        compiler_params=pltpu.CompilerParams(vmem_limit_bytes=ATTEND_VMEM),
        cost_estimate=pl.CostEstimate(
            flops=12 * HEADS_HERE * ROWS * ROWS * HD * 12, bytes_accessed=8000000, transcendentals=0
        ),
        name="attend_" + call,
    )(ids, live, level, *operands)


def stats_of(tail):
    tail = tail.astype(jnp.float32)
    flat = jnp.concatenate([tail[0:16], tail[16:32, : ROWS - WIDTH]], axis=1)
    noise = flat[3 * HEADS_HERE : 3 * HEADS_HERE + 1, 0:1]
    padded = jnp.concatenate([flat, jnp.zeros((HD - 16, ROWS), jnp.float32)])
    return jnp.transpose(padded), noise


def merged(parts):
    highest = parts[0][1]
    for part in parts[1:]:
        highest = jnp.maximum(highest, part[1])
    values = total = None
    for value, row_max, row_sum in parts:
        factor = jnp.exp2(row_max - highest)
        values = value * factor if values is None else values + value * factor
        total = row_sum * factor if total is None else total + row_sum * factor
    return values, highest, total


def share_of(ref, stats, head, present):
    value = ref[0:ROWS, head * HD : (head + 1) * HD].astype(jnp.float32)
    row_max = stats[:, head : head + 1]
    row_sum = (
        stats[:, HEADS_HERE + head : HEADS_HERE + head + 1]
        + stats[:, 2 * HEADS_HERE + head : 2 * HEADS_HERE + head + 1]
    )
    return (
        jnp.where(present, value, 0.0),
        jnp.where(present, row_max, LOWEST),
        jnp.where(present, row_sum, 0.0),
    )


def combine_later_kernel(ids, one_first, one_later, two_first, two_later, three, values, sides):
    home = ids[3]
    lane = lax.broadcasted_iota(jnp.int32, (ROWS, HD), 1)

    def picked(first, later, is_first):
        return jnp.where(is_first, first[...], later[...])

    shares = (
        (picked(one_first, one_later, home == 1), home >= 1),
        (picked(two_first, two_later, home == 2), home >= 2),
        (three[...], home >= 3),
    )
    stats = [stats_of(share[ROWS : ROWS + STAT, :])[0] for share, unused in shares]
    side = jnp.zeros((ROWS, HD), jnp.float32)
    for head in range(HEADS_HERE):
        value, row_max, row_sum = merged(
            [
                share_of(share, stat, head, present)
                for (share, present), stat in zip(shares, stats)
            ]
        )
        values[:, head * HD : (head + 1) * HD] = value
        side = jnp.where(lane == head, row_max, side)
        side = jnp.where(lane == HEADS_HERE + head, row_sum, side)
    sides[...] = side


def combine_later(ids, ones, twos, three):
    vmem = pl.BlockSpec(memory_space=pltpu.VMEM)
    return pl.pallas_call(
        combine_later_kernel,
        out_shape=[
            jax.ShapeDtypeStruct((ROWS, WIDTH), jnp.float32),
            jax.ShapeDtypeStruct((ROWS, HD), jnp.float32),
        ],
        in_specs=[pl.BlockSpec(memory_space=pltpu.SMEM)] + [vmem] * 5,
        out_specs=[vmem] * 2,
        compiler_params=pltpu.CompilerParams(vmem_limit_bytes=SMALL_VMEM),
        cost_estimate=pl.CostEstimate(
            flops=10**11, bytes_accessed=2 * 10**8, transcendentals=0
        ),
        name="combine_later",
    )(ids, *ones, *twos, three)


def combine_kernel(table, zero, values, sides, out, gate):
    own, noise = stats_of(zero[ROWS : ROWS + STAT, :])
    for head in range(HEADS_HERE):
        at = slice(head * HD, (head + 1) * HD)
        value, unused, row_sum = merged(
            [
                share_of(zero, own, head, True),
                (
                    values[:, at],
                    sides[:, head : head + 1],
                    sides[:, HEADS_HERE + head : HEADS_HERE + head + 1],
                ),
            ]
        )
        out[:, at] = (value / row_sum).astype(jnp.bfloat16)
    index = lax.broadcasted_iota(jnp.int32, table.shape, 0).astype(jnp.float32)
    gate[...] = jnp.sum(jnp.where(index == noise, table[...], 0.0), axis=0, keepdims=True)


def combine(table, zero, values, sides):
    vmem = pl.BlockSpec(memory_space=pltpu.VMEM)
    return pl.pallas_call(
        combine_kernel,
        out_shape=[
            jax.ShapeDtypeStruct((ROWS, WIDTH), jnp.bfloat16),
            jax.ShapeDtypeStruct((1, table.shape[1]), jnp.float32),
        ],
        in_specs=[vmem] * 4,
        out_specs=[vmem] * 2,
        compiler_params=pltpu.CompilerParams(vmem_limit_bytes=SMALL_VMEM),
        name="combine",
    )(table, zero, values, sides)


def finish_kernel(hidden, near, arrived, gate, out):
    projected = near[...] + arrived[...].astype(jnp.float32)
    out[...] = (hidden[...].astype(jnp.float32) + gate[...] * projected).astype(jnp.bfloat16)


def finish(hidden, near, arrived, gate):
    part = hidden.shape[1]
    rows = pl.BlockSpec((ROWS // 4, part), lambda i: (i, 0))
    return pl.pallas_call(
        finish_kernel,
        grid=(4,),
        out_shape=jax.ShapeDtypeStruct(hidden.shape, jnp.bfloat16),
        in_specs=[rows, rows, rows, pl.BlockSpec((1, part), lambda i: (0, 0))],
        out_specs=rows,
        compiler_params=pltpu.CompilerParams(vmem_limit_bytes=SMALL_VMEM),
        name="finish",
    )(hidden, near, arrived, gate)


def pack_kernel(keys, values, pair):
    pair[:, :WIDTH] = keys[...]
    pair[:, WIDTH:] = values[...]


def pack(keys, values):
    vmem = pl.BlockSpec(memory_space=pltpu.VMEM)
    return pl.pallas_call(
        pack_kernel,
        out_shape=jax.ShapeDtypeStruct((ROWS, 2 * WIDTH), jnp.bfloat16),
        in_specs=[vmem] * 2,
        out_specs=vmem,
        compiler_params=pltpu.CompilerParams(vmem_limit_bytes=WHOLE_VMEM),
        name="pack",
    )(keys, values)


def copies_kernel(plan, ids, *refs):
    inputs, outs, sem = refs[: plan[0]], refs[plan[0] : -1], refs[-1]
    copies = []
    for n, (kind, source, target, number) in enumerate(plan[1]):
        src, dst = inputs[source], outs[target]
        if kind == "columns":
            width = dst.shape[1]
            src = src.at[:, pl.ds(pl.multiple_of(ids[number] * width, width), width)]
        else:
            dst = dst.at[number]
        copies.append(pltpu.make_async_copy(src, dst, sem.at[n]))
    for copy in copies:
        copy.start()
    for copy in copies:
        copy.wait()


def copied(name, ids, inputs, shapes, plan):
    anywhere = pl.BlockSpec(memory_space=pl.ANY)
    return pl.pallas_call(
        functools.partial(copies_kernel, (len(inputs), plan)),
        out_shape=[jax.ShapeDtypeStruct(shape, jnp.bfloat16) for shape in shapes],
        in_specs=[pl.BlockSpec(memory_space=pltpu.SMEM)] + [anywhere] * len(inputs),
        out_specs=[anywhere] * len(shapes),
        scratch_shapes=[pltpu.SemaphoreType.DMA((len(plan),))],
        compiler_params=pltpu.CompilerParams(vmem_limit_bytes=SMALL_VMEM),
        name=name,
    )(ids, *inputs)


def project_kernel(far, ids, *refs):
    rows, own, fetched, swapped, out, held, sem = refs[0:4], refs[4], refs[5], refs[6], refs[7], refs[8], refs[9]
    mine = ids[2] == (1 if far else 0)

    @pl.when(mine)
    def _():
        pltpu.make_async_copy(fetched, held, sem).start()

    @pl.when(jnp.logical_not(mine))
    def _():
        pltpu.make_async_copy(swapped, held, sem).start()

    pltpu.make_async_copy(fetched, held, sem).wait()
    block = out.shape[1] // 3

    def columns(n, unused):
        at = pl.ds(pl.multiple_of(n * block, block), block)
        total = jnp.dot(rows[0][...], own[:, at], preferred_element_type=jnp.float32)
        for k in range(3):
            total = total + jnp.dot(
                rows[k + 1][...], held[k, :, at], preferred_element_type=jnp.float32
            )
        out[:, at] = total.astype(out.dtype)
        return 0

    lax.fori_loop(0, 3, columns, 0)


def project(far, ids, rows, own, fetched, swapped):
    vmem = pl.BlockSpec(memory_space=pltpu.VMEM)
    anywhere = pl.BlockSpec(memory_space=pl.ANY)
    part = own.shape[1]
    return pl.pallas_call(
        functools.partial(project_kernel, far),
        out_shape=jax.ShapeDtypeStruct((ROWS, part), jnp.bfloat16 if far else jnp.float32),
        in_specs=[pl.BlockSpec(memory_space=pltpu.SMEM)] + [vmem] * 5 + [anywhere] * 2,
        out_specs=vmem,
        scratch_shapes=[pltpu.VMEM((3, WIDTH, part), jnp.bfloat16), pltpu.SemaphoreType.DMA],
        compiler_params=pltpu.CompilerParams(vmem_limit_bytes=SMALL_VMEM),
        cost_estimate=pl.CostEstimate(
            flops=8 * ROWS * WIDTH * part, bytes_accessed=5 * 10**6, transcendentals=0
        ),
        name="project",
    )(ids, *rows, own, fetched, swapped)


def around(value, axis, steps):
    count = lax.axis_size(axis)
    return lax.ppermute(value, axis, [(i, (i + steps) % count) for i in range(count)])


def together(*values):
    return lax.optimization_barrier(values)


def per_device(hidden, queries, key_rows, values, out_weight, level_table, noise_level, group_live):
    z, y, core = lax.axis_index("z"), lax.axis_index("y"), lax.axis_index("c")
    w, x = lax.axis_index("w"), lax.axis_index("x")
    slot = z * 8 + y * 2 + core
    home = lax.rem(slot + 1, 32) // 8
    block = jnp.where(core == 0, w, 1 - w) * 4
    owners = [block + lax.rem(x + step, 4) for step in (1, 2, 3)] + [w * 4 + x, (1 - w) * 4 + x]
    ids = jnp.stack([z, y, core, home, *owners]).astype(jnp.int32)
    column_block = (out_weight.shape[0], out_weight.shape[1] // 8)

    def to_level(value, d):
        return lax.ppermute(value, "z", [(i, i - d) for i in range(d, 4)])

    pair = pack(key_rows, values)
    *pieces, weight_near, weight_far = copied(
        "columns",
        ids,
        [out_weight],
        [column_block] * 5,
        tuple(("columns", 0, k, 4 + k) for k in range(5)),
    )
    next_one, next_three, below, above, pair_there, pair, queries, hidden, *pieces = together(
        to_level(queries, 1),
        to_level(queries, 3),
        around(pair, "y", 1),
        around(pair, "y", -1),
        around(pair, "c", 1),
        pair,
        queries,
        hidden,
        *pieces,
    )
    states = attend(
        "early",
        ids,
        group_live,
        noise_level,
        [next_one, next_three],
        [pair, below, above, None, pair_there],
    )
    next_two, across, piece_one, piece_three, below_there, piece_two, above, *states = together(
        to_level(queries, 2),
        around(pair, "y", 2),
        around(pieces[0], "x", 1),
        around(pieces[2], "x", 3),
        around(below, "c", 1),
        pieces[1],
        above,
        *states,
    )
    above_there, across_there = around(above, "c", 1), around(across, "c", 1)
    pairs = [pair, below, above, across, pair_there, below_there, above_there, across_there]
    piece_two = around(piece_two, "x", 2)

    def back(share, d, levels):
        pairs_back = [(8 * i + j, (8 * (i + d) + j - 1) % 32) for i in levels for j in range(8)]
        return lax.ppermute(share, SLOT, pairs_back)

    two, one, three = attend(
        "middle", ids, group_live, noise_level, [next_two, next_one, next_three], pairs, states
    )
    one_later, two_later = back(one, 1, (1, 2)), back(two, 2, (1,))
    one_first, two_first, three_first, piece_two = together(one, two, three, piece_two)
    values_later, sides_later = combine_later(
        ids,
        [back(one_first, 1, (0,)), one_later],
        [back(two_first, 2, (0,)), two_later],
        back(three_first, 3, (0,)),
    )
    live_later, one = together(group_live, one)
    (zero,) = attend("late", ids, live_later, noise_level, [queries], pairs)
    zero, one_later, two_later = together(zero, one_later, two_later)
    (fetched,) = copied(
        "stack",
        ids,
        [piece_one, piece_two, piece_three],
        [(3, *column_block)],
        tuple(("stack", k, 0, k) for k in range(3)),
    )
    swapped = around(fetched, "c", 1)
    attended, gate_row = combine(
        level_table, back(zero, 0, (0, 1, 2, 3)), values_later, sides_later
    )

    attended, hidden = together(attended, hidden)
    hidden_next = around(hidden, SLOT, -1)
    rows = [attended] + [around(attended, "x", step) for step in (1, 2, 3)]
    far_sum = project(True, ids, rows, weight_far, fetched, swapped)
    arrived = around(far_sum, "w", 1)
    near_sum = project(False, ids, rows, weight_near, fetched, swapped)
    return finish(hidden_next, near_sum, arrived, gate_row)


def solution(mesh):
    fine = Mesh(np.asarray(mesh.devices).reshape(4, 4, 2, 2, 4), ("z", "y", "c", "w", "x"))
    tp = ("w", "x")
    block = P(SLOT, tp)
    in_specs = (block, block, block, block, P(tp, None), P(None, tp), P(SLOT), P())
    return jax.shard_map(
        per_device, mesh=fine, in_specs=in_specs, out_specs=block, check_vma=False
    )
```

```python
import functools
import math

import jax
import jax.numpy as jnp
import numpy as np
from jax import lax
from jax.experimental import pallas as pl
from jax.experimental.pallas import tpu as pltpu
from jax.sharding import Mesh
from jax.sharding import PartitionSpec as P

HD = 128
ROWS = 448
HEADS_HERE = 3
WIDTH = HEADS_HERE * HD
STAT = 32
LOWEST = -(2.0**100)
EXP2_SCALE = HD**-0.5 * math.log2(math.e)
Y_STEPS = (0, -1, 1, 2)
SLOT = ("z", "y", "c")
ATTEND_VMEM = 22 * 1024 * 1024
SMALL_VMEM = 8 * 1024 * 1024
WHOLE_VMEM = 60 * 1024 * 1024


def score(query, key):
    return lax.dot_general(
        query, key, (((1,), (1,)), ((), ())), preferred_element_type=jnp.float32
    )


CALLS = {"early": (1, 3), "middle": (1, 3), "third": (2,), "late": (0,)}
EARLY, LATER, ALL = (0, 1, 2, 4), (3, 5, 6, 7), tuple(range(8))
COSTS = {"early": 10**10, "middle": 10**10, "third": 5 * 10**10, "late": 10**6}
MEMBERS = {"early": EARLY, "middle": LATER, "third": ALL, "late": ALL}


def attend_kernel(call, ids, live, level, *refs):
    steps = CALLS[call]
    many = len(steps)
    early, middle, late = call == "early", call == "middle", call == "late"
    members = MEMBERS[call]
    resumed = (0, 1) if middle else ()
    kept = many if early else len(resumed)
    refs = list(refs)

    def take(count):
        taken = refs[:count]
        del refs[:count]
        return taken

    query_in, pair_in = take(many), take(len(members))
    state_in = [] if early else take(2 * kept)
    out = take(2 * many if early else many)
    raw, scaled, pairs, held, acc, top, done, raw_sem, pair_sem, state_sem, out_sem = refs
    here, y, core = ids[0], ids[1], ids[2]
    first = here * 8
    mine = first + y * 2 + core
    groups = {}
    for p in members:
        core_there = core if p < 4 else 1 - core
        groups[p] = first + lax.rem(y + Y_STEPS[p % 4] + 4, 4) * 2 + core_there

    def live_before(group):
        count = jnp.int32(0)
        for p in members:
            count = count + jnp.where(groups[p] < group, live[groups[p]], 0)
        return count

    bound = mine if late else first + 8
    n_live = live_before(bound)
    count = n_live + 1 if late else n_live
    chunks = (count + 1) // 2

    def raw_copy(i):
        return pltpu.make_async_copy(query_in[i], raw.at[i], raw_sem.at[i])

    def place_copy(j, place):
        at = pl.ds(pl.multiple_of(place * ROWS, 64), ROWS)
        return pltpu.make_async_copy(pair_in[j], pairs.at[at], pair_sem.at[place])

    def state_copies(k):
        i = resumed[k]
        return (
            pltpu.make_async_copy(state_in[2 * k], acc.at[i], state_sem.at[2 * k]),
            pltpu.make_async_copy(state_in[2 * k + 1], top.at[i], state_sem.at[2 * k + 1]),
        )

    def out_copies(i):
        if early:
            return (
                pltpu.make_async_copy(acc.at[i], out[2 * i], out_sem.at[2 * i]),
                pltpu.make_async_copy(top.at[i], out[2 * i + 1], out_sem.at[2 * i + 1]),
            )
        return (pltpu.make_async_copy(done.at[i], out[i], out_sem.at[i]),)

    def active(i):
        return here + steps[i] <= 3

    def step_of(i):
        step = jnp.int32(steps[-1])
        for k in range(many - 1):
            step = jnp.where(i == k, steps[k], step)
        return step

    def run():
        for j, p in enumerate(members):
            if late and p == 0:
                place_copy(j, n_live).start()
                continue

            @pl.when((live[groups[p]] == 1) & (groups[p] < bound))
            def _():
                place_copy(j, live_before(groups[p])).start()

        for i in range(many):

            @pl.when(active(i))
            def _():
                raw_copy(i).start()

        for k in range(len(resumed)):

            @pl.when(active(resumed[k]))
            def _():
                for copy in state_copies(k):
                    copy.start()

        for i in range(many):

            @pl.when(active(i))
            def _():
                raw_copy(i).wait()

        def one(i, unused):
            @pl.when(here + step_of(i) <= 3)
            def _():
                source(i)

            return 0

        lax.fori_loop(0, many, one, 0)
        for i in range(many):

            @pl.when(active(i))
            def _():
                for copy in out_copies(i):
                    copy.wait()

    def source(i):
        waits = i == 0

        def arrive(t):
            for k in (2 * t, 2 * t + 1):

                @pl.when(waits & (k < count))
                def _():
                    place_copy(0, k).wait()

        def at(k):
            place = jnp.maximum(jnp.minimum(k, count - 1), 0)
            return pl.ds(pl.multiple_of(place * ROWS, 64), ROWS)

        for head in range(HEADS_HERE):
            exact = raw[i, :, head * HD : (head + 1) * HD].astype(jnp.float32) * EXP2_SCALE
            high = exact.astype(jnp.bfloat16)
            scaled[head, :, :HD] = high
            scaled[head, :, HD:] = (exact - high.astype(jnp.float32)).astype(jnp.bfloat16)

        def fresh():
            top[i] = jnp.full(top.shape[1:], LOWEST, jnp.float32)
            acc[i] = jnp.zeros(acc.shape[1:], jnp.float32)

        if not middle:
            fresh()

        def scores_of(t, head):
            cols = slice(head * HD, (head + 1) * HD)
            key = jnp.concatenate([pairs[at(2 * t), cols], pairs[at(2 * t + 1), cols]], axis=0)
            return score(scaled[head], jnp.concatenate([key, key], axis=1))

        def absorb(t, head, scores):
            old = top[i, head]
            new = jnp.maximum(old, jnp.max(scores, axis=1, keepdims=True))
            weights = jnp.exp2(scores - jnp.concatenate([new] * (2 * ROWS // HD), axis=1))
            cols = slice(WIDTH + head * HD, WIDTH + (head + 1) * HD)
            there = jnp.where(2 * t + 1 < count, 1.0, 0.0).astype(jnp.bfloat16)
            ones = jnp.ones((ROWS, HD), jnp.bfloat16)
            value = jnp.concatenate(
                [
                    jnp.concatenate([pairs[at(2 * t), cols], ones], axis=1),
                    jnp.concatenate([pairs[at(2 * t + 1), cols], ones], axis=1) * there,
                ],
                axis=0,
            )
            weighted = jnp.dot(
                weights.astype(jnp.bfloat16), value, preferred_element_type=jnp.float32
            )
            shrink = jnp.exp2(old - new)
            acc[i, head] = acc[i, head] * jnp.concatenate([shrink, shrink], axis=1) + weighted
            top[i, head] = new

        arrive(0)

        @pl.when(chunks > 0)
        def _():
            held[...] = scores_of(0, 0)

        for k in range(len(resumed)):

            @pl.when(i == resumed[k])
            def _():
                for copy in state_copies(k):
                    copy.wait()

        def chunk(t, unused):
            scores = held[...]
            following = scores_of(t, 1)
            absorb(t, 0, scores)
            scores = scores_of(t, 2)
            absorb(t, 1, following)
            arrive(t + 1)
            held[...] = scores_of(t + 1, 0)
            absorb(t, 2, scores)
            return 0

        lax.fori_loop(0, chunks, chunk, 0)
        if not early:
            finish(i)
        for k in range(many):

            @pl.when(i == k)
            def _():
                for copy in out_copies(k):
                    copy.start()

    def finish(i):
        lane = lax.broadcasted_iota(jnp.int32, (ROWS, HD), 1)
        stats = jnp.where(lane == 3 * HEADS_HERE, level[0].astype(jnp.float32), 0.0)
        for head in range(HEADS_HERE):
            exact = top[i, head]
            sent = exact.astype(jnp.bfloat16).astype(jnp.float32)
            factor = jnp.exp2(exact - sent)
            both = acc[i, head]
            done[i, 0:ROWS, head * HD : (head + 1) * HD] = (both[:, :HD] * factor).astype(
                jnp.bfloat16
            )
            total = both[:, HD:] * factor
            high = total.astype(jnp.bfloat16).astype(jnp.float32)
            stats = jnp.where(lane == head, sent, stats)
            stats = jnp.where(lane == HEADS_HERE + head, high, stats)
            stats = jnp.where(lane == 2 * HEADS_HERE + head, total - high, stats)
        flat = jnp.transpose(stats)[:16].astype(jnp.bfloat16)
        done[i, ROWS : ROWS + 16, :] = flat[:, :WIDTH]
        pad = jnp.zeros((16, 2 * WIDTH - ROWS), jnp.bfloat16)
        done[i, ROWS + 16 : ROWS + 32, :] = jnp.concatenate([flat[:, WIDTH:], pad], axis=1)

    pl.when(active(0))(run)


def attend(call, ids, live, level, queries, pairs, states=()):
    smem = pl.BlockSpec(memory_space=pltpu.SMEM)
    anywhere = pl.BlockSpec(memory_space=pl.ANY)
    bf16, f32 = jnp.bfloat16, jnp.float32
    many = len(CALLS[call])
    early = call == "early"
    members = MEMBERS[call]
    state = [(HEADS_HERE, ROWS, 2 * HD), (HEADS_HERE, ROWS, HD)]
    if early:
        out_shape = [jax.ShapeDtypeStruct(shape, f32) for shape in state * many]
    else:
        out_shape = [jax.ShapeDtypeStruct((ROWS + STAT, WIDTH), bf16)] * many
    operands = [*queries, *[pairs[p] for p in members], *states]
    return pl.pallas_call(
        functools.partial(attend_kernel, call),
        out_shape=out_shape,
        in_specs=[smem] * 3 + [anywhere] * len(operands),
        out_specs=[anywhere] * len(out_shape),
        scratch_shapes=[
            pltpu.VMEM((many, ROWS, WIDTH), bf16),
            pltpu.VMEM((HEADS_HERE, ROWS, 2 * HD), bf16),
            pltpu.VMEM((8 * ROWS, 2 * WIDTH), bf16),
            pltpu.VMEM((ROWS, 2 * ROWS), f32),
            pltpu.VMEM((many, *state[0]), f32),
            pltpu.VMEM((many, *state[1]), f32),
            pltpu.VMEM((many, ROWS + STAT, WIDTH), bf16),
            pltpu.SemaphoreType.DMA((many,)),
            pltpu.SemaphoreType.DMA((8,)),
            pltpu.SemaphoreType.DMA((4,)),
            pltpu.SemaphoreType.DMA((2 * many,)),
        ],
        compiler_params=pltpu.CompilerParams(vmem_limit_bytes=ATTEND_VMEM),
        cost_estimate=pl.CostEstimate(
            flops=COSTS[call], bytes_accessed=10**6, transcendentals=0
        ),
        name="attend_" + call,
    )(ids, live, level, *operands)


def stats_of(tail):
    tail = tail.astype(jnp.float32)
    flat = jnp.concatenate([tail[0:16], tail[16:32, : ROWS - WIDTH]], axis=1)
    noise = flat[3 * HEADS_HERE : 3 * HEADS_HERE + 1, 0:1]
    padded = jnp.concatenate([flat, jnp.zeros((HD - 16, ROWS), jnp.float32)])
    return jnp.transpose(padded), noise


def merged(parts):
    highest = parts[0][1]
    for part in parts[1:]:
        highest = jnp.maximum(highest, part[1])
    values = total = None
    for value, row_max, row_sum in parts:
        factor = jnp.exp2(row_max - highest)
        values = value * factor if values is None else values + value * factor
        total = row_sum * factor if total is None else total + row_sum * factor
    return values, highest, total


def share_of(ref, stats, head, present):
    value = ref[0:ROWS, head * HD : (head + 1) * HD].astype(jnp.float32)
    row_max = stats[:, head : head + 1]
    row_sum = (
        stats[:, HEADS_HERE + head : HEADS_HERE + head + 1]
        + stats[:, 2 * HEADS_HERE + head : 2 * HEADS_HERE + head + 1]
    )
    return (
        jnp.where(present, value, 0.0),
        jnp.where(present, row_max, LOWEST),
        jnp.where(present, row_sum, 0.0),
    )


def combine_later_kernel(ids, one, two, three, values, sides):
    home = ids[3]
    stats = [stats_of(ref[ROWS : ROWS + STAT, :])[0] for ref in (one, two, three)]
    lane = lax.broadcasted_iota(jnp.int32, (ROWS, HD), 1)
    side = jnp.zeros((ROWS, HD), jnp.float32)
    for head in range(HEADS_HERE):
        value, row_max, row_sum = merged(
            [
                share_of(one, stats[0], head, home >= 1),
                share_of(two, stats[1], head, home >= 2),
                share_of(three, stats[2], head, home >= 3),
            ]
        )
        values[:, head * HD : (head + 1) * HD] = value
        side = jnp.where(lane == head, row_max, side)
        side = jnp.where(lane == HEADS_HERE + head, row_sum, side)
    sides[...] = side


def combine_later(ids, one, two, three):
    vmem = pl.BlockSpec(memory_space=pltpu.VMEM)
    return pl.pallas_call(
        combine_later_kernel,
        out_shape=[
            jax.ShapeDtypeStruct((ROWS, WIDTH), jnp.float32),
            jax.ShapeDtypeStruct((ROWS, HD), jnp.float32),
        ],
        in_specs=[pl.BlockSpec(memory_space=pltpu.SMEM)] + [vmem] * 3,
        out_specs=[vmem] * 2,
        compiler_params=pltpu.CompilerParams(vmem_limit_bytes=SMALL_VMEM),
        cost_estimate=pl.CostEstimate(
            flops=10**11, bytes_accessed=2 * 10**8, transcendentals=0
        ),
        name="combine_later",
    )(ids, one, two, three)


def combine_kernel(table, zero, values, sides, out, gate):
    own, noise = stats_of(zero[ROWS : ROWS + STAT, :])
    for head in range(HEADS_HERE):
        at = slice(head * HD, (head + 1) * HD)
        value, unused, row_sum = merged(
            [
                share_of(zero, own, head, True),
                (
                    values[:, at],
                    sides[:, head : head + 1],
                    sides[:, HEADS_HERE + head : HEADS_HERE + head + 1],
                ),
            ]
        )
        out[:, at] = (value / row_sum).astype(jnp.bfloat16)
    index = lax.broadcasted_iota(jnp.int32, table.shape, 0).astype(jnp.float32)
    gate[...] = jnp.sum(jnp.where(index == noise, table[...], 0.0), axis=0, keepdims=True)


def combine(table, zero, values, sides):
    vmem = pl.BlockSpec(memory_space=pltpu.VMEM)
    return pl.pallas_call(
        combine_kernel,
        out_shape=[
            jax.ShapeDtypeStruct((ROWS, WIDTH), jnp.bfloat16),
            jax.ShapeDtypeStruct((1, table.shape[1]), jnp.float32),
        ],
        in_specs=[vmem] * 4,
        out_specs=[vmem] * 2,
        compiler_params=pltpu.CompilerParams(vmem_limit_bytes=SMALL_VMEM),
        name="combine",
    )(table, zero, values, sides)


def finish_kernel(hidden, near, arrived, gate, out):
    projected = near[...] + arrived[...].astype(jnp.float32)
    out[...] = (hidden[...].astype(jnp.float32) + gate[...] * projected).astype(jnp.bfloat16)


def finish(hidden, near, arrived, gate):
    part = hidden.shape[1]
    rows = pl.BlockSpec((ROWS // 4, part), lambda i: (i, 0))
    return pl.pallas_call(
        finish_kernel,
        grid=(4,),
        out_shape=jax.ShapeDtypeStruct(hidden.shape, jnp.bfloat16),
        in_specs=[rows, rows, rows, pl.BlockSpec((1, part), lambda i: (0, 0))],
        out_specs=rows,
        compiler_params=pltpu.CompilerParams(vmem_limit_bytes=SMALL_VMEM),
        name="finish",
    )(hidden, near, arrived, gate)


def pack_kernel(keys, values, pair):
    pair[:, :WIDTH] = keys[...]
    pair[:, WIDTH:] = values[...]


def pack(keys, values):
    vmem = pl.BlockSpec(memory_space=pltpu.VMEM)
    return pl.pallas_call(
        pack_kernel,
        out_shape=jax.ShapeDtypeStruct((ROWS, 2 * WIDTH), jnp.bfloat16),
        in_specs=[vmem] * 2,
        out_specs=vmem,
        compiler_params=pltpu.CompilerParams(vmem_limit_bytes=WHOLE_VMEM),
        name="pack",
    )(keys, values)


def copies_kernel(plan, ids, *refs):
    inputs, outs, sem = refs[: plan[0]], refs[plan[0] : -1], refs[-1]
    copies = []
    for n, (kind, source, target, number) in enumerate(plan[1]):
        src, dst = inputs[source], outs[target]
        if kind == "columns":
            width = dst.shape[1]
            src = src.at[:, pl.ds(pl.multiple_of(ids[number] * width, width), width)]
        else:
            dst = dst.at[number]
        copies.append(pltpu.make_async_copy(src, dst, sem.at[n]))
    for copy in copies:
        copy.start()
    for copy in copies:
        copy.wait()


def copied(name, ids, inputs, shapes, plan):
    anywhere = pl.BlockSpec(memory_space=pl.ANY)
    return pl.pallas_call(
        functools.partial(copies_kernel, (len(inputs), plan)),
        out_shape=[jax.ShapeDtypeStruct(shape, jnp.bfloat16) for shape in shapes],
        in_specs=[pl.BlockSpec(memory_space=pltpu.SMEM)] + [anywhere] * len(inputs),
        out_specs=[anywhere] * len(shapes),
        scratch_shapes=[pltpu.SemaphoreType.DMA((len(plan),))],
        compiler_params=pltpu.CompilerParams(vmem_limit_bytes=SMALL_VMEM),
        name=name,
    )(ids, *inputs)


def project_kernel(far, ids, *refs):
    rows, own, fetched, swapped, out, held, sem = refs[0:4], refs[4], refs[5], refs[6], refs[7], refs[8], refs[9]
    mine = ids[2] == (1 if far else 0)

    @pl.when(mine)
    def _():
        pltpu.make_async_copy(fetched, held, sem).start()

    @pl.when(jnp.logical_not(mine))
    def _():
        pltpu.make_async_copy(swapped, held, sem).start()

    pltpu.make_async_copy(fetched, held, sem).wait()
    block = out.shape[1] // 3

    def columns(n, unused):
        at = pl.ds(pl.multiple_of(n * block, block), block)
        total = jnp.dot(rows[0][...], own[:, at], preferred_element_type=jnp.float32)
        for k in range(3):
            total = total + jnp.dot(
                rows[k + 1][...], held[k, :, at], preferred_element_type=jnp.float32
            )
        out[:, at] = total.astype(out.dtype)
        return 0

    lax.fori_loop(0, 3, columns, 0)


def project(far, ids, rows, own, fetched, swapped):
    vmem = pl.BlockSpec(memory_space=pltpu.VMEM)
    anywhere = pl.BlockSpec(memory_space=pl.ANY)
    part = own.shape[1]
    return pl.pallas_call(
        functools.partial(project_kernel, far),
        out_shape=jax.ShapeDtypeStruct((ROWS, part), jnp.bfloat16 if far else jnp.float32),
        in_specs=[pl.BlockSpec(memory_space=pltpu.SMEM)] + [vmem] * 5 + [anywhere] * 2,
        out_specs=vmem,
        scratch_shapes=[pltpu.VMEM((3, WIDTH, part), jnp.bfloat16), pltpu.SemaphoreType.DMA],
        compiler_params=pltpu.CompilerParams(vmem_limit_bytes=SMALL_VMEM),
        cost_estimate=pl.CostEstimate(
            flops=8 * ROWS * WIDTH * part, bytes_accessed=5 * 10**6, transcendentals=0
        ),
        name="project",
    )(ids, *rows, own, fetched, swapped)


def around(value, axis, steps):
    count = lax.axis_size(axis)
    return lax.ppermute(value, axis, [(i, (i + steps) % count) for i in range(count)])


def together(*values):
    return lax.optimization_barrier(values)


def per_device(hidden, queries, key_rows, values, out_weight, level_table, noise_level, group_live):
    z, y, core = lax.axis_index("z"), lax.axis_index("y"), lax.axis_index("c")
    w, x = lax.axis_index("w"), lax.axis_index("x")
    slot = z * 8 + y * 2 + core
    home = lax.rem(slot + 1, 32) // 8
    block = jnp.where(core == 0, w, 1 - w) * 4
    owners = [block + lax.rem(x + step, 4) for step in (1, 2, 3)] + [w * 4 + x, (1 - w) * 4 + x]
    ids = jnp.stack([z, y, core, home, *owners]).astype(jnp.int32)
    column_block = (out_weight.shape[0], out_weight.shape[1] // 8)

    def to_level(value, d):
        return lax.ppermute(value, "z", [(i, i - d) for i in range(d, 4)])

    pair = pack(key_rows, values)
    *pieces, weight_near, weight_far = copied(
        "columns",
        ids,
        [out_weight],
        [column_block] * 5,
        tuple(("columns", 0, k, 4 + k) for k in range(5)),
    )
    next_one, next_three, below, above, pair_there, pair, queries, hidden, *pieces = together(
        to_level(queries, 1),
        to_level(queries, 3),
        around(pair, "y", 1),
        around(pair, "y", -1),
        around(pair, "c", 1),
        pair,
        queries,
        hidden,
        *pieces,
    )
    states = attend(
        "early",
        ids,
        group_live,
        noise_level,
        [next_one, next_three],
        [pair, below, above, None, pair_there],
    )
    next_two, across, piece_one, piece_three, below_there, piece_two, above, *states = together(
        to_level(queries, 2),
        around(pair, "y", 2),
        around(pieces[0], "x", 1),
        around(pieces[2], "x", 3),
        around(below, "c", 1),
        pieces[1],
        above,
        *states,
    )
    above_there, across_there = around(above, "c", 1), around(across, "c", 1)
    pairs = [pair, below, above, across, pair_there, below_there, above_there, across_there]
    piece_two = around(piece_two, "x", 2)

    def back(share, d):
        pairs_back = [
            (8 * (i - d) + j, (8 * i + j - 1) % 32) for i in range(d, 4) for j in range(8)
        ]
        return lax.ppermute(share, SLOT, pairs_back)

    one, three = attend(
        "middle", ids, group_live, noise_level, [next_one, next_three], pairs, states
    )
    back_one, back_three = back(one, 1), back(three, 3)
    live_third, one = together(group_live, one)
    (two,) = attend("third", ids, live_third, noise_level, [next_two], pairs)
    back_two = back(two, 2)
    live_late, two = together(group_live, two)
    (zero,) = attend("late", ids, live_late, noise_level, [queries], pairs)
    zero, back_one, back_three, piece_two = together(zero, back_one, back_three, piece_two)
    values_later, sides_later = combine_later(ids, back_one, back_two, back_three)
    (fetched,) = copied(
        "stack",
        ids,
        [piece_one, piece_two, piece_three],
        [(3, *column_block)],
        tuple(("stack", k, 0, k) for k in range(3)),
    )
    swapped = around(fetched, "c", 1)
    attended, gate_row = combine(level_table, back(zero, 0), values_later, sides_later)

    attended, hidden = together(attended, hidden)
    hidden_next = around(hidden, SLOT, -1)
    rows = [attended] + [around(attended, "x", step) for step in (1, 2, 3)]
    far_sum = project(True, ids, rows, weight_far, fetched, swapped)
    arrived = around(far_sum, "w", 1)
    near_sum = project(False, ids, rows, weight_near, fetched, swapped)
    return finish(hidden_next, near_sum, arrived, gate_row)


def solution(mesh):
    fine = Mesh(np.asarray(mesh.devices).reshape(4, 4, 2, 2, 4), ("z", "y", "c", "w", "x"))
    tp = ("w", "x")
    block = P(SLOT, tp)
    in_specs = (block, block, block, block, P(tp, None), P(None, tp), P(SLOT), P())
    return jax.shard_map(
        per_device, mesh=fine, in_specs=in_specs, out_specs=block, check_vma=False
    )
```

```python
import functools
import math

import jax
import jax.numpy as jnp
import numpy as np
from jax import lax
from jax.experimental import pallas as pl
from jax.experimental.pallas import tpu as pltpu
from jax.sharding import Mesh
from jax.sharding import PartitionSpec as P

HD = 128
ROWS = 448
HEADS_HERE = 3
WIDTH = HEADS_HERE * HD
STAT = 32
LOWEST = -(2.0**100)
EXP2_SCALE = HD**-0.5 * math.log2(math.e)
Y_STEPS = (0, -1, 1, 2)
SLOT = ("z", "y", "c")
ATTEND_VMEM = 30 * 1024 * 1024
SMALL_VMEM = 8 * 1024 * 1024
WHOLE_VMEM = 60 * 1024 * 1024


def score(query, key):
    return lax.dot_general(
        query, key, (((1,), (1,)), ((), ())), preferred_element_type=jnp.float32
    )


CALLS = {"early": (1, 3, 0), "third": (2,), "middle": (1, 3), "late": (0,)}
EARLY, LATER, ALL = (0, 1, 2, 4), (3, 5, 6, 7), tuple(range(8))
MEMBERS = {"early": EARLY, "third": ALL, "middle": LATER, "late": LATER}
COSTS = {"early": 10**10, "third": 10**10, "middle": 5 * 10**10, "late": 10**6}


def attend_kernel(call, ids, live, level, *refs):
    steps = CALLS[call]
    many = len(steps)
    early, resumed = call == "early", call in ("middle", "late")
    members = MEMBERS[call]
    refs = list(refs)

    def take(count):
        taken = refs[:count]
        del refs[:count]
        return taken

    query_in, pair_in = take(many), take(len(members))
    state_in = take(2) if resumed else []
    out = take(4 if early else many)
    raw, scaled, pairs, held, acc, top, done, raw_sem, pair_sem, state_sem, out_sem = refs
    here, y, core = ids[0], ids[1], ids[2]
    first = here * 8
    mine = first + y * 2 + core
    groups = {}
    for p in members:
        core_there = core if p < 4 else 1 - core
        groups[p] = first + lax.rem(y + Y_STEPS[p % 4] + 4, 4) * 2 + core_there

    def live_before(group):
        count = jnp.int32(0)
        for p in members:
            count = count + jnp.where(groups[p] < group, live[groups[p]], 0)
        return count

    bound = mine if call == "late" else first + 8
    n_live, n_before = live_before(bound), live_before(mine)
    own_place = jnp.where(live[mine] == 1, n_before, n_live)

    def active(i):
        return here + steps[i] <= 3

    def raw_copy(i):
        return pltpu.make_async_copy(query_in[i], raw.at[i], raw_sem.at[i])

    def place_copy(j, place):
        at = pl.ds(pl.multiple_of(place * ROWS, 64), ROWS)
        return pltpu.make_async_copy(pair_in[j], pairs.at[at], pair_sem.at[place])

    def state_copies():
        return (
            pltpu.make_async_copy(state_in[0], acc, state_sem.at[0]),
            pltpu.make_async_copy(state_in[1], top, state_sem.at[1]),
        )

    def out_copies(part):
        at = pl.ds(0, 2 * ROWS) if part == 0 else pl.ds(2 * ROWS, ROWS)
        return (
            pltpu.make_async_copy(acc.at[:, at], out[2 * part], out_sem.at[2 * part]),
            pltpu.make_async_copy(top.at[:, at], out[2 * part + 1], out_sem.at[2 * part + 1]),
        )

    def share_copy(i):
        return pltpu.make_async_copy(done.at[i], out[i], out_sem.at[i])

    def prepare(i):
        raw_copy(i).wait()
        at = slice(i * ROWS, (i + 1) * ROWS)
        for head in range(HEADS_HERE):
            exact = raw[i, :, head * HD : (head + 1) * HD].astype(jnp.float32) * EXP2_SCALE
            high = exact.astype(jnp.bfloat16)
            scaled[head, at, :HD] = high
            scaled[head, at, HD:] = (exact - high.astype(jnp.float32)).astype(jnp.bfloat16)

    def sweep(start, rows, count, place_of, waits):
        span = slice(start, start + rows)
        chunks = (count + 1) // 2

        def arrive(t):
            if waits:
                for k in (2 * t, 2 * t + 1):

                    @pl.when(k < count)
                    def _():
                        place_copy(0, k).wait()

        def at(k):
            place = place_of(jnp.maximum(jnp.minimum(k, count - 1), 0))
            return pl.ds(pl.multiple_of(place * ROWS, 64), ROWS)

        def columns(base, head):
            if isinstance(head, int):
                return slice(base + head * HD, base + (head + 1) * HD)
            return pl.ds(pl.multiple_of(base + head * HD, HD), HD)

        def scores_of(t, head):
            cols = columns(0, head)
            key = jnp.concatenate([pairs[at(2 * t), cols], pairs[at(2 * t + 1), cols]], axis=0)
            return score(scaled[head, span], jnp.concatenate([key, key], axis=1))

        def absorb(t, head, scores):
            old = top[head, span]
            new = jnp.maximum(old, jnp.max(scores, axis=1, keepdims=True))
            weights = jnp.exp2(scores - jnp.concatenate([new] * (2 * ROWS // HD), axis=1))
            cols = columns(WIDTH, head)
            there = jnp.where(2 * t + 1 < count, 1.0, 0.0).astype(jnp.bfloat16)
            ones = jnp.ones((ROWS, HD), jnp.bfloat16)
            value = jnp.concatenate(
                [
                    jnp.concatenate([pairs[at(2 * t), cols], ones], axis=1),
                    jnp.concatenate([pairs[at(2 * t + 1), cols], ones], axis=1) * there,
                ],
                axis=0,
            )
            weighted = jnp.dot(
                weights.astype(jnp.bfloat16), value, preferred_element_type=jnp.float32
            )
            shrink = jnp.exp2(old - new)
            acc[head, span] = (
                acc[head, span] * jnp.concatenate([shrink, shrink], axis=1) + weighted
            )
            top[head, span] = new

        arrive(0)

        @pl.when(chunks > 0)
        def _():
            held[0:rows] = scores_of(0, 0)

        if rows > ROWS:

            def unit(u, unused):
                head, t = lax.rem(u, HEADS_HERE), u // HEADS_HERE
                scores = held[0:rows]

                @pl.when(head == 1)
                def _():
                    arrive(t + 1)

                following = jnp.minimum(u + 1, HEADS_HERE * chunks - 1)
                upcoming = scores_of(following // HEADS_HERE, lax.rem(following, HEADS_HERE))
                absorb(t, head, scores)
                held[0:rows] = upcoming
                return 0

            lax.fori_loop(0, HEADS_HERE * chunks, unit, 0)
            return

        def chunk(t, unused):
            scores = held[0:rows]
            following = scores_of(t, 1)
            absorb(t, 0, scores)
            scores = scores_of(t, 2)
            absorb(t, 1, following)
            arrive(t + 1)
            held[0:rows] = scores_of(t + 1, 0)
            absorb(t, 2, scores)
            return 0

        lax.fori_loop(0, chunks, chunk, 0)

    def finish(i, unused):
        span = pl.ds(pl.multiple_of(i * ROWS, 64), ROWS)
        lane = lax.broadcasted_iota(jnp.int32, (ROWS, HD), 1)
        stats = jnp.where(lane == 3 * HEADS_HERE, level[0].astype(jnp.float32), 0.0)
        for head in range(HEADS_HERE):
            exact = top[head, span]
            sent = exact.astype(jnp.bfloat16).astype(jnp.float32)
            factor = jnp.exp2(exact - sent)
            weighted = acc[head, span]
            done[i, 0:ROWS, head * HD : (head + 1) * HD] = (weighted[:, :HD] * factor).astype(
                jnp.bfloat16
            )
            total = weighted[:, HD:] * factor
            high = total.astype(jnp.bfloat16).astype(jnp.float32)
            stats = jnp.where(lane == head, sent, stats)
            stats = jnp.where(lane == HEADS_HERE + head, high, stats)
            stats = jnp.where(lane == 2 * HEADS_HERE + head, total - high, stats)
        flat = jnp.transpose(stats)[:16].astype(jnp.bfloat16)
        done[i, ROWS : ROWS + 16, :] = flat[:, :WIDTH]
        pad = jnp.zeros((16, 2 * WIDTH - ROWS), jnp.bfloat16)
        done[i, ROWS + 16 : ROWS + 32, :] = jnp.concatenate([flat[:, WIDTH:], pad], axis=1)
        for k in range(many):

            @pl.when(i == k)
            def _():
                share_copy(k).start()

        return 0

    def run():
        if resumed:
            for copy in state_copies():
                copy.start()
        for j, p in enumerate(members):
            if early and p == 0:
                place_copy(j, own_place).start()
                continue

            @pl.when((live[groups[p]] == 1) & (groups[p] < bound))
            def _():
                place_copy(j, live_before(groups[p])).start()

        for i in range(many):
            raw_copy(i).start()
        if early:
            place_copy(0, own_place).wait()
            for k in range(len(EARLY)):

                @pl.when((k < n_live) & (k != own_place))
                def _():
                    place_copy(0, k).wait()

        for i in range(many):
            prepare(i)
        if resumed:
            for copy in state_copies():
                copy.wait()
        else:
            top[...] = jnp.full(top.shape, LOWEST, jnp.float32)
            acc[...] = jnp.zeros(acc.shape, jnp.float32)
        if early:

            @pl.when(active(0))
            def _():
                sweep(0, 2 * ROWS, n_live, lambda k: k, False)
                for copy in out_copies(0):
                    copy.start()

            sweep(
                2 * ROWS,
                ROWS,
                n_before + 1,
                lambda k: jnp.where(k < n_before, k, own_place),
                False,
            )
            for copy in out_copies(1):
                copy.start()
            for copy in out_copies(1):
                copy.wait()

            @pl.when(active(0))
            def _():
                for copy in out_copies(0):
                    copy.wait()

            return

        sweep(0, many * ROWS, n_live, lambda k: k, True)
        lax.fori_loop(0, many, finish, 0)
        for i in range(many):
            share_copy(i).wait()

    if early:
        run()
    else:
        pl.when(active(0))(run)


def attend(call, ids, live, level, queries, pairs, states=()):
    smem = pl.BlockSpec(memory_space=pltpu.SMEM)
    anywhere = pl.BlockSpec(memory_space=pl.ANY)
    bf16, f32 = jnp.bfloat16, jnp.float32
    many = len(CALLS[call])
    members = MEMBERS[call]
    together_rows = 2 * ROWS if call in ("early", "middle") else ROWS

    def state(rows):
        return [(HEADS_HERE, rows, 2 * HD), (HEADS_HERE, rows, HD)]

    if call == "early":
        out_shape = [jax.ShapeDtypeStruct(shape, f32) for shape in state(2 * ROWS) + state(ROWS)]
    else:
        out_shape = [jax.ShapeDtypeStruct((ROWS + STAT, WIDTH), bf16)] * many
    operands = [*queries, *[pairs[p] for p in members], *states]
    rows = many * ROWS
    return pl.pallas_call(
        functools.partial(attend_kernel, call),
        out_shape=out_shape,
        in_specs=[smem] * 3 + [anywhere] * len(operands),
        out_specs=[anywhere] * len(out_shape),
        scratch_shapes=[
            pltpu.VMEM((many, ROWS, WIDTH), bf16),
            pltpu.VMEM((HEADS_HERE, rows, 2 * HD), bf16),
            pltpu.VMEM((8 * ROWS, 2 * WIDTH), bf16),
            pltpu.VMEM((together_rows, 2 * ROWS), f32),
            pltpu.VMEM(state(rows)[0], f32),
            pltpu.VMEM(state(rows)[1], f32),
            pltpu.VMEM((many, ROWS + STAT, WIDTH), bf16),
            pltpu.SemaphoreType.DMA((many,)),
            pltpu.SemaphoreType.DMA((8,)),
            pltpu.SemaphoreType.DMA((2,)),
            pltpu.SemaphoreType.DMA((4,)),
        ],
        compiler_params=pltpu.CompilerParams(vmem_limit_bytes=ATTEND_VMEM),
        cost_estimate=pl.CostEstimate(
            flops=COSTS[call], bytes_accessed=10**6, transcendentals=0
        ),
        name="attend_" + call,
    )(ids, live, level, *operands)


def stats_of(tail):
    tail = tail.astype(jnp.float32)
    flat = jnp.concatenate([tail[0:16], tail[16:32, : ROWS - WIDTH]], axis=1)
    noise = flat[3 * HEADS_HERE : 3 * HEADS_HERE + 1, 0:1]
    padded = jnp.concatenate([flat, jnp.zeros((HD - 16, ROWS), jnp.float32)])
    return jnp.transpose(padded), noise


def merged(parts):
    highest = parts[0][1]
    for part in parts[1:]:
        highest = jnp.maximum(highest, part[1])
    values = total = None
    for value, row_max, row_sum in parts:
        factor = jnp.exp2(row_max - highest)
        values = value * factor if values is None else values + value * factor
        total = row_sum * factor if total is None else total + row_sum * factor
    return values, highest, total


def share_of(ref, stats, head, present):
    value = ref[0:ROWS, head * HD : (head + 1) * HD].astype(jnp.float32)
    row_max = stats[:, head : head + 1]
    row_sum = (
        stats[:, HEADS_HERE + head : HEADS_HERE + head + 1]
        + stats[:, 2 * HEADS_HERE + head : 2 * HEADS_HERE + head + 1]
    )
    return (
        jnp.where(present, value, 0.0),
        jnp.where(present, row_max, LOWEST),
        jnp.where(present, row_sum, 0.0),
    )


def combine_later_kernel(ids, one, two, three, values, sides):
    home = ids[3]
    stats = [stats_of(ref[ROWS : ROWS + STAT, :])[0] for ref in (one, two, three)]
    lane = lax.broadcasted_iota(jnp.int32, (ROWS, HD), 1)
    side = jnp.zeros((ROWS, HD), jnp.float32)
    for head in range(HEADS_HERE):
        value, row_max, row_sum = merged(
            [
                share_of(one, stats[0], head, home >= 1),
                share_of(two, stats[1], head, home >= 2),
                share_of(three, stats[2], head, home >= 3),
            ]
        )
        values[:, head * HD : (head + 1) * HD] = value
        side = jnp.where(lane == head, row_max, side)
        side = jnp.where(lane == HEADS_HERE + head, row_sum, side)
    sides[...] = side


def combine_later(ids, one, two, three):
    vmem = pl.BlockSpec(memory_space=pltpu.VMEM)
    return pl.pallas_call(
        combine_later_kernel,
        out_shape=[
            jax.ShapeDtypeStruct((ROWS, WIDTH), jnp.float32),
            jax.ShapeDtypeStruct((ROWS, HD), jnp.float32),
        ],
        in_specs=[pl.BlockSpec(memory_space=pltpu.SMEM)] + [vmem] * 3,
        out_specs=[vmem] * 2,
        compiler_params=pltpu.CompilerParams(vmem_limit_bytes=SMALL_VMEM),
        cost_estimate=pl.CostEstimate(
            flops=10**11, bytes_accessed=2 * 10**8, transcendentals=0
        ),
        name="combine_later",
    )(ids, one, two, three)


def combine_kernel(table, zero, values, sides, out, gate):
    own, noise = stats_of(zero[ROWS : ROWS + STAT, :])
    for head in range(HEADS_HERE):
        at = slice(head * HD, (head + 1) * HD)
        value, unused, row_sum = merged(
            [
                share_of(zero, own, head, True),
                (
                    values[:, at],
                    sides[:, head : head + 1],
                    sides[:, HEADS_HERE + head : HEADS_HERE + head + 1],
                ),
            ]
        )
        out[:, at] = (value / row_sum).astype(jnp.bfloat16)
    index = lax.broadcasted_iota(jnp.int32, table.shape, 0).astype(jnp.float32)
    gate[...] = jnp.sum(jnp.where(index == noise, table[...], 0.0), axis=0, keepdims=True)


def combine(table, zero, values, sides):
    vmem = pl.BlockSpec(memory_space=pltpu.VMEM)
    return pl.pallas_call(
        combine_kernel,
        out_shape=[
            jax.ShapeDtypeStruct((ROWS, WIDTH), jnp.bfloat16),
            jax.ShapeDtypeStruct((1, table.shape[1]), jnp.float32),
        ],
        in_specs=[vmem] * 4,
        out_specs=[vmem] * 2,
        compiler_params=pltpu.CompilerParams(vmem_limit_bytes=SMALL_VMEM),
        name="combine",
    )(table, zero, values, sides)


def finish_kernel(hidden, near, arrived, gate, out):
    projected = near[...] + arrived[...].astype(jnp.float32)
    out[...] = (hidden[...].astype(jnp.float32) + gate[...] * projected).astype(jnp.bfloat16)


def finish(hidden, near, arrived, gate):
    part = hidden.shape[1]
    rows = pl.BlockSpec((ROWS // 4, part), lambda i: (i, 0))
    return pl.pallas_call(
        finish_kernel,
        grid=(4,),
        out_shape=jax.ShapeDtypeStruct(hidden.shape, jnp.bfloat16),
        in_specs=[rows, rows, rows, pl.BlockSpec((1, part), lambda i: (0, 0))],
        out_specs=rows,
        compiler_params=pltpu.CompilerParams(vmem_limit_bytes=SMALL_VMEM),
        name="finish",
    )(hidden, near, arrived, gate)


def pack_kernel(keys, values, pair):
    pair[:, :WIDTH] = keys[...]
    pair[:, WIDTH:] = values[...]


def pack(keys, values):
    vmem = pl.BlockSpec(memory_space=pltpu.VMEM)
    return pl.pallas_call(
        pack_kernel,
        out_shape=jax.ShapeDtypeStruct((ROWS, 2 * WIDTH), jnp.bfloat16),
        in_specs=[vmem] * 2,
        out_specs=vmem,
        compiler_params=pltpu.CompilerParams(vmem_limit_bytes=WHOLE_VMEM),
        name="pack",
    )(keys, values)


def copies_kernel(plan, ids, *refs):
    inputs, outs, sem = refs[: plan[0]], refs[plan[0] : -1], refs[-1]
    copies = []
    for n, (kind, source, target, number) in enumerate(plan[1]):
        src, dst = inputs[source], outs[target]
        if kind == "columns":
            width = dst.shape[1]
            src = src.at[:, pl.ds(pl.multiple_of(ids[number] * width, width), width)]
        else:
            dst = dst.at[number]
        copies.append(pltpu.make_async_copy(src, dst, sem.at[n]))
    for copy in copies:
        copy.start()
    for copy in copies:
        copy.wait()


def copied(name, ids, inputs, shapes, plan):
    anywhere = pl.BlockSpec(memory_space=pl.ANY)
    return pl.pallas_call(
        functools.partial(copies_kernel, (len(inputs), plan)),
        out_shape=[jax.ShapeDtypeStruct(shape, jnp.bfloat16) for shape in shapes],
        in_specs=[pl.BlockSpec(memory_space=pltpu.SMEM)] + [anywhere] * len(inputs),
        out_specs=[anywhere] * len(shapes),
        scratch_shapes=[pltpu.SemaphoreType.DMA((len(plan),))],
        compiler_params=pltpu.CompilerParams(vmem_limit_bytes=SMALL_VMEM),
        name=name,
    )(ids, *inputs)


def project_kernel(far, ids, *refs):
    rows, own, fetched, swapped, out, held, sem = refs[0:4], refs[4], refs[5], refs[6], refs[7], refs[8], refs[9]
    mine = ids[2] == (1 if far else 0)

    @pl.when(mine)
    def _():
        pltpu.make_async_copy(fetched, held, sem).start()

    @pl.when(jnp.logical_not(mine))
    def _():
        pltpu.make_async_copy(swapped, held, sem).start()

    pltpu.make_async_copy(fetched, held, sem).wait()
    block = out.shape[1] // 3

    def columns(n, unused):
        at = pl.ds(pl.multiple_of(n * block, block), block)
        total = jnp.dot(rows[0][...], own[:, at], preferred_element_type=jnp.float32)
        for k in range(3):
            total = total + jnp.dot(
                rows[k + 1][...], held[k, :, at], preferred_element_type=jnp.float32
            )
        out[:, at] = total.astype(out.dtype)
        return 0

    lax.fori_loop(0, 3, columns, 0)


def project(far, ids, rows, own, fetched, swapped):
    vmem = pl.BlockSpec(memory_space=pltpu.VMEM)
    anywhere = pl.BlockSpec(memory_space=pl.ANY)
    part = own.shape[1]
    return pl.pallas_call(
        functools.partial(project_kernel, far),
        out_shape=jax.ShapeDtypeStruct((ROWS, part), jnp.bfloat16 if far else jnp.float32),
        in_specs=[pl.BlockSpec(memory_space=pltpu.SMEM)] + [vmem] * 5 + [anywhere] * 2,
        out_specs=vmem,
        scratch_shapes=[pltpu.VMEM((3, WIDTH, part), jnp.bfloat16), pltpu.SemaphoreType.DMA],
        compiler_params=pltpu.CompilerParams(vmem_limit_bytes=SMALL_VMEM),
        cost_estimate=pl.CostEstimate(
            flops=8 * ROWS * WIDTH * part, bytes_accessed=5 * 10**6, transcendentals=0
        ),
        name="project",
    )(ids, *rows, own, fetched, swapped)


def around(value, axis, steps):
    count = lax.axis_size(axis)
    return lax.ppermute(value, axis, [(i, (i + steps) % count) for i in range(count)])


def together(*values):
    return lax.optimization_barrier(values)


def per_device(hidden, queries, key_rows, values, out_weight, level_table, noise_level, group_live):
    z, y, core = lax.axis_index("z"), lax.axis_index("y"), lax.axis_index("c")
    w, x = lax.axis_index("w"), lax.axis_index("x")
    slot = z * 8 + y * 2 + core
    home = lax.rem(slot + 1, 32) // 8
    block = jnp.where(core == 0, w, 1 - w) * 4
    owners = [block + lax.rem(x + step, 4) for step in (1, 2, 3)] + [w * 4 + x, (1 - w) * 4 + x]
    ids = jnp.stack([z, y, core, home, *owners]).astype(jnp.int32)
    column_block = (out_weight.shape[0], out_weight.shape[1] // 8)

    def to_level(value, d):
        return lax.ppermute(value, "z", [(i, i - d) for i in range(d, 4)])

    pair = pack(key_rows, values)
    *pieces, weight_near, weight_far = copied(
        "columns",
        ids,
        [out_weight],
        [column_block] * 5,
        tuple(("columns", 0, k, 4 + k) for k in range(5)),
    )
    next_one, next_three, below, above, pair_there, pair, queries, hidden, *pieces = together(
        to_level(queries, 1),
        to_level(queries, 3),
        around(pair, "y", 1),
        around(pair, "y", -1),
        around(pair, "c", 1),
        pair,
        queries,
        hidden,
        *pieces,
    )
    states = attend(
        "early",
        ids,
        group_live,
        noise_level,
        [next_one, next_three, queries],
        [pair, below, above, None, pair_there],
    )
    next_two, across, piece_one, piece_three, below_there, piece_two, above, *states = together(
        to_level(queries, 2),
        around(pair, "y", 2),
        around(pieces[0], "x", 1),
        around(pieces[2], "x", 3),
        around(below, "c", 1),
        pieces[1],
        above,
        *states,
    )
    above_there, across_there = around(above, "c", 1), around(across, "c", 1)
    pairs = [pair, below, above, across, pair_there, below_there, above_there, across_there]
    piece_two = around(piece_two, "x", 2)

    def back(share, d):
        pairs_back = [
            (8 * (i - d) + j, (8 * i + j - 1) % 32) for i in range(d, 4) for j in range(8)
        ]
        return lax.ppermute(share, SLOT, pairs_back)

    (two,) = attend("third", ids, group_live, noise_level, [next_two], pairs)
    back_two = back(two, 2)
    live_middle, two = together(group_live, two)
    one, three = attend(
        "middle", ids, live_middle, noise_level, [next_one, next_three], pairs, states[0:2]
    )
    back_one, back_three = back(one, 1), back(three, 3)
    live_late, one = together(group_live, one)
    (zero,) = attend("late", ids, live_late, noise_level, [queries], pairs, states[2:4])
    zero, back_two, piece_two = together(zero, back_two, piece_two)
    (fetched,) = copied(
        "stack",
        ids,
        [piece_one, piece_two, piece_three],
        [(3, *column_block)],
        tuple(("stack", k, 0, k) for k in range(3)),
    )
    swapped = around(fetched, "c", 1)
    values_later, sides_later = combine_later(ids, back_one, back_two, back_three)
    attended, gate_row = combine(level_table, back(zero, 0), values_later, sides_later)

    attended, hidden = together(attended, hidden)
    hidden_next = around(hidden, SLOT, -1)
    rows = [attended] + [around(attended, "x", step) for step in (1, 2, 3)]
    far_sum = project(True, ids, rows, weight_far, fetched, swapped)
    arrived = around(far_sum, "w", 1)
    near_sum = project(False, ids, rows, weight_near, fetched, swapped)
    return finish(hidden_next, near_sum, arrived, gate_row)


def solution(mesh):
    fine = Mesh(np.asarray(mesh.devices).reshape(4, 4, 2, 2, 4), ("z", "y", "c", "w", "x"))
    tp = ("w", "x")
    block = P(SLOT, tp)
    in_specs = (block, block, block, block, P(tp, None), P(None, tp), P(SLOT), P())
    return jax.shard_map(
        per_device, mesh=fine, in_specs=in_specs, out_specs=block, check_vma=False
    )
```

```python
import functools
import math

import jax
import jax.numpy as jnp
import numpy as np
from jax import lax
from jax.experimental import pallas as pl
from jax.experimental.pallas import tpu as pltpu
from jax.sharding import Mesh
from jax.sharding import PartitionSpec as P

HD = 128
ROWS = 448
HEADS_HERE = 3
WIDTH = HEADS_HERE * HD
STAT = 32
LOWEST = -(2.0**100)
EXP2_SCALE = HD**-0.5 * math.log2(math.e)
Y_STEPS = (0, -1, 1, 2)
SLOT = ("z", "y", "c")
ATTEND_VMEM = 30 * 1024 * 1024
SMALL_VMEM = 8 * 1024 * 1024
WHOLE_VMEM = 60 * 1024 * 1024


def score(query, key):
    return lax.dot_general(
        query, key, (((1,), (1,)), ((), ())), preferred_element_type=jnp.float32
    )


CALLS = {"early": (1, 3, 0), "third": (2,), "middle": (1, 3), "late": (0,)}
EARLY, LATER, ALL = (0, 1, 2, 4), (3, 5, 6, 7), tuple(range(8))
MEMBERS = {"early": EARLY, "third": ALL, "middle": LATER, "late": LATER}
COSTS = {"early": 10**10, "third": 10**10, "middle": 5 * 10**10, "late": 10**6}


def attend_kernel(call, ids, live, level, *refs):
    steps = CALLS[call]
    many = len(steps)
    early, resumed = call == "early", call in ("middle", "late")
    members = MEMBERS[call]
    refs = list(refs)

    def take(count):
        taken = refs[:count]
        del refs[:count]
        return taken

    query_in, pair_in = take(many), take(len(members))
    state_in = take(2) if resumed else []
    out = take(4 if early else many)
    raw, scaled, pairs, held, acc, top, done, raw_sem, pair_sem, state_sem, out_sem = refs
    here, y, core = ids[0], ids[1], ids[2]
    first = here * 8
    mine = first + y * 2 + core
    groups = {}
    for p in members:
        core_there = core if p < 4 else 1 - core
        groups[p] = first + lax.rem(y + Y_STEPS[p % 4] + 4, 4) * 2 + core_there

    def live_before(group):
        count = jnp.int32(0)
        for p in members:
            count = count + jnp.where(groups[p] < group, live[groups[p]], 0)
        return count

    bound = mine if call == "late" else first + 8
    n_live, n_before = live_before(bound), live_before(mine)
    own_place = jnp.where(live[mine] == 1, n_before, n_live)

    def active(i):
        return here + steps[i] <= 3

    def raw_copy(i):
        return pltpu.make_async_copy(query_in[i], raw.at[i], raw_sem.at[i])

    def place_copy(j, place):
        at = pl.ds(pl.multiple_of(place * ROWS, 64), ROWS)
        return pltpu.make_async_copy(pair_in[j], pairs.at[at], pair_sem.at[place])

    def state_copies():
        return (
            pltpu.make_async_copy(state_in[0], acc, state_sem.at[0]),
            pltpu.make_async_copy(state_in[1], top, state_sem.at[1]),
        )

    def out_copies(part):
        at = pl.ds(0, 2 * ROWS) if part == 0 else pl.ds(2 * ROWS, ROWS)
        return (
            pltpu.make_async_copy(acc.at[:, at], out[2 * part], out_sem.at[2 * part]),
            pltpu.make_async_copy(top.at[:, at], out[2 * part + 1], out_sem.at[2 * part + 1]),
        )

    def share_copy(i):
        return pltpu.make_async_copy(done.at[i], out[i], out_sem.at[i])

    def prepare(i):
        raw_copy(i).wait()
        at = slice(i * ROWS, (i + 1) * ROWS)
        for head in range(HEADS_HERE):
            exact = raw[i, :, head * HD : (head + 1) * HD].astype(jnp.float32) * EXP2_SCALE
            high = exact.astype(jnp.bfloat16)
            scaled[head, at, :HD] = high
            scaled[head, at, HD:] = (exact - high.astype(jnp.float32)).astype(jnp.bfloat16)

    def sweep(start, rows, count, place_of, waits, loop_heads):
        span = slice(start, start + rows)
        chunks = (count + 1) // 2

        def arrive(t):
            if waits:
                for k in (2 * t, 2 * t + 1):

                    @pl.when(k < count)
                    def _():
                        place_copy(0, k).wait()

        def at(k):
            place = place_of(jnp.maximum(jnp.minimum(k, count - 1), 0))
            return pl.ds(pl.multiple_of(place * ROWS, 64), ROWS)

        def columns(base, head):
            if isinstance(head, int):
                return slice(base + head * HD, base + (head + 1) * HD)
            return pl.ds(pl.multiple_of(base + head * HD, HD), HD)

        def scores_of(t, head):
            cols = columns(0, head)
            key = jnp.concatenate([pairs[at(2 * t), cols], pairs[at(2 * t + 1), cols]], axis=0)
            return score(scaled[head, span], jnp.concatenate([key, key], axis=1))

        def absorb(t, head, scores):
            old = top[head, span]
            new = jnp.maximum(old, jnp.max(scores, axis=1, keepdims=True))
            weights = jnp.exp2(scores - jnp.concatenate([new] * (2 * ROWS // HD), axis=1))
            cols = columns(WIDTH, head)
            there = jnp.where(2 * t + 1 < count, 1.0, 0.0).astype(jnp.bfloat16)
            ones = jnp.ones((ROWS, HD), jnp.bfloat16)
            value = jnp.concatenate(
                [
                    jnp.concatenate([pairs[at(2 * t), cols], ones], axis=1),
                    jnp.concatenate([pairs[at(2 * t + 1), cols], ones], axis=1) * there,
                ],
                axis=0,
            )
            weighted = jnp.dot(
                weights.astype(jnp.bfloat16), value, preferred_element_type=jnp.float32
            )
            shrink = jnp.exp2(old - new)
            acc[head, span] = (
                acc[head, span] * jnp.concatenate([shrink, shrink], axis=1) + weighted
            )
            top[head, span] = new

        arrive(0)

        @pl.when(chunks > 0)
        def _():
            held[0:rows] = scores_of(0, 0)

        if loop_heads:

            def unit(u, unused):
                head, t = lax.rem(u, HEADS_HERE), u // HEADS_HERE
                scores = held[0:rows]

                @pl.when(head == 1)
                def _():
                    arrive(t + 1)

                following = jnp.minimum(u + 1, HEADS_HERE * chunks - 1)
                upcoming = scores_of(following // HEADS_HERE, lax.rem(following, HEADS_HERE))
                absorb(t, head, scores)
                held[0:rows] = upcoming
                return 0

            lax.fori_loop(0, HEADS_HERE * chunks, unit, 0)
            return

        def chunk(t, unused):
            scores = held[0:rows]
            following = scores_of(t, 1)
            absorb(t, 0, scores)
            scores = scores_of(t, 2)
            absorb(t, 1, following)
            arrive(t + 1)
            held[0:rows] = scores_of(t + 1, 0)
            absorb(t, 2, scores)
            return 0

        lax.fori_loop(0, chunks, chunk, 0)

    def finish(i, unused):
        span = pl.ds(pl.multiple_of(i * ROWS, 64), ROWS)
        lane = lax.broadcasted_iota(jnp.int32, (ROWS, HD), 1)
        stats = jnp.where(lane == 3 * HEADS_HERE, level[0].astype(jnp.float32), 0.0)
        for head in range(HEADS_HERE):
            exact = top[head, span]
            sent = exact.astype(jnp.bfloat16).astype(jnp.float32)
            factor = jnp.exp2(exact - sent)
            weighted = acc[head, span]
            done[i, 0:ROWS, head * HD : (head + 1) * HD] = (weighted[:, :HD] * factor).astype(
                jnp.bfloat16
            )
            total = weighted[:, HD:] * factor
            high = total.astype(jnp.bfloat16).astype(jnp.float32)
            stats = jnp.where(lane == head, sent, stats)
            stats = jnp.where(lane == HEADS_HERE + head, high, stats)
            stats = jnp.where(lane == 2 * HEADS_HERE + head, total - high, stats)
        flat = jnp.transpose(stats)[:16].astype(jnp.bfloat16)
        done[i, ROWS : ROWS + 16, :] = flat[:, :WIDTH]
        pad = jnp.zeros((16, 2 * WIDTH - ROWS), jnp.bfloat16)
        done[i, ROWS + 16 : ROWS + 32, :] = jnp.concatenate([flat[:, WIDTH:], pad], axis=1)
        for k in range(many):

            @pl.when(i == k)
            def _():
                share_copy(k).start()

        return 0

    def first_sources(waits):
        @pl.when(active(1))
        def _():
            sweep(0, 2 * ROWS, n_live, lambda k: k, waits, True)

        @pl.when(active(0) & jnp.logical_not(active(1)))
        def _():
            sweep(0, ROWS, n_live, lambda k: k, waits, True)

    def run():
        if resumed:
            for copy in state_copies():
                copy.start()
        for j, p in enumerate(members):
            if early and p == 0:
                place_copy(j, own_place).start()
                continue

            @pl.when((live[groups[p]] == 1) & (groups[p] < bound))
            def _():
                place_copy(j, live_before(groups[p])).start()

        for i in range(many):
            pl.when(active(i))(raw_copy(i).start)
        if early:
            place_copy(0, own_place).wait()
            for k in range(len(EARLY)):

                @pl.when((k < n_live) & (k != own_place))
                def _():
                    place_copy(0, k).wait()

        for i in range(many):
            pl.when(active(i))(functools.partial(prepare, i))
        if resumed:
            for copy in state_copies():
                copy.wait()
        else:
            top[...] = jnp.full(top.shape, LOWEST, jnp.float32)
            acc[...] = jnp.zeros(acc.shape, jnp.float32)
        if early:

            first_sources(False)

            @pl.when(active(0))
            def _():
                for copy in out_copies(0):
                    copy.start()

            sweep(
                2 * ROWS,
                ROWS,
                n_before + 1,
                lambda k: jnp.where(k < n_before, k, own_place),
                False,
                False,
            )
            for copy in out_copies(1):
                copy.start()
            for copy in out_copies(1):
                copy.wait()

            @pl.when(active(0))
            def _():
                for copy in out_copies(0):
                    copy.wait()

            return

        if many == 2:
            first_sources(True)
        else:
            sweep(0, ROWS, n_live, lambda k: k, True, False)
        lax.fori_loop(0, jnp.where(active(many - 1), many, 1), finish, 0)
        for i in range(many):
            pl.when(active(i))(share_copy(i).wait)

    if early:
        run()
    else:
        pl.when(active(0))(run)


def attend(call, ids, live, level, queries, pairs, states=()):
    smem = pl.BlockSpec(memory_space=pltpu.SMEM)
    anywhere = pl.BlockSpec(memory_space=pl.ANY)
    bf16, f32 = jnp.bfloat16, jnp.float32
    many = len(CALLS[call])
    members = MEMBERS[call]
    together_rows = 2 * ROWS if call in ("early", "middle") else ROWS

    def state(rows):
        return [(HEADS_HERE, rows, 2 * HD), (HEADS_HERE, rows, HD)]

    if call == "early":
        out_shape = [jax.ShapeDtypeStruct(shape, f32) for shape in state(2 * ROWS) + state(ROWS)]
    else:
        out_shape = [jax.ShapeDtypeStruct((ROWS + STAT, WIDTH), bf16)] * many
    operands = [*queries, *[pairs[p] for p in members], *states]
    rows = many * ROWS
    return pl.pallas_call(
        functools.partial(attend_kernel, call),
        out_shape=out_shape,
        in_specs=[smem] * 3 + [anywhere] * len(operands),
        out_specs=[anywhere] * len(out_shape),
        scratch_shapes=[
            pltpu.VMEM((many, ROWS, WIDTH), bf16),
            pltpu.VMEM((HEADS_HERE, rows, 2 * HD), bf16),
            pltpu.VMEM((8 * ROWS, 2 * WIDTH), bf16),
            pltpu.VMEM((together_rows, 2 * ROWS), f32),
            pltpu.VMEM(state(rows)[0], f32),
            pltpu.VMEM(state(rows)[1], f32),
            pltpu.VMEM((many, ROWS + STAT, WIDTH), bf16),
            pltpu.SemaphoreType.DMA((many,)),
            pltpu.SemaphoreType.DMA((8,)),
            pltpu.SemaphoreType.DMA((2,)),
            pltpu.SemaphoreType.DMA((4,)),
        ],
        compiler_params=pltpu.CompilerParams(vmem_limit_bytes=ATTEND_VMEM),
        cost_estimate=pl.CostEstimate(
            flops=COSTS[call], bytes_accessed=10**6, transcendentals=0
        ),
        name="attend_" + call,
    )(ids, live, level, *operands)


def stats_of(tail):
    tail = tail.astype(jnp.float32)
    flat = jnp.concatenate([tail[0:16], tail[16:32, : ROWS - WIDTH]], axis=1)
    noise = flat[3 * HEADS_HERE : 3 * HEADS_HERE + 1, 0:1]
    padded = jnp.concatenate([flat, jnp.zeros((HD - 16, ROWS), jnp.float32)])
    return jnp.transpose(padded), noise


def merged(parts):
    highest = parts[0][1]
    for part in parts[1:]:
        highest = jnp.maximum(highest, part[1])
    values = total = None
    for value, row_max, row_sum in parts:
        factor = jnp.exp2(row_max - highest)
        values = value * factor if values is None else values + value * factor
        total = row_sum * factor if total is None else total + row_sum * factor
    return values, highest, total


def share_of(ref, stats, head, present):
    value = ref[0:ROWS, head * HD : (head + 1) * HD].astype(jnp.float32)
    row_max = stats[:, head : head + 1]
    row_sum = (
        stats[:, HEADS_HERE + head : HEADS_HERE + head + 1]
        + stats[:, 2 * HEADS_HERE + head : 2 * HEADS_HERE + head + 1]
    )
    return (
        jnp.where(present, value, 0.0),
        jnp.where(present, row_max, LOWEST),
        jnp.where(present, row_sum, 0.0),
    )


def combine_later_kernel(ids, one, two, three, values, sides):
    home = ids[3]
    stats = [stats_of(ref[ROWS : ROWS + STAT, :])[0] for ref in (one, two, three)]
    lane = lax.broadcasted_iota(jnp.int32, (ROWS, HD), 1)
    side = jnp.zeros((ROWS, HD), jnp.float32)
    for head in range(HEADS_HERE):
        value, row_max, row_sum = merged(
            [
                share_of(one, stats[0], head, home >= 1),
                share_of(two, stats[1], head, home >= 2),
                share_of(three, stats[2], head, home >= 3),
            ]
        )
        values[:, head * HD : (head + 1) * HD] = value
        side = jnp.where(lane == head, row_max, side)
        side = jnp.where(lane == HEADS_HERE + head, row_sum, side)
    sides[...] = side


def combine_later(ids, one, two, three):
    vmem = pl.BlockSpec(memory_space=pltpu.VMEM)
    return pl.pallas_call(
        combine_later_kernel,
        out_shape=[
            jax.ShapeDtypeStruct((ROWS, WIDTH), jnp.float32),
            jax.ShapeDtypeStruct((ROWS, HD), jnp.float32),
        ],
        in_specs=[pl.BlockSpec(memory_space=pltpu.SMEM)] + [vmem] * 3,
        out_specs=[vmem] * 2,
        compiler_params=pltpu.CompilerParams(vmem_limit_bytes=SMALL_VMEM),
        cost_estimate=pl.CostEstimate(
            flops=10**11, bytes_accessed=2 * 10**8, transcendentals=0
        ),
        name="combine_later",
    )(ids, one, two, three)


def combine_kernel(table, zero, values, sides, out, gate):
    own, noise = stats_of(zero[ROWS : ROWS + STAT, :])
    for head in range(HEADS_HERE):
        at = slice(head * HD, (head + 1) * HD)
        value, unused, row_sum = merged(
            [
                share_of(zero, own, head, True),
                (
                    values[:, at],
                    sides[:, head : head + 1],
                    sides[:, HEADS_HERE + head : HEADS_HERE + head + 1],
                ),
            ]
        )
        out[:, at] = (value / row_sum).astype(jnp.bfloat16)
    index = lax.broadcasted_iota(jnp.int32, table.shape, 0).astype(jnp.float32)
    gate[...] = jnp.sum(jnp.where(index == noise, table[...], 0.0), axis=0, keepdims=True)


def combine(table, zero, values, sides):
    vmem = pl.BlockSpec(memory_space=pltpu.VMEM)
    return pl.pallas_call(
        combine_kernel,
        out_shape=[
            jax.ShapeDtypeStruct((ROWS, WIDTH), jnp.bfloat16),
            jax.ShapeDtypeStruct((1, table.shape[1]), jnp.float32),
        ],
        in_specs=[vmem] * 4,
        out_specs=[vmem] * 2,
        compiler_params=pltpu.CompilerParams(vmem_limit_bytes=SMALL_VMEM),
        name="combine",
    )(table, zero, values, sides)


def finish_kernel(hidden, near, arrived, gate, out):
    projected = near[...] + arrived[...].astype(jnp.float32)
    out[...] = (hidden[...].astype(jnp.float32) + gate[...] * projected).astype(jnp.bfloat16)


def finish(hidden, near, arrived, gate):
    part = hidden.shape[1]
    rows = pl.BlockSpec((ROWS // 4, part), lambda i: (i, 0))
    return pl.pallas_call(
        finish_kernel,
        grid=(4,),
        out_shape=jax.ShapeDtypeStruct(hidden.shape, jnp.bfloat16),
        in_specs=[rows, rows, rows, pl.BlockSpec((1, part), lambda i: (0, 0))],
        out_specs=rows,
        compiler_params=pltpu.CompilerParams(vmem_limit_bytes=SMALL_VMEM),
        name="finish",
    )(hidden, near, arrived, gate)


def pack_kernel(keys, values, pair):
    pair[:, :WIDTH] = keys[...]
    pair[:, WIDTH:] = values[...]


def pack(keys, values):
    vmem = pl.BlockSpec(memory_space=pltpu.VMEM)
    return pl.pallas_call(
        pack_kernel,
        out_shape=jax.ShapeDtypeStruct((ROWS, 2 * WIDTH), jnp.bfloat16),
        in_specs=[vmem] * 2,
        out_specs=vmem,
        compiler_params=pltpu.CompilerParams(vmem_limit_bytes=WHOLE_VMEM),
        name="pack",
    )(keys, values)


def copies_kernel(plan, ids, *refs):
    inputs, outs, sem = refs[: plan[0]], refs[plan[0] : -1], refs[-1]
    copies = []
    for n, (kind, source, target, number) in enumerate(plan[1]):
        src, dst = inputs[source], outs[target]
        if kind == "columns":
            width = dst.shape[1]
            src = src.at[:, pl.ds(pl.multiple_of(ids[number] * width, width), width)]
        else:
            dst = dst.at[number]
        copies.append(pltpu.make_async_copy(src, dst, sem.at[n]))
    for copy in copies:
        copy.start()
    for copy in copies:
        copy.wait()


def copied(name, ids, inputs, shapes, plan):
    anywhere = pl.BlockSpec(memory_space=pl.ANY)
    return pl.pallas_call(
        functools.partial(copies_kernel, (len(inputs), plan)),
        out_shape=[jax.ShapeDtypeStruct(shape, jnp.bfloat16) for shape in shapes],
        in_specs=[pl.BlockSpec(memory_space=pltpu.SMEM)] + [anywhere] * len(inputs),
        out_specs=[anywhere] * len(shapes),
        scratch_shapes=[pltpu.SemaphoreType.DMA((len(plan),))],
        compiler_params=pltpu.CompilerParams(vmem_limit_bytes=SMALL_VMEM),
        name=name,
    )(ids, *inputs)


def project_kernel(far, ids, *refs):
    rows, own, fetched, swapped, out, held, sem = refs[0:4], refs[4], refs[5], refs[6], refs[7], refs[8], refs[9]
    mine = ids[2] == (1 if far else 0)

    @pl.when(mine)
    def _():
        pltpu.make_async_copy(fetched, held, sem).start()

    @pl.when(jnp.logical_not(mine))
    def _():
        pltpu.make_async_copy(swapped, held, sem).start()

    pltpu.make_async_copy(fetched, held, sem).wait()
    block = out.shape[1] // 3

    def columns(n, unused):
        at = pl.ds(pl.multiple_of(n * block, block), block)
        total = jnp.dot(rows[0][...], own[:, at], preferred_element_type=jnp.float32)
        for k in range(3):
            total = total + jnp.dot(
                rows[k + 1][...], held[k, :, at], preferred_element_type=jnp.float32
            )
        out[:, at] = total.astype(out.dtype)
        return 0

    lax.fori_loop(0, 3, columns, 0)


def project(far, ids, rows, own, fetched, swapped):
    vmem = pl.BlockSpec(memory_space=pltpu.VMEM)
    anywhere = pl.BlockSpec(memory_space=pl.ANY)
    part = own.shape[1]
    return pl.pallas_call(
        functools.partial(project_kernel, far),
        out_shape=jax.ShapeDtypeStruct((ROWS, part), jnp.bfloat16 if far else jnp.float32),
        in_specs=[pl.BlockSpec(memory_space=pltpu.SMEM)] + [vmem] * 5 + [anywhere] * 2,
        out_specs=vmem,
        scratch_shapes=[pltpu.VMEM((3, WIDTH, part), jnp.bfloat16), pltpu.SemaphoreType.DMA],
        compiler_params=pltpu.CompilerParams(vmem_limit_bytes=SMALL_VMEM),
        cost_estimate=pl.CostEstimate(
            flops=8 * ROWS * WIDTH * part, bytes_accessed=5 * 10**6, transcendentals=0
        ),
        name="project",
    )(ids, *rows, own, fetched, swapped)


def around(value, axis, steps):
    count = lax.axis_size(axis)
    return lax.ppermute(value, axis, [(i, (i + steps) % count) for i in range(count)])


def together(*values):
    return lax.optimization_barrier(values)


def per_device(hidden, queries, key_rows, values, out_weight, level_table, noise_level, group_live):
    z, y, core = lax.axis_index("z"), lax.axis_index("y"), lax.axis_index("c")
    w, x = lax.axis_index("w"), lax.axis_index("x")
    slot = z * 8 + y * 2 + core
    home = lax.rem(slot + 1, 32) // 8
    block = jnp.where(core == 0, w, 1 - w) * 4
    owners = [block + lax.rem(x + step, 4) for step in (1, 2, 3)] + [w * 4 + x, (1 - w) * 4 + x]
    ids = jnp.stack([z, y, core, home, *owners]).astype(jnp.int32)
    column_block = (out_weight.shape[0], out_weight.shape[1] // 8)

    def to_level(value, d):
        return lax.ppermute(value, "z", [(i, i - d) for i in range(d, 4)])

    pair = pack(key_rows, values)
    *pieces, weight_near, weight_far = copied(
        "columns",
        ids,
        [out_weight],
        [column_block] * 5,
        tuple(("columns", 0, k, 4 + k) for k in range(5)),
    )
    next_one, next_three, below, above, pair_there, pair, queries, hidden, *pieces = together(
        to_level(queries, 1),
        to_level(queries, 3),
        around(pair, "y", 1),
        around(pair, "y", -1),
        around(pair, "c", 1),
        pair,
        queries,
        hidden,
        *pieces,
    )
    states = attend(
        "early",
        ids,
        group_live,
        noise_level,
        [next_one, next_three, queries],
        [pair, below, above, None, pair_there],
    )
    next_two, across, piece_one, piece_three, below_there, piece_two, above, *states = together(
        to_level(queries, 2),
        around(pair, "y", 2),
        around(pieces[0], "x", 1),
        around(pieces[2], "x", 3),
        around(below, "c", 1),
        pieces[1],
        above,
        *states,
    )
    above_there, across_there = around(above, "c", 1), around(across, "c", 1)
    pairs = [pair, below, above, across, pair_there, below_there, above_there, across_there]
    piece_two = around(piece_two, "x", 2)

    def back(share, d):
        pairs_back = [
            (8 * (i - d) + j, (8 * i + j - 1) % 32) for i in range(d, 4) for j in range(8)
        ]
        return lax.ppermute(share, SLOT, pairs_back)

    (two,) = attend("third", ids, group_live, noise_level, [next_two], pairs)
    back_two = back(two, 2)
    live_middle, two = together(group_live, two)
    one, three = attend(
        "middle", ids, live_middle, noise_level, [next_one, next_three], pairs, states[0:2]
    )
    back_one, back_three = back(one, 1), back(three, 3)
    live_late, one = together(group_live, one)
    (zero,) = attend("late", ids, live_late, noise_level, [queries], pairs, states[2:4])
    zero, back_two, piece_two = together(zero, back_two, piece_two)
    (fetched,) = copied(
        "stack",
        ids,
        [piece_one, piece_two, piece_three],
        [(3, *column_block)],
        tuple(("stack", k, 0, k) for k in range(3)),
    )
    swapped = around(fetched, "c", 1)
    values_later, sides_later = combine_later(ids, back_one, back_two, back_three)
    attended, gate_row = combine(level_table, back(zero, 0), values_later, sides_later)

    attended, hidden = together(attended, hidden)
    hidden_next = around(hidden, SLOT, -1)
    rows = [attended] + [around(attended, "x", step) for step in (1, 2, 3)]
    far_sum = project(True, ids, rows, weight_far, fetched, swapped)
    arrived = around(far_sum, "w", 1)
    near_sum = project(False, ids, rows, weight_near, fetched, swapped)
    return finish(hidden_next, near_sum, arrived, gate_row)


def solution(mesh):
    fine = Mesh(np.asarray(mesh.devices).reshape(4, 4, 2, 2, 4), ("z", "y", "c", "w", "x"))
    tp = ("w", "x")
    block = P(SLOT, tp)
    in_specs = (block, block, block, block, P(tp, None), P(None, tp), P(SLOT), P())
    return jax.shard_map(
        per_device, mesh=fine, in_specs=in_specs, out_specs=block, check_vma=False
    )
```

```python
import functools
import math

import jax
import jax.numpy as jnp
import numpy as np
from jax import lax
from jax.experimental import pallas as pl
from jax.experimental.pallas import tpu as pltpu
from jax.sharding import Mesh
from jax.sharding import PartitionSpec as P

HD = 128
ROWS = 448
HEADS_HERE = 3
WIDTH = HEADS_HERE * HD
STAT = 32
LOWEST = -(2.0**100)
EXP2_SCALE = HD**-0.5 * math.log2(math.e)
Y_STEPS = (0, -1, 1, 2)
SLOT = ("z", "y", "c")
ATTEND_VMEM = 30 * 1024 * 1024
SMALL_VMEM = 8 * 1024 * 1024
WHOLE_VMEM = 60 * 1024 * 1024


def score(query, key):
    return lax.dot_general(
        query, key, (((1,), (1,)), ((), ())), preferred_element_type=jnp.float32
    )


CALLS = {"early": (1, 3, 0), "third": (2,), "middle": (1, 3), "late": (0,)}
EARLY, LATER, ALL = (0, 1, 2, 4), (3, 5, 6, 7), tuple(range(8))
MEMBERS = {"early": EARLY, "third": ALL, "middle": LATER, "late": LATER}
COSTS = {"early": 10**10, "third": 10**10, "middle": 5 * 10**10, "late": 10**6}


def attend_kernel(call, ids, live, level, *refs):
    steps = CALLS[call]
    many = len(steps)
    early, resumed = call == "early", call in ("middle", "late")
    members = MEMBERS[call]
    refs = list(refs)

    def take(count):
        taken = refs[:count]
        del refs[:count]
        return taken

    query_in, pair_in = take(many), take(len(members))
    state_in = take(2) if resumed else []
    out = take(4 if early else many)
    raw, scaled, pairs, held, acc, top, done, raw_sem, pair_sem, state_sem, out_sem = refs
    here, y, core = ids[0], ids[1], ids[2]
    first = here * 8
    mine = first + y * 2 + core
    groups = {}
    for p in members:
        core_there = core if p < 4 else 1 - core
        groups[p] = first + lax.rem(y + Y_STEPS[p % 4] + 4, 4) * 2 + core_there

    def live_before(group):
        count = jnp.int32(0)
        for p in members:
            count = count + jnp.where(groups[p] < group, live[groups[p]], 0)
        return count

    bound = mine if call == "late" else first + 8
    n_live, n_before = live_before(bound), live_before(mine)
    own_place = jnp.where(live[mine] == 1, n_before, n_live)

    def active(i):
        return here + steps[i] <= 3

    def raw_copy(i):
        return pltpu.make_async_copy(query_in[i], raw.at[i], raw_sem.at[i])

    def place_copy(j, place):
        at = pl.ds(pl.multiple_of(place * ROWS, 64), ROWS)
        return pltpu.make_async_copy(pair_in[j], pairs.at[at], pair_sem.at[place])

    def state_copies():
        return (
            pltpu.make_async_copy(state_in[0], acc, state_sem.at[0]),
            pltpu.make_async_copy(state_in[1], top, state_sem.at[1]),
        )

    def out_copies(part):
        at = pl.ds(0, 2 * ROWS) if part == 0 else pl.ds(2 * ROWS, ROWS)
        return (
            pltpu.make_async_copy(acc.at[:, at], out[2 * part], out_sem.at[2 * part]),
            pltpu.make_async_copy(top.at[:, at], out[2 * part + 1], out_sem.at[2 * part + 1]),
        )

    def share_copy(i):
        return pltpu.make_async_copy(done.at[i], out[i], out_sem.at[i])

    def prepare(i):
        raw_copy(i).wait()
        at = slice(i * ROWS, (i + 1) * ROWS)
        for head in range(HEADS_HERE):
            exact = raw[i, :, head * HD : (head + 1) * HD].astype(jnp.float32) * EXP2_SCALE
            high = exact.astype(jnp.bfloat16)
            scaled[head, at, :HD] = high
            scaled[head, at, HD:] = (exact - high.astype(jnp.float32)).astype(jnp.bfloat16)

    def sweep(start, rows, count, place_of, waits, loop_heads):
        span = slice(start, start + rows)
        chunks = (count + 1) // 2

        def arrive(t):
            if waits:
                for k in (2 * t, 2 * t + 1):

                    @pl.when(k < count)
                    def _():
                        place_copy(0, k).wait()

        def at(k):
            place = place_of(jnp.maximum(jnp.minimum(k, count - 1), 0))
            return pl.ds(pl.multiple_of(place * ROWS, 64), ROWS)

        def columns(base, head):
            if isinstance(head, int):
                return slice(base + head * HD, base + (head + 1) * HD)
            return pl.ds(pl.multiple_of(base + head * HD, HD), HD)

        def scores_of(t, head):
            cols = columns(0, head)
            key = jnp.concatenate([pairs[at(2 * t), cols], pairs[at(2 * t + 1), cols]], axis=0)
            return score(scaled[head, span], jnp.concatenate([key, key], axis=1))

        def absorb(t, head, scores):
            old = top[head, span]
            new = jnp.maximum(old, jnp.max(scores, axis=1, keepdims=True))
            weights = jnp.exp2(scores - jnp.concatenate([new] * (2 * ROWS // HD), axis=1))
            cols = columns(WIDTH, head)
            there = jnp.where(2 * t + 1 < count, 1.0, 0.0).astype(jnp.bfloat16)
            ones = jnp.ones((ROWS, HD), jnp.bfloat16)
            value = jnp.concatenate(
                [
                    jnp.concatenate([pairs[at(2 * t), cols], ones], axis=1),
                    jnp.concatenate([pairs[at(2 * t + 1), cols], ones], axis=1) * there,
                ],
                axis=0,
            )
            weighted = jnp.dot(
                weights.astype(jnp.bfloat16), value, preferred_element_type=jnp.float32
            )
            shrink = jnp.exp2(old - new)
            acc[head, span] = (
                acc[head, span] * jnp.concatenate([shrink, shrink], axis=1) + weighted
            )
            top[head, span] = new

        arrive(0)

        @pl.when(chunks > 0)
        def _():
            held[0:rows] = scores_of(0, 0)

        if loop_heads:

            def unit(u, unused):
                head, t = lax.rem(u, HEADS_HERE), u // HEADS_HERE
                scores = held[0:rows]

                @pl.when(head == 1)
                def _():
                    arrive(t + 1)

                following = jnp.minimum(u + 1, HEADS_HERE * chunks - 1)
                upcoming = scores_of(following // HEADS_HERE, lax.rem(following, HEADS_HERE))
                absorb(t, head, scores)
                held[0:rows] = upcoming
                return 0

            lax.fori_loop(0, HEADS_HERE * chunks, unit, 0)
            return

        def chunk(t, unused):
            scores = held[0:rows]
            following = scores_of(t, 1)
            absorb(t, 0, scores)
            scores = scores_of(t, 2)
            absorb(t, 1, following)
            arrive(t + 1)
            held[0:rows] = scores_of(t + 1, 0)
            absorb(t, 2, scores)
            return 0

        lax.fori_loop(0, chunks, chunk, 0)

    def finish(i, unused):
        span = pl.ds(pl.multiple_of(i * ROWS, 64), ROWS)
        lane = lax.broadcasted_iota(jnp.int32, (ROWS, HD), 1)
        stats = jnp.where(lane == 3 * HEADS_HERE, level[0].astype(jnp.float32), 0.0)
        for head in range(HEADS_HERE):
            exact = top[head, span]
            sent = exact.astype(jnp.bfloat16).astype(jnp.float32)
            factor = jnp.exp2(exact - sent)
            weighted = acc[head, span]
            done[i, 0:ROWS, head * HD : (head + 1) * HD] = (weighted[:, :HD] * factor).astype(
                jnp.bfloat16
            )
            total = weighted[:, HD:] * factor
            high = total.astype(jnp.bfloat16).astype(jnp.float32)
            stats = jnp.where(lane == head, sent, stats)
            stats = jnp.where(lane == HEADS_HERE + head, high, stats)
            stats = jnp.where(lane == 2 * HEADS_HERE + head, total - high, stats)
        flat = jnp.transpose(stats)[:16].astype(jnp.bfloat16)
        done[i, ROWS : ROWS + 16, :] = flat[:, :WIDTH]
        pad = jnp.zeros((16, 2 * WIDTH - ROWS), jnp.bfloat16)
        done[i, ROWS + 16 : ROWS + 32, :] = jnp.concatenate([flat[:, WIDTH:], pad], axis=1)
        for k in range(many):

            @pl.when(i == k)
            def _():
                share_copy(k).start()

        return 0

    def first_sources(waits):
        @pl.when(active(1))
        def _():
            sweep(0, 2 * ROWS, n_live, lambda k: k, waits, True)

        @pl.when(active(0) & jnp.logical_not(active(1)))
        def _():
            sweep(0, ROWS, n_live, lambda k: k, waits, True)

    def run():
        if resumed:
            for copy in state_copies():
                copy.start()
        for j, p in enumerate(members):
            if early and p == 0:
                place_copy(j, own_place).start()
                continue

            @pl.when((live[groups[p]] == 1) & (groups[p] < bound))
            def _():
                place_copy(j, live_before(groups[p])).start()

        for i in range(many):
            pl.when(active(i))(raw_copy(i).start)
        if early:
            place_copy(0, own_place).wait()
            for k in range(len(EARLY)):

                @pl.when((k < n_live) & (k != own_place))
                def _():
                    place_copy(0, k).wait()

        for i in range(many):
            pl.when(active(i))(functools.partial(prepare, i))
        if resumed:
            for copy in state_copies():
                copy.wait()
        else:
            top[...] = jnp.full(top.shape, LOWEST, jnp.float32)
            acc[...] = jnp.zeros(acc.shape, jnp.float32)
        if early:

            first_sources(False)

            @pl.when(active(0))
            def _():
                for copy in out_copies(0):
                    copy.start()

            sweep(
                2 * ROWS,
                ROWS,
                n_before + 1,
                lambda k: jnp.where(k < n_before, k, own_place),
                False,
                False,
            )
            for copy in out_copies(1):
                copy.start()
            for copy in out_copies(1):
                copy.wait()

            @pl.when(active(0))
            def _():
                for copy in out_copies(0):
                    copy.wait()

            return

        if many == 2:
            first_sources(True)
        else:
            sweep(0, ROWS, n_live, lambda k: k, True, False)
        lax.fori_loop(0, jnp.where(active(many - 1), many, 1), finish, 0)
        for i in range(many):
            pl.when(active(i))(share_copy(i).wait)

    if early:
        run()
    else:
        pl.when(active(0))(run)


def attend(call, ids, live, level, queries, pairs, states=()):
    smem = pl.BlockSpec(memory_space=pltpu.SMEM)
    anywhere = pl.BlockSpec(memory_space=pl.ANY)
    bf16, f32 = jnp.bfloat16, jnp.float32
    many = len(CALLS[call])
    members = MEMBERS[call]
    together_rows = 2 * ROWS if call in ("early", "middle") else ROWS

    def state(rows):
        return [(HEADS_HERE, rows, 2 * HD), (HEADS_HERE, rows, HD)]

    if call == "early":
        out_shape = [jax.ShapeDtypeStruct(shape, f32) for shape in state(2 * ROWS) + state(ROWS)]
    else:
        out_shape = [jax.ShapeDtypeStruct((ROWS + STAT, WIDTH), bf16)] * many
    operands = [*queries, *[pairs[p] for p in members], *states]
    rows = many * ROWS
    return pl.pallas_call(
        functools.partial(attend_kernel, call),
        out_shape=out_shape,
        in_specs=[smem] * 3 + [anywhere] * len(operands),
        out_specs=[anywhere] * len(out_shape),
        scratch_shapes=[
            pltpu.VMEM((many, ROWS, WIDTH), bf16),
            pltpu.VMEM((HEADS_HERE, rows, 2 * HD), bf16),
            pltpu.VMEM((8 * ROWS, 2 * WIDTH), bf16),
            pltpu.VMEM((together_rows, 2 * ROWS), f32),
            pltpu.VMEM(state(rows)[0], f32),
            pltpu.VMEM(state(rows)[1], f32),
            pltpu.VMEM((many, ROWS + STAT, WIDTH), bf16),
            pltpu.SemaphoreType.DMA((many,)),
            pltpu.SemaphoreType.DMA((8,)),
            pltpu.SemaphoreType.DMA((2,)),
            pltpu.SemaphoreType.DMA((4,)),
        ],
        compiler_params=pltpu.CompilerParams(vmem_limit_bytes=ATTEND_VMEM),
        cost_estimate=pl.CostEstimate(
            flops=COSTS[call], bytes_accessed=10**6, transcendentals=0
        ),
        name="attend_" + call,
    )(ids, live, level, *operands)


def stats_of(tail):
    tail = tail.astype(jnp.float32)
    flat = jnp.concatenate([tail[0:16], tail[16:32, : ROWS - WIDTH]], axis=1)
    noise = flat[3 * HEADS_HERE : 3 * HEADS_HERE + 1, 0:1]
    padded = jnp.concatenate([flat, jnp.zeros((HD - 16, ROWS), jnp.float32)])
    return jnp.transpose(padded), noise


def merged(parts):
    highest = parts[0][1]
    for part in parts[1:]:
        highest = jnp.maximum(highest, part[1])
    values = total = None
    for value, row_max, row_sum in parts:
        factor = jnp.exp2(row_max - highest)
        values = value * factor if values is None else values + value * factor
        total = row_sum * factor if total is None else total + row_sum * factor
    return values, highest, total


def share_of(ref, stats, head, present):
    value = ref[0:ROWS, head * HD : (head + 1) * HD].astype(jnp.float32)
    row_max = stats[:, head : head + 1]
    row_sum = (
        stats[:, HEADS_HERE + head : HEADS_HERE + head + 1]
        + stats[:, 2 * HEADS_HERE + head : 2 * HEADS_HERE + head + 1]
    )
    return (
        jnp.where(present, value, 0.0),
        jnp.where(present, row_max, LOWEST),
        jnp.where(present, row_sum, 0.0),
    )


def combine_later_kernel(ids, one, two, three, values, sides):
    home = ids[3]
    stats = [stats_of(ref[ROWS : ROWS + STAT, :])[0] for ref in (one, two, three)]
    lane = lax.broadcasted_iota(jnp.int32, (ROWS, HD), 1)
    side = jnp.zeros((ROWS, HD), jnp.float32)
    for head in range(HEADS_HERE):
        value, row_max, row_sum = merged(
            [
                share_of(one, stats[0], head, home >= 1),
                share_of(two, stats[1], head, home >= 2),
                share_of(three, stats[2], head, home >= 3),
            ]
        )
        values[:, head * HD : (head + 1) * HD] = value
        side = jnp.where(lane == head, row_max, side)
        side = jnp.where(lane == HEADS_HERE + head, row_sum, side)
    sides[...] = side


def combine_later(ids, one, two, three):
    vmem = pl.BlockSpec(memory_space=pltpu.VMEM)
    return pl.pallas_call(
        combine_later_kernel,
        out_shape=[
            jax.ShapeDtypeStruct((ROWS, WIDTH), jnp.float32),
            jax.ShapeDtypeStruct((ROWS, HD), jnp.float32),
        ],
        in_specs=[pl.BlockSpec(memory_space=pltpu.SMEM)] + [vmem] * 3,
        out_specs=[vmem] * 2,
        compiler_params=pltpu.CompilerParams(vmem_limit_bytes=SMALL_VMEM),
        cost_estimate=pl.CostEstimate(
            flops=10**11, bytes_accessed=2 * 10**8, transcendentals=0
        ),
        name="combine_later",
    )(ids, one, two, three)


def combine_kernel(table, zero, values, sides, out, gate):
    own, noise = stats_of(zero[ROWS : ROWS + STAT, :])
    for head in range(HEADS_HERE):
        at = slice(head * HD, (head + 1) * HD)
        value, unused, row_sum = merged(
            [
                share_of(zero, own, head, True),
                (
                    values[:, at],
                    sides[:, head : head + 1],
                    sides[:, HEADS_HERE + head : HEADS_HERE + head + 1],
                ),
            ]
        )
        out[:, at] = (value / row_sum).astype(jnp.bfloat16)
    index = lax.broadcasted_iota(jnp.int32, table.shape, 0).astype(jnp.float32)
    gate[...] = jnp.sum(jnp.where(index == noise, table[...], 0.0), axis=0, keepdims=True)


def combine(table, zero, values, sides):
    vmem = pl.BlockSpec(memory_space=pltpu.VMEM)
    return pl.pallas_call(
        combine_kernel,
        out_shape=[
            jax.ShapeDtypeStruct((ROWS, WIDTH), jnp.bfloat16),
            jax.ShapeDtypeStruct((1, table.shape[1]), jnp.float32),
        ],
        in_specs=[vmem] * 4,
        out_specs=[vmem] * 2,
        compiler_params=pltpu.CompilerParams(vmem_limit_bytes=SMALL_VMEM),
        name="combine",
    )(table, zero, values, sides)


def finish_kernel(hidden, near, arrived, gate, out):
    projected = near[...] + arrived[...].astype(jnp.float32)
    out[...] = (hidden[...].astype(jnp.float32) + gate[...] * projected).astype(jnp.bfloat16)


def finish(hidden, near, arrived, gate):
    part = hidden.shape[1]
    rows = pl.BlockSpec((ROWS // 4, part), lambda i: (i, 0))
    return pl.pallas_call(
        finish_kernel,
        grid=(4,),
        out_shape=jax.ShapeDtypeStruct(hidden.shape, jnp.bfloat16),
        in_specs=[rows, rows, rows, pl.BlockSpec((1, part), lambda i: (0, 0))],
        out_specs=rows,
        compiler_params=pltpu.CompilerParams(vmem_limit_bytes=SMALL_VMEM),
        name="finish",
    )(hidden, near, arrived, gate)


def pack_kernel(keys, values, pair):
    pair[:, :WIDTH] = keys[...]
    pair[:, WIDTH:] = values[...]


def pack(keys, values):
    vmem = pl.BlockSpec(memory_space=pltpu.VMEM)
    return pl.pallas_call(
        pack_kernel,
        out_shape=jax.ShapeDtypeStruct((ROWS, 2 * WIDTH), jnp.bfloat16),
        in_specs=[vmem] * 2,
        out_specs=vmem,
        compiler_params=pltpu.CompilerParams(vmem_limit_bytes=WHOLE_VMEM),
        name="pack",
    )(keys, values)


def copies_kernel(plan, ids, *refs):
    inputs, outs, sem = refs[: plan[0]], refs[plan[0] : -1], refs[-1]
    copies = []
    for n, (kind, source, target, number) in enumerate(plan[1]):
        src, dst = inputs[source], outs[target]
        if kind == "columns":
            width = dst.shape[1]
            src = src.at[:, pl.ds(pl.multiple_of(ids[number] * width, width), width)]
        else:
            dst = dst.at[number]
        copies.append(pltpu.make_async_copy(src, dst, sem.at[n]))
    for copy in copies:
        copy.start()
    for copy in copies:
        copy.wait()


def copied(name, ids, inputs, shapes, plan):
    anywhere = pl.BlockSpec(memory_space=pl.ANY)
    return pl.pallas_call(
        functools.partial(copies_kernel, (len(inputs), plan)),
        out_shape=[jax.ShapeDtypeStruct(shape, jnp.bfloat16) for shape in shapes],
        in_specs=[pl.BlockSpec(memory_space=pltpu.SMEM)] + [anywhere] * len(inputs),
        out_specs=[anywhere] * len(shapes),
        scratch_shapes=[pltpu.SemaphoreType.DMA((len(plan),))],
        compiler_params=pltpu.CompilerParams(vmem_limit_bytes=SMALL_VMEM),
        name=name,
    )(ids, *inputs)


def project_kernel(far, ids, *refs):
    rows, own, fetched, swapped, out, held, sem = refs[0:4], refs[4], refs[5], refs[6], refs[7], refs[8], refs[9]
    mine = ids[2] == (1 if far else 0)

    @pl.when(mine)
    def _():
        pltpu.make_async_copy(fetched, held, sem).start()

    @pl.when(jnp.logical_not(mine))
    def _():
        pltpu.make_async_copy(swapped, held, sem).start()

    block = out.shape[1] // 3

    def columns(n, unused):
        at = pl.ds(pl.multiple_of(n * block, block), block)
        total = jnp.dot(rows[0][...], own[:, at], preferred_element_type=jnp.float32)

        @pl.when(n == 0)
        def _():
            pltpu.make_async_copy(fetched, held, sem).wait()

        for k in range(3):
            total = total + jnp.dot(
                rows[k + 1][...], held[k, :, at], preferred_element_type=jnp.float32
            )
        out[:, at] = total.astype(out.dtype)
        return 0

    lax.fori_loop(0, 3, columns, 0)


def project(far, ids, rows, own, fetched, swapped):
    vmem = pl.BlockSpec(memory_space=pltpu.VMEM)
    anywhere = pl.BlockSpec(memory_space=pl.ANY)
    part = own.shape[1]
    return pl.pallas_call(
        functools.partial(project_kernel, far),
        out_shape=jax.ShapeDtypeStruct((ROWS, part), jnp.bfloat16 if far else jnp.float32),
        in_specs=[pl.BlockSpec(memory_space=pltpu.SMEM)] + [vmem] * 5 + [anywhere] * 2,
        out_specs=vmem,
        scratch_shapes=[pltpu.VMEM((3, WIDTH, part), jnp.bfloat16), pltpu.SemaphoreType.DMA],
        compiler_params=pltpu.CompilerParams(vmem_limit_bytes=SMALL_VMEM),
        cost_estimate=pl.CostEstimate(
            flops=8 * ROWS * WIDTH * part, bytes_accessed=5 * 10**6, transcendentals=0
        ),
        name="project",
    )(ids, *rows, own, fetched, swapped)


def around(value, axis, steps):
    count = lax.axis_size(axis)
    return lax.ppermute(value, axis, [(i, (i + steps) % count) for i in range(count)])


def together(*values):
    return lax.optimization_barrier(values)


def per_device(hidden, queries, key_rows, values, out_weight, level_table, noise_level, group_live):
    z, y, core = lax.axis_index("z"), lax.axis_index("y"), lax.axis_index("c")
    w, x = lax.axis_index("w"), lax.axis_index("x")
    slot = z * 8 + y * 2 + core
    home = lax.rem(slot + 1, 32) // 8
    block = jnp.where(core == 0, w, 1 - w) * 4
    owners = [block + lax.rem(x + step, 4) for step in (1, 2, 3)] + [w * 4 + x, (1 - w) * 4 + x]
    ids = jnp.stack([z, y, core, home, *owners]).astype(jnp.int32)
    column_block = (out_weight.shape[0], out_weight.shape[1] // 8)

    def to_level(value, d):
        return lax.ppermute(value, "z", [(i, i - d) for i in range(d, 4)])

    pair = pack(key_rows, values)
    *pieces, weight_near, weight_far = copied(
        "columns",
        ids,
        [out_weight],
        [column_block] * 5,
        tuple(("columns", 0, k, 4 + k) for k in range(5)),
    )
    next_one, next_three, below, above, pair_there, pair, queries, hidden, *pieces = together(
        to_level(queries, 1),
        to_level(queries, 3),
        around(pair, "y", 1),
        around(pair, "y", -1),
        around(pair, "c", 1),
        pair,
        queries,
        hidden,
        *pieces,
    )
    states = attend(
        "early",
        ids,
        group_live,
        noise_level,
        [next_one, next_three, queries],
        [pair, below, above, None, pair_there],
    )
    next_two, across, piece_three, below_there, above_there, piece_one, piece_two, *states = together(
        to_level(queries, 2),
        around(pair, "y", 2),
        around(pieces[2], "x", 3),
        around(below, "c", 1),
        around(above, "c", 1),
        pieces[0],
        pieces[1],
        *states,
    )
    across_there = around(across, "c", 1)
    pairs = [pair, below, above, across, pair_there, below_there, above_there, across_there]
    piece_one, piece_two = around(piece_one, "x", 1), around(piece_two, "x", 2)

    def back(share, d):
        pairs_back = [
            (8 * (i - d) + j, (8 * i + j - 1) % 32) for i in range(d, 4) for j in range(8)
        ]
        return lax.ppermute(share, SLOT, pairs_back)

    (two,) = attend("third", ids, group_live, noise_level, [next_two], pairs)
    back_two = back(two, 2)
    live_middle, two = together(group_live, two)
    one, three = attend(
        "middle", ids, live_middle, noise_level, [next_one, next_three], pairs, states[0:2]
    )
    back_one, back_three = back(one, 1), back(three, 3)
    live_late, one = together(group_live, one)
    (zero,) = attend("late", ids, live_late, noise_level, [queries], pairs, states[2:4])
    zero, back_two, piece_one, piece_two = together(zero, back_two, piece_one, piece_two)
    (fetched,) = copied(
        "stack",
        ids,
        [piece_one, piece_two, piece_three],
        [(3, *column_block)],
        tuple(("stack", k, 0, k) for k in range(3)),
    )
    swapped = around(fetched, "c", 1)
    values_later, sides_later = combine_later(ids, back_one, back_two, back_three)
    attended, gate_row = combine(level_table, back(zero, 0), values_later, sides_later)

    attended, hidden = together(attended, hidden)
    hidden_next = around(hidden, SLOT, -1)
    rows = [attended] + [around(attended, "x", step) for step in (1, 2, 3)]
    far_sum = project(True, ids, rows, weight_far, fetched, swapped)
    arrived = around(far_sum, "w", 1)
    near_sum = project(False, ids, rows, weight_near, fetched, swapped)
    return finish(hidden_next, near_sum, arrived, gate_row)


def solution(mesh):
    fine = Mesh(np.asarray(mesh.devices).reshape(4, 4, 2, 2, 4), ("z", "y", "c", "w", "x"))
    tp = ("w", "x")
    block = P(SLOT, tp)
    in_specs = (block, block, block, block, P(tp, None), P(None, tp), P(SLOT), P())
    return jax.shard_map(
        per_device, mesh=fine, in_specs=in_specs, out_specs=block, check_vma=False
    )
```

```python
import functools
import math

import jax
import jax.numpy as jnp
import numpy as np
from jax import lax
from jax.experimental import pallas as pl
from jax.experimental.pallas import tpu as pltpu
from jax.sharding import Mesh
from jax.sharding import PartitionSpec as P

HD = 128
ROWS = 448
HEADS_HERE = 3
WIDTH = HEADS_HERE * HD
STAT = 32
LOWEST = -(2.0**100)
EXP2_SCALE = HD**-0.5 * math.log2(math.e)
Y_STEPS = (0, -1, 1, 2)
SLOT = ("z", "y", "c")
ATTEND_VMEM = 30 * 1024 * 1024
SMALL_VMEM = 8 * 1024 * 1024
WHOLE_VMEM = 60 * 1024 * 1024


def score(query, key):
    return lax.dot_general(
        query, key, (((1,), (1,)), ((), ())), preferred_element_type=jnp.float32
    )


CALLS = {"early": (1, 3, 0), "third": (2,), "middle": (1, 3), "late": (0,)}
EARLY, LATER, ALL = (0, 1, 2, 4), (3, 5, 6, 7), tuple(range(8))
MEMBERS = {"early": EARLY, "third": ALL, "middle": LATER, "late": LATER}
COSTS = {"early": 10**10, "third": 10**10, "middle": 5 * 10**10, "late": 10**6}


def attend_kernel(call, ids, live, level, *refs):
    steps = CALLS[call]
    many = len(steps)
    early, resumed = call == "early", call in ("middle", "late")
    members = MEMBERS[call]
    refs = list(refs)

    def take(count):
        taken = refs[:count]
        del refs[:count]
        return taken

    query_in, pair_in = take(many), take(len(members))
    state_in = take(2) if resumed else []
    out = take(4 if early else many)
    raw, scaled, pairs, held, acc, top, done, raw_sem, pair_sem, state_sem, out_sem = refs
    here, y, core = ids[0], ids[1], ids[2]
    first = here * 8
    mine = first + y * 2 + core
    groups = {}
    for p in members:
        core_there = core if p < 4 else 1 - core
        groups[p] = first + lax.rem(y + Y_STEPS[p % 4] + 4, 4) * 2 + core_there

    def live_before(group):
        count = jnp.int32(0)
        for p in members:
            count = count + jnp.where(groups[p] < group, live[groups[p]], 0)
        return count

    bound = mine if call == "late" else first + 8
    n_live, n_before = live_before(bound), live_before(mine)
    own_place = jnp.where(live[mine] == 1, n_before, n_live)

    def active(i):
        return here + steps[i] <= 3

    def raw_copy(i):
        return pltpu.make_async_copy(query_in[i], raw.at[i], raw_sem.at[i])

    def place_copy(j, place):
        at = pl.ds(pl.multiple_of(place * ROWS, 64), ROWS)
        return pltpu.make_async_copy(pair_in[j], pairs.at[at], pair_sem.at[place])

    def state_copies():
        return (
            pltpu.make_async_copy(state_in[0], acc, state_sem.at[0]),
            pltpu.make_async_copy(state_in[1], top, state_sem.at[1]),
        )

    def out_copies(part):
        at = pl.ds(0, 2 * ROWS) if part == 0 else pl.ds(2 * ROWS, ROWS)
        return (
            pltpu.make_async_copy(acc.at[:, at], out[2 * part], out_sem.at[2 * part]),
            pltpu.make_async_copy(top.at[:, at], out[2 * part + 1], out_sem.at[2 * part + 1]),
        )

    def share_copy(i):
        return pltpu.make_async_copy(done.at[i], out[i], out_sem.at[i])

    def prepare(i):
        raw_copy(i).wait()
        at = slice(i * ROWS, (i + 1) * ROWS)
        for head in range(HEADS_HERE):
            exact = raw[i, :, head * HD : (head + 1) * HD].astype(jnp.float32) * EXP2_SCALE
            high = exact.astype(jnp.bfloat16)
            scaled[head, at, :HD] = high
            scaled[head, at, HD:] = (exact - high.astype(jnp.float32)).astype(jnp.bfloat16)

    def sweep(start, rows, count, place_of, waits, loop_heads):
        span = slice(start, start + rows)
        chunks = (count + 1) // 2

        def arrive(t):
            if waits:
                for k in (2 * t, 2 * t + 1):

                    @pl.when(k < count)
                    def _():
                        place_copy(0, k).wait()

        def at(k):
            place = place_of(jnp.maximum(jnp.minimum(k, count - 1), 0))
            return pl.ds(pl.multiple_of(place * ROWS, 64), ROWS)

        def columns(base, head):
            if isinstance(head, int):
                return slice(base + head * HD, base + (head + 1) * HD)
            return pl.ds(pl.multiple_of(base + head * HD, HD), HD)

        def scores_of(t, head):
            cols = columns(0, head)
            key = jnp.concatenate([pairs[at(2 * t), cols], pairs[at(2 * t + 1), cols]], axis=0)
            return score(scaled[head, span], jnp.concatenate([key, key], axis=1))

        def absorb(t, head, scores):
            old = top[head, span]
            new = jnp.maximum(old, jnp.max(scores, axis=1, keepdims=True))
            weights = jnp.exp2(scores - jnp.concatenate([new] * (2 * ROWS // HD), axis=1))
            cols = columns(WIDTH, head)
            there = jnp.where(2 * t + 1 < count, 1.0, 0.0).astype(jnp.bfloat16)
            ones = jnp.ones((ROWS, HD), jnp.bfloat16)
            value = jnp.concatenate(
                [
                    jnp.concatenate([pairs[at(2 * t), cols], ones], axis=1),
                    jnp.concatenate([pairs[at(2 * t + 1), cols], ones], axis=1) * there,
                ],
                axis=0,
            )
            weighted = jnp.dot(
                weights.astype(jnp.bfloat16), value, preferred_element_type=jnp.float32
            )
            shrink = jnp.exp2(old - new)
            acc[head, span] = (
                acc[head, span] * jnp.concatenate([shrink, shrink], axis=1) + weighted
            )
            top[head, span] = new

        arrive(0)

        @pl.when(chunks > 0)
        def _():
            held[0:rows] = scores_of(0, 0)

        if loop_heads:

            def unit(u, unused):
                head, t = lax.rem(u, HEADS_HERE), u // HEADS_HERE
                scores = held[0:rows]

                @pl.when(head == 1)
                def _():
                    arrive(t + 1)

                following = jnp.minimum(u + 1, HEADS_HERE * chunks - 1)
                upcoming = scores_of(following // HEADS_HERE, lax.rem(following, HEADS_HERE))
                absorb(t, head, scores)
                held[0:rows] = upcoming
                return 0

            lax.fori_loop(0, HEADS_HERE * chunks, unit, 0)
            return

        def chunk(t, unused):
            scores = held[0:rows]
            following = scores_of(t, 1)
            absorb(t, 0, scores)
            scores = scores_of(t, 2)
            absorb(t, 1, following)
            arrive(t + 1)
            held[0:rows] = scores_of(t + 1, 0)
            absorb(t, 2, scores)
            return 0

        lax.fori_loop(0, chunks, chunk, 0)

    def finish(i, unused):
        span = pl.ds(pl.multiple_of(i * ROWS, 64), ROWS)
        lane = lax.broadcasted_iota(jnp.int32, (ROWS, HD), 1)
        stats = jnp.where(lane == 3 * HEADS_HERE, level[0].astype(jnp.float32), 0.0)
        for head in range(HEADS_HERE):
            exact = top[head, span]
            sent = exact.astype(jnp.bfloat16).astype(jnp.float32)
            factor = jnp.exp2(exact - sent)
            weighted = acc[head, span]
            done[i, 0:ROWS, head * HD : (head + 1) * HD] = (weighted[:, :HD] * factor).astype(
                jnp.bfloat16
            )
            total = weighted[:, HD:] * factor
            high = total.astype(jnp.bfloat16).astype(jnp.float32)
            stats = jnp.where(lane == head, sent, stats)
            stats = jnp.where(lane == HEADS_HERE + head, high, stats)
            stats = jnp.where(lane == 2 * HEADS_HERE + head, total - high, stats)
        flat = jnp.transpose(stats)[:16].astype(jnp.bfloat16)
        done[i, ROWS : ROWS + 16, :] = flat[:, :WIDTH]
        pad = jnp.zeros((16, 2 * WIDTH - ROWS), jnp.bfloat16)
        done[i, ROWS + 16 : ROWS + 32, :] = jnp.concatenate([flat[:, WIDTH:], pad], axis=1)
        for k in range(many):

            @pl.when(i == k)
            def _():
                share_copy(k).start()

        return 0

    def first_sources(waits):
        @pl.when(active(1))
        def _():
            sweep(0, 2 * ROWS, n_live, lambda k: k, waits, True)

        @pl.when(active(0) & jnp.logical_not(active(1)))
        def _():
            sweep(0, ROWS, n_live, lambda k: k, waits, True)

    def run():
        for i in range(many):
            pl.when(active(i))(raw_copy(i).start)
        for j, p in enumerate(members):
            if early and p == 0:
                place_copy(j, own_place).start()
                continue

            @pl.when((live[groups[p]] == 1) & (groups[p] < bound))
            def _():
                place_copy(j, live_before(groups[p])).start()

        if resumed:
            for copy in state_copies():
                copy.start()
        for i in range(many):
            pl.when(active(i))(functools.partial(prepare, i))
        if early:
            place_copy(0, own_place).wait()
            for k in range(len(EARLY)):

                @pl.when((k < n_live) & (k != own_place))
                def _():
                    place_copy(0, k).wait()

        if resumed:
            for copy in state_copies():
                copy.wait()
        else:
            top[...] = jnp.full(top.shape, LOWEST, jnp.float32)
            acc[...] = jnp.zeros(acc.shape, jnp.float32)
        if early:

            first_sources(False)

            @pl.when(active(0))
            def _():
                for copy in out_copies(0):
                    copy.start()

            sweep(
                2 * ROWS,
                ROWS,
                n_before + 1,
                lambda k: jnp.where(k < n_before, k, own_place),
                False,
                False,
            )
            for copy in out_copies(1):
                copy.start()
            for copy in out_copies(1):
                copy.wait()

            @pl.when(active(0))
            def _():
                for copy in out_copies(0):
                    copy.wait()

            return

        if many == 2:
            first_sources(True)
        else:
            sweep(0, ROWS, n_live, lambda k: k, True, False)
        lax.fori_loop(0, jnp.where(active(many - 1), many, 1), finish, 0)
        for i in range(many):
            pl.when(active(i))(share_copy(i).wait)

    if early:
        run()
    else:
        pl.when(active(0))(run)


def attend(call, ids, live, level, queries, pairs, states=()):
    smem = pl.BlockSpec(memory_space=pltpu.SMEM)
    anywhere = pl.BlockSpec(memory_space=pl.ANY)
    bf16, f32 = jnp.bfloat16, jnp.float32
    many = len(CALLS[call])
    members = MEMBERS[call]
    together_rows = 2 * ROWS if call in ("early", "middle") else ROWS

    def state(rows):
        return [(HEADS_HERE, rows, 2 * HD), (HEADS_HERE, rows, HD)]

    if call == "early":
        out_shape = [jax.ShapeDtypeStruct(shape, f32) for shape in state(2 * ROWS) + state(ROWS)]
    else:
        out_shape = [jax.ShapeDtypeStruct((ROWS + STAT, WIDTH), bf16)] * many
    operands = [*queries, *[pairs[p] for p in members], *states]
    rows = many * ROWS
    return pl.pallas_call(
        functools.partial(attend_kernel, call),
        out_shape=out_shape,
        in_specs=[smem] * 3 + [anywhere] * len(operands),
        out_specs=[anywhere] * len(out_shape),
        scratch_shapes=[
            pltpu.VMEM((many, ROWS, WIDTH), bf16),
            pltpu.VMEM((HEADS_HERE, rows, 2 * HD), bf16),
            pltpu.VMEM((8 * ROWS, 2 * WIDTH), bf16),
            pltpu.VMEM((together_rows, 2 * ROWS), f32),
            pltpu.VMEM(state(rows)[0], f32),
            pltpu.VMEM(state(rows)[1], f32),
            pltpu.VMEM((many, ROWS + STAT, WIDTH), bf16),
            pltpu.SemaphoreType.DMA((many,)),
            pltpu.SemaphoreType.DMA((8,)),
            pltpu.SemaphoreType.DMA((2,)),
            pltpu.SemaphoreType.DMA((4,)),
        ],
        compiler_params=pltpu.CompilerParams(vmem_limit_bytes=ATTEND_VMEM),
        cost_estimate=pl.CostEstimate(
            flops=COSTS[call], bytes_accessed=10**6, transcendentals=0
        ),
        name="attend_" + call,
    )(ids, live, level, *operands)


def stats_of(tail):
    tail = tail.astype(jnp.float32)
    flat = jnp.concatenate([tail[0:16], tail[16:32, : ROWS - WIDTH]], axis=1)
    noise = flat[3 * HEADS_HERE : 3 * HEADS_HERE + 1, 0:1]
    padded = jnp.concatenate([flat, jnp.zeros((HD - 16, ROWS), jnp.float32)])
    return jnp.transpose(padded), noise


def merged(parts):
    highest = parts[0][1]
    for part in parts[1:]:
        highest = jnp.maximum(highest, part[1])
    values = total = None
    for value, row_max, row_sum in parts:
        factor = jnp.exp2(row_max - highest)
        values = value * factor if values is None else values + value * factor
        total = row_sum * factor if total is None else total + row_sum * factor
    return values, highest, total


def share_of(ref, stats, head, present):
    value = ref[0:ROWS, head * HD : (head + 1) * HD].astype(jnp.float32)
    row_max = stats[:, head : head + 1]
    row_sum = (
        stats[:, HEADS_HERE + head : HEADS_HERE + head + 1]
        + stats[:, 2 * HEADS_HERE + head : 2 * HEADS_HERE + head + 1]
    )
    return (
        jnp.where(present, value, 0.0),
        jnp.where(present, row_max, LOWEST),
        jnp.where(present, row_sum, 0.0),
    )


def combine_later_kernel(ids, one, two, three, values, sides):
    home = ids[3]
    stats = [stats_of(ref[ROWS : ROWS + STAT, :])[0] for ref in (one, two, three)]
    lane = lax.broadcasted_iota(jnp.int32, (ROWS, HD), 1)
    side = jnp.zeros((ROWS, HD), jnp.float32)
    for head in range(HEADS_HERE):
        value, row_max, row_sum = merged(
            [
                share_of(one, stats[0], head, home >= 1),
                share_of(two, stats[1], head, home >= 2),
                share_of(three, stats[2], head, home >= 3),
            ]
        )
        values[:, head * HD : (head + 1) * HD] = value
        side = jnp.where(lane == head, row_max, side)
        side = jnp.where(lane == HEADS_HERE + head, row_sum, side)
    sides[...] = side


def combine_later(ids, one, two, three):
    vmem = pl.BlockSpec(memory_space=pltpu.VMEM)
    return pl.pallas_call(
        combine_later_kernel,
        out_shape=[
            jax.ShapeDtypeStruct((ROWS, WIDTH), jnp.float32),
            jax.ShapeDtypeStruct((ROWS, HD), jnp.float32),
        ],
        in_specs=[pl.BlockSpec(memory_space=pltpu.SMEM)] + [vmem] * 3,
        out_specs=[vmem] * 2,
        compiler_params=pltpu.CompilerParams(vmem_limit_bytes=SMALL_VMEM),
        cost_estimate=pl.CostEstimate(
            flops=10**11, bytes_accessed=2 * 10**8, transcendentals=0
        ),
        name="combine_later",
    )(ids, one, two, three)


def combine_kernel(table, zero, values, sides, out, gate):
    own, noise = stats_of(zero[ROWS : ROWS + STAT, :])
    for head in range(HEADS_HERE):
        at = slice(head * HD, (head + 1) * HD)
        value, unused, row_sum = merged(
            [
                share_of(zero, own, head, True),
                (
                    values[:, at],
                    sides[:, head : head + 1],
                    sides[:, HEADS_HERE + head : HEADS_HERE + head + 1],
                ),
            ]
        )
        out[:, at] = (value / row_sum).astype(jnp.bfloat16)
    index = lax.broadcasted_iota(jnp.int32, table.shape, 0).astype(jnp.float32)
    gate[...] = jnp.sum(jnp.where(index == noise, table[...], 0.0), axis=0, keepdims=True)


def combine(table, zero, values, sides):
    vmem = pl.BlockSpec(memory_space=pltpu.VMEM)
    return pl.pallas_call(
        combine_kernel,
        out_shape=[
            jax.ShapeDtypeStruct((ROWS, WIDTH), jnp.bfloat16),
            jax.ShapeDtypeStruct((1, table.shape[1]), jnp.float32),
        ],
        in_specs=[vmem] * 4,
        out_specs=[vmem] * 2,
        compiler_params=pltpu.CompilerParams(vmem_limit_bytes=SMALL_VMEM),
        name="combine",
    )(table, zero, values, sides)


def finish_kernel(hidden, near, arrived, gate, out):
    projected = near[...] + arrived[...].astype(jnp.float32)
    out[...] = (hidden[...].astype(jnp.float32) + gate[...] * projected).astype(jnp.bfloat16)


def finish(hidden, near, arrived, gate):
    part = hidden.shape[1]
    rows = pl.BlockSpec((ROWS // 4, part), lambda i: (i, 0))
    return pl.pallas_call(
        finish_kernel,
        grid=(4,),
        out_shape=jax.ShapeDtypeStruct(hidden.shape, jnp.bfloat16),
        in_specs=[rows, rows, rows, pl.BlockSpec((1, part), lambda i: (0, 0))],
        out_specs=rows,
        compiler_params=pltpu.CompilerParams(vmem_limit_bytes=SMALL_VMEM),
        name="finish",
    )(hidden, near, arrived, gate)


def pack_kernel(keys, values, pair):
    pair[:, :WIDTH] = keys[...]
    pair[:, WIDTH:] = values[...]


def pack(keys, values):
    vmem = pl.BlockSpec(memory_space=pltpu.VMEM)
    return pl.pallas_call(
        pack_kernel,
        out_shape=jax.ShapeDtypeStruct((ROWS, 2 * WIDTH), jnp.bfloat16),
        in_specs=[vmem] * 2,
        out_specs=vmem,
        compiler_params=pltpu.CompilerParams(vmem_limit_bytes=WHOLE_VMEM),
        name="pack",
    )(keys, values)


def copies_kernel(plan, ids, *refs):
    inputs, outs, sem = refs[: plan[0]], refs[plan[0] : -1], refs[-1]
    copies = []
    for n, (kind, source, target, number) in enumerate(plan[1]):
        src, dst = inputs[source], outs[target]
        if kind == "columns":
            width = dst.shape[1]
            src = src.at[:, pl.ds(pl.multiple_of(ids[number] * width, width), width)]
        else:
            dst = dst.at[number]
        copies.append(pltpu.make_async_copy(src, dst, sem.at[n]))
    for copy in copies:
        copy.start()
    for copy in copies:
        copy.wait()


def copied(name, ids, inputs, shapes, plan):
    anywhere = pl.BlockSpec(memory_space=pl.ANY)
    return pl.pallas_call(
        functools.partial(copies_kernel, (len(inputs), plan)),
        out_shape=[jax.ShapeDtypeStruct(shape, jnp.bfloat16) for shape in shapes],
        in_specs=[pl.BlockSpec(memory_space=pltpu.SMEM)] + [anywhere] * len(inputs),
        out_specs=[anywhere] * len(shapes),
        scratch_shapes=[pltpu.SemaphoreType.DMA((len(plan),))],
        compiler_params=pltpu.CompilerParams(vmem_limit_bytes=SMALL_VMEM),
        name=name,
    )(ids, *inputs)


def project_kernel(far, ids, *refs):
    rows, own, fetched, swapped, out, held, sem = refs[0:4], refs[4], refs[5], refs[6], refs[7], refs[8], refs[9]
    mine = ids[2] == (1 if far else 0)

    @pl.when(mine)
    def _():
        pltpu.make_async_copy(fetched, held, sem).start()

    @pl.when(jnp.logical_not(mine))
    def _():
        pltpu.make_async_copy(swapped, held, sem).start()

    pltpu.make_async_copy(fetched, held, sem).wait()
    block = out.shape[1] // 3

    def columns(n, unused):
        at = pl.ds(pl.multiple_of(n * block, block), block)
        total = jnp.dot(rows[0][...], own[:, at], preferred_element_type=jnp.float32)
        for k in range(3):
            total = total + jnp.dot(
                rows[k + 1][...], held[k, :, at], preferred_element_type=jnp.float32
            )
        out[:, at] = total.astype(out.dtype)
        return 0

    lax.fori_loop(0, 3, columns, 0)


def project(far, ids, rows, own, fetched, swapped):
    vmem = pl.BlockSpec(memory_space=pltpu.VMEM)
    anywhere = pl.BlockSpec(memory_space=pl.ANY)
    part = own.shape[1]
    return pl.pallas_call(
        functools.partial(project_kernel, far),
        out_shape=jax.ShapeDtypeStruct((ROWS, part), jnp.bfloat16 if far else jnp.float32),
        in_specs=[pl.BlockSpec(memory_space=pltpu.SMEM)] + [vmem] * 5 + [anywhere] * 2,
        out_specs=vmem,
        scratch_shapes=[pltpu.VMEM((3, WIDTH, part), jnp.bfloat16), pltpu.SemaphoreType.DMA],
        compiler_params=pltpu.CompilerParams(vmem_limit_bytes=SMALL_VMEM),
        cost_estimate=pl.CostEstimate(
            flops=8 * ROWS * WIDTH * part, bytes_accessed=5 * 10**6, transcendentals=0
        ),
        name="project",
    )(ids, *rows, own, fetched, swapped)


def around(value, axis, steps):
    count = lax.axis_size(axis)
    return lax.ppermute(value, axis, [(i, (i + steps) % count) for i in range(count)])


def together(*values):
    return lax.optimization_barrier(values)


def per_device(hidden, queries, key_rows, values, out_weight, level_table, noise_level, group_live):
    z, y, core = lax.axis_index("z"), lax.axis_index("y"), lax.axis_index("c")
    w, x = lax.axis_index("w"), lax.axis_index("x")
    slot = z * 8 + y * 2 + core
    home = lax.rem(slot + 1, 32) // 8
    block = jnp.where(core == 0, w, 1 - w) * 4
    owners = [block + lax.rem(x + step, 4) for step in (1, 2, 3)] + [w * 4 + x, (1 - w) * 4 + x]
    ids = jnp.stack([z, y, core, home, *owners]).astype(jnp.int32)
    column_block = (out_weight.shape[0], out_weight.shape[1] // 8)

    def to_level(value, d):
        return lax.ppermute(value, "z", [(i, i - d) for i in range(d, 4)])

    pair = pack(key_rows, values)
    *pieces, weight_near, weight_far = copied(
        "columns",
        ids,
        [out_weight],
        [column_block] * 5,
        tuple(("columns", 0, k, 4 + k) for k in range(5)),
    )
    next_one, next_three, below, above, pair_there, pair, queries, hidden, *pieces = together(
        to_level(queries, 1),
        to_level(queries, 3),
        around(pair, "y", 1),
        around(pair, "y", -1),
        around(pair, "c", 1),
        pair,
        queries,
        hidden,
        *pieces,
    )
    states = attend(
        "early",
        ids,
        group_live,
        noise_level,
        [next_one, next_three, queries],
        [pair, below, above, None, pair_there],
    )
    next_two, across, piece_one, piece_three, below_there, piece_two, above, *states = together(
        to_level(queries, 2),
        around(pair, "y", 2),
        around(pieces[0], "x", 1),
        around(pieces[2], "x", 3),
        around(below, "c", 1),
        pieces[1],
        above,
        *states,
    )
    above_there, across_there = around(above, "c", 1), around(across, "c", 1)
    pairs = [pair, below, above, across, pair_there, below_there, above_there, across_there]
    piece_two = around(piece_two, "x", 2)

    def back(share, d):
        pairs_back = [
            (8 * (i - d) + j, (8 * i + j - 1) % 32) for i in range(d, 4) for j in range(8)
        ]
        return lax.ppermute(share, SLOT, pairs_back)

    (two,) = attend("third", ids, group_live, noise_level, [next_two], pairs)
    back_two = back(two, 2)
    live_middle, two = together(group_live, two)
    one, three = attend(
        "middle", ids, live_middle, noise_level, [next_one, next_three], pairs, states[0:2]
    )
    back_one, back_three = back(one, 1), back(three, 3)
    live_late, one = together(group_live, one)
    (zero,) = attend("late", ids, live_late, noise_level, [queries], pairs, states[2:4])
    zero, back_two, piece_two = together(zero, back_two, piece_two)
    (fetched,) = copied(
        "stack",
        ids,
        [piece_one, piece_two, piece_three],
        [(3, *column_block)],
        tuple(("stack", k, 0, k) for k in range(3)),
    )
    swapped = around(fetched, "c", 1)
    values_later, sides_later = combine_later(ids, back_one, back_two, back_three)
    attended, gate_row = combine(level_table, back(zero, 0), values_later, sides_later)

    attended, hidden = together(attended, hidden)
    hidden_next = around(hidden, SLOT, -1)
    rows = [attended] + [around(attended, "x", step) for step in (1, 2, 3)]
    far_sum = project(True, ids, rows, weight_far, fetched, swapped)
    arrived = around(far_sum, "w", 1)
    near_sum = project(False, ids, rows, weight_near, fetched, swapped)
    return finish(hidden_next, near_sum, arrived, gate_row)


def solution(mesh):
    fine = Mesh(np.asarray(mesh.devices).reshape(4, 4, 2, 2, 4), ("z", "y", "c", "w", "x"))
    tp = ("w", "x")
    block = P(SLOT, tp)
    in_specs = (block, block, block, block, P(tp, None), P(None, tp), P(SLOT), P())
    return jax.shard_map(
        per_device, mesh=fine, in_specs=in_specs, out_specs=block, check_vma=False
    )
```

```python
import functools
import math

import jax
import jax.numpy as jnp
import numpy as np
from jax import lax
from jax.experimental import pallas as pl
from jax.experimental.pallas import tpu as pltpu
from jax.sharding import Mesh
from jax.sharding import PartitionSpec as P

HD = 128
ROWS = 448
HEADS_HERE = 3
WIDTH = HEADS_HERE * HD
STAT = 32
LOWEST = -(2.0**100)
EXP2_SCALE = HD**-0.5 * math.log2(math.e)
Y_STEPS = (0, -1, 1, 2)
SLOT = ("z", "y", "c")
ATTEND_VMEM = 30 * 1024 * 1024
SMALL_VMEM = 8 * 1024 * 1024
WHOLE_VMEM = 60 * 1024 * 1024


def score(query, key):
    return lax.dot_general(
        query, key, (((1,), (1,)), ((), ())), preferred_element_type=jnp.float32
    )


CALLS = {"early": (1, 3, 0), "third": (2,), "middle": (1, 3), "late": (0,)}
EARLY, LATER, ALL = (0, 1, 2, 4), (3, 5, 6, 7), tuple(range(8))
MEMBERS = {"early": EARLY, "third": ALL, "middle": LATER, "late": LATER}
COSTS = {"early": 10**10, "third": 10**10, "middle": 5 * 10**10, "late": 10**6}


def attend_kernel(call, ids, live, level, *refs):
    steps = CALLS[call]
    many = len(steps)
    early, resumed = call == "early", call in ("middle", "late")
    members = MEMBERS[call]
    refs = list(refs)

    def take(count):
        taken = refs[:count]
        del refs[:count]
        return taken

    query_in, pair_in = take(many), take(len(members))
    state_in = take(2) if resumed else []
    out = take(4 if early else many)
    raw, scaled, pairs, held, acc, top, done, raw_sem, pair_sem, state_sem, out_sem = refs
    here, y, core = ids[0], ids[1], ids[2]
    first = here * 8
    mine = first + y * 2 + core
    groups = {}
    for p in members:
        core_there = core if p < 4 else 1 - core
        groups[p] = first + lax.rem(y + Y_STEPS[p % 4] + 4, 4) * 2 + core_there

    def live_before(group):
        count = jnp.int32(0)
        for p in members:
            count = count + jnp.where(groups[p] < group, live[groups[p]], 0)
        return count

    bound = mine if call == "late" else first + 8
    n_live, n_before = live_before(bound), live_before(mine)
    own_place = jnp.where(live[mine] == 1, n_before, n_live)

    def active(i):
        return here + steps[i] <= 3

    def raw_copy(i):
        return pltpu.make_async_copy(query_in[i], raw.at[i], raw_sem.at[i])

    def place_copy(j, place):
        at = pl.ds(pl.multiple_of(place * ROWS, 64), ROWS)
        return pltpu.make_async_copy(pair_in[j], pairs.at[at], pair_sem.at[place])

    def state_copies():
        return (
            pltpu.make_async_copy(state_in[0], acc, state_sem.at[0]),
            pltpu.make_async_copy(state_in[1], top, state_sem.at[1]),
        )

    def out_copies(part):
        at = pl.ds(0, 2 * ROWS) if part == 0 else pl.ds(2 * ROWS, ROWS)
        return (
            pltpu.make_async_copy(acc.at[:, at], out[2 * part], out_sem.at[2 * part]),
            pltpu.make_async_copy(top.at[:, at], out[2 * part + 1], out_sem.at[2 * part + 1]),
        )

    def share_copy(i):
        return pltpu.make_async_copy(done.at[i], out[i], out_sem.at[i])

    def prepare(i):
        raw_copy(i).wait()
        at = slice(i * ROWS, (i + 1) * ROWS)
        for head in range(HEADS_HERE):
            exact = raw[i, :, head * HD : (head + 1) * HD].astype(jnp.float32) * EXP2_SCALE
            high = exact.astype(jnp.bfloat16)
            scaled[head, at, :HD] = high
            scaled[head, at, HD:] = (exact - high.astype(jnp.float32)).astype(jnp.bfloat16)

    def sweep(start, rows, count, place_of, waits, loop_heads):
        span = slice(start, start + rows)
        chunks = (count + 1) // 2

        def arrive(t):
            if waits:
                for k in (2 * t, 2 * t + 1):

                    @pl.when(k < count)
                    def _():
                        place_copy(0, k).wait()

        def at(k):
            place = place_of(jnp.maximum(jnp.minimum(k, count - 1), 0))
            return pl.ds(pl.multiple_of(place * ROWS, 64), ROWS)

        def columns(base, head):
            if isinstance(head, int):
                return slice(base + head * HD, base + (head + 1) * HD)
            return pl.ds(pl.multiple_of(base + head * HD, HD), HD)

        def scores_of(t, head):
            cols = columns(0, head)
            key = jnp.concatenate([pairs[at(2 * t), cols], pairs[at(2 * t + 1), cols]], axis=0)
            return score(scaled[head, span], jnp.concatenate([key, key], axis=1))

        def absorb(t, head, scores):
            old = top[head, span]
            new = jnp.maximum(old, jnp.max(scores, axis=1, keepdims=True))
            weights = jnp.exp2(scores - jnp.concatenate([new] * (2 * ROWS // HD), axis=1))
            cols = columns(WIDTH, head)
            there = jnp.where(2 * t + 1 < count, 1.0, 0.0).astype(jnp.bfloat16)
            ones = jnp.ones((ROWS, HD), jnp.bfloat16)
            value = jnp.concatenate(
                [
                    jnp.concatenate([pairs[at(2 * t), cols], ones], axis=1),
                    jnp.concatenate([pairs[at(2 * t + 1), cols], ones], axis=1) * there,
                ],
                axis=0,
            )
            weighted = jnp.dot(
                weights.astype(jnp.bfloat16), value, preferred_element_type=jnp.float32
            )
            shrink = jnp.exp2(old - new)
            acc[head, span] = (
                acc[head, span] * jnp.concatenate([shrink, shrink], axis=1) + weighted
            )
            top[head, span] = new

        arrive(0)

        @pl.when(chunks > 0)
        def _():
            held[0:rows] = scores_of(0, 0)

        if loop_heads:

            def unit(u, unused):
                head, t = lax.rem(u, HEADS_HERE), u // HEADS_HERE
                scores = held[0:rows]

                @pl.when(head == 1)
                def _():
                    arrive(t + 1)

                following = jnp.minimum(u + 1, HEADS_HERE * chunks - 1)
                upcoming = scores_of(following // HEADS_HERE, lax.rem(following, HEADS_HERE))
                absorb(t, head, scores)
                held[0:rows] = upcoming
                return 0

            lax.fori_loop(0, HEADS_HERE * chunks, unit, 0)
            return

        def chunk(t, unused):
            scores = held[0:rows]
            following = scores_of(t, 1)
            absorb(t, 0, scores)
            scores = scores_of(t, 2)
            absorb(t, 1, following)
            arrive(t + 1)
            held[0:rows] = scores_of(t + 1, 0)
            absorb(t, 2, scores)
            return 0

        lax.fori_loop(0, chunks, chunk, 0)

    def finish(i, unused):
        span = pl.ds(pl.multiple_of(i * ROWS, 64), ROWS)
        lane = lax.broadcasted_iota(jnp.int32, (ROWS, HD), 1)
        stats = jnp.where(lane == 3 * HEADS_HERE, level[0].astype(jnp.float32), 0.0)
        for head in range(HEADS_HERE):
            exact = top[head, span]
            sent = exact.astype(jnp.bfloat16).astype(jnp.float32)
            factor = jnp.exp2(exact - sent)
            weighted = acc[head, span]
            done[i, 0:ROWS, head * HD : (head + 1) * HD] = (weighted[:, :HD] * factor).astype(
                jnp.bfloat16
            )
            total = weighted[:, HD:] * factor
            high = total.astype(jnp.bfloat16).astype(jnp.float32)
            stats = jnp.where(lane == head, sent, stats)
            stats = jnp.where(lane == HEADS_HERE + head, high, stats)
            stats = jnp.where(lane == 2 * HEADS_HERE + head, total - high, stats)
        flat = jnp.transpose(stats)[:16].astype(jnp.bfloat16)
        done[i, ROWS : ROWS + 16, :] = flat[:, :WIDTH]
        pad = jnp.zeros((16, 2 * WIDTH - ROWS), jnp.bfloat16)
        done[i, ROWS + 16 : ROWS + 32, :] = jnp.concatenate([flat[:, WIDTH:], pad], axis=1)
        for k in range(many):

            @pl.when(i == k)
            def _():
                share_copy(k).start()

        return 0

    def first_sources(waits):
        @pl.when(active(1))
        def _():
            sweep(0, 2 * ROWS, n_live, lambda k: k, waits, True)

        @pl.when(active(0) & jnp.logical_not(active(1)))
        def _():
            sweep(0, ROWS, n_live, lambda k: k, waits, True)

    def run():
        for i in range(many):
            pl.when(active(i))(raw_copy(i).start)
        for j, p in enumerate(members):
            if early and p == 0:
                place_copy(j, own_place).start()
                continue

            @pl.when((live[groups[p]] == 1) & (groups[p] < bound))
            def _():
                place_copy(j, live_before(groups[p])).start()

        if resumed:
            for copy in state_copies():
                copy.start()
        for i in range(many):
            pl.when(active(i))(functools.partial(prepare, i))
        if early:
            place_copy(0, own_place).wait()
            for k in range(len(EARLY)):

                @pl.when((k < n_live) & (k != own_place))
                def _():
                    place_copy(0, k).wait()

        if resumed:
            for copy in state_copies():
                copy.wait()
        else:
            top[...] = jnp.full(top.shape, LOWEST, jnp.float32)
            acc[...] = jnp.zeros(acc.shape, jnp.float32)
        if early:

            first_sources(False)

            @pl.when(active(0))
            def _():
                for copy in out_copies(0):
                    copy.start()

            sweep(
                2 * ROWS,
                ROWS,
                n_before + 1,
                lambda k: jnp.where(k < n_before, k, own_place),
                False,
                False,
            )
            for copy in out_copies(1):
                copy.start()
            for copy in out_copies(1):
                copy.wait()

            @pl.when(active(0))
            def _():
                for copy in out_copies(0):
                    copy.wait()

            return

        if many == 2:
            first_sources(True)
        else:
            sweep(0, ROWS, n_live, lambda k: k, True, False)
        lax.fori_loop(0, jnp.where(active(many - 1), many, 1), finish, 0)
        for i in range(many):
            pl.when(active(i))(share_copy(i).wait)

    if early:
        run()
    else:
        pl.when(active(0))(run)


def attend(call, ids, live, level, queries, pairs, states=()):
    smem = pl.BlockSpec(memory_space=pltpu.SMEM)
    anywhere = pl.BlockSpec(memory_space=pl.ANY)
    bf16, f32 = jnp.bfloat16, jnp.float32
    many = len(CALLS[call])
    members = MEMBERS[call]
    together_rows = 2 * ROWS if call in ("early", "middle") else ROWS

    def state(rows):
        return [(HEADS_HERE, rows, 2 * HD), (HEADS_HERE, rows, HD)]

    if call == "early":
        out_shape = [jax.ShapeDtypeStruct(shape, f32) for shape in state(2 * ROWS) + state(ROWS)]
    else:
        out_shape = [jax.ShapeDtypeStruct((ROWS + STAT, WIDTH), bf16)] * many
    operands = [*queries, *[pairs[p] for p in members], *states]
    rows = many * ROWS
    return pl.pallas_call(
        functools.partial(attend_kernel, call),
        out_shape=out_shape,
        in_specs=[smem] * 3 + [anywhere] * len(operands),
        out_specs=[anywhere] * len(out_shape),
        scratch_shapes=[
            pltpu.VMEM((many, ROWS, WIDTH), bf16),
            pltpu.VMEM((HEADS_HERE, rows, 2 * HD), bf16),
            pltpu.VMEM((8 * ROWS, 2 * WIDTH), bf16),
            pltpu.VMEM((together_rows, 2 * ROWS), f32),
            pltpu.VMEM(state(rows)[0], f32),
            pltpu.VMEM(state(rows)[1], f32),
            pltpu.VMEM((many, ROWS + STAT, WIDTH), bf16),
            pltpu.SemaphoreType.DMA((many,)),
            pltpu.SemaphoreType.DMA((8,)),
            pltpu.SemaphoreType.DMA((2,)),
            pltpu.SemaphoreType.DMA((4,)),
        ],
        compiler_params=pltpu.CompilerParams(vmem_limit_bytes=ATTEND_VMEM),
        cost_estimate=pl.CostEstimate(
            flops=COSTS[call], bytes_accessed=10**6, transcendentals=0
        ),
        name="attend_" + call,
    )(ids, live, level, *operands)


def stats_of(tail):
    tail = tail.astype(jnp.float32)
    flat = jnp.concatenate([tail[0:16], tail[16:32, : ROWS - WIDTH]], axis=1)
    noise = flat[3 * HEADS_HERE : 3 * HEADS_HERE + 1, 0:1]
    padded = jnp.concatenate([flat, jnp.zeros((HD - 16, ROWS), jnp.float32)])
    return jnp.transpose(padded), noise


def merged(parts):
    highest = parts[0][1]
    for part in parts[1:]:
        highest = jnp.maximum(highest, part[1])
    values = total = None
    for value, row_max, row_sum in parts:
        factor = jnp.exp2(row_max - highest)
        values = value * factor if values is None else values + value * factor
        total = row_sum * factor if total is None else total + row_sum * factor
    return values, highest, total


def share_of(ref, stats, head, present):
    value = ref[0:ROWS, head * HD : (head + 1) * HD].astype(jnp.float32)
    row_max = stats[:, head : head + 1]
    row_sum = (
        stats[:, HEADS_HERE + head : HEADS_HERE + head + 1]
        + stats[:, 2 * HEADS_HERE + head : 2 * HEADS_HERE + head + 1]
    )
    return (
        jnp.where(present, value, 0.0),
        jnp.where(present, row_max, LOWEST),
        jnp.where(present, row_sum, 0.0),
    )


def combine_later_kernel(ids, one, two, three, values, sides):
    home = ids[3]
    stats = [stats_of(ref[ROWS : ROWS + STAT, :])[0] for ref in (one, two, three)]
    lane = lax.broadcasted_iota(jnp.int32, (ROWS, HD), 1)
    side = jnp.zeros((ROWS, HD), jnp.float32)
    for head in range(HEADS_HERE):
        value, row_max, row_sum = merged(
            [
                share_of(one, stats[0], head, home >= 1),
                share_of(two, stats[1], head, home >= 2),
                share_of(three, stats[2], head, home >= 3),
            ]
        )
        values[:, head * HD : (head + 1) * HD] = value
        side = jnp.where(lane == head, row_max, side)
        side = jnp.where(lane == HEADS_HERE + head, row_sum, side)
    sides[...] = side


def combine_later(ids, one, two, three):
    vmem = pl.BlockSpec(memory_space=pltpu.VMEM)
    return pl.pallas_call(
        combine_later_kernel,
        out_shape=[
            jax.ShapeDtypeStruct((ROWS, WIDTH), jnp.float32),
            jax.ShapeDtypeStruct((ROWS, HD), jnp.float32),
        ],
        in_specs=[pl.BlockSpec(memory_space=pltpu.SMEM)] + [vmem] * 3,
        out_specs=[vmem] * 2,
        compiler_params=pltpu.CompilerParams(vmem_limit_bytes=SMALL_VMEM),
        cost_estimate=pl.CostEstimate(
            flops=10**11, bytes_accessed=2 * 10**8, transcendentals=0
        ),
        name="combine_later",
    )(ids, one, two, three)


def combine_kernel(table, zero, values, sides, out, gate):
    own, noise = stats_of(zero[ROWS : ROWS + STAT, :])
    for head in range(HEADS_HERE):
        at = slice(head * HD, (head + 1) * HD)
        value, unused, row_sum = merged(
            [
                share_of(zero, own, head, True),
                (
                    values[:, at],
                    sides[:, head : head + 1],
                    sides[:, HEADS_HERE + head : HEADS_HERE + head + 1],
                ),
            ]
        )
        out[:, at] = (value / row_sum).astype(jnp.bfloat16)
    index = lax.broadcasted_iota(jnp.int32, table.shape, 0).astype(jnp.float32)
    gate[...] = jnp.sum(jnp.where(index == noise, table[...], 0.0), axis=0, keepdims=True)


def combine(table, zero, values, sides):
    vmem = pl.BlockSpec(memory_space=pltpu.VMEM)
    return pl.pallas_call(
        combine_kernel,
        out_shape=[
            jax.ShapeDtypeStruct((ROWS, WIDTH), jnp.bfloat16),
            jax.ShapeDtypeStruct((1, table.shape[1]), jnp.float32),
        ],
        in_specs=[vmem] * 4,
        out_specs=[vmem] * 2,
        compiler_params=pltpu.CompilerParams(vmem_limit_bytes=SMALL_VMEM),
        name="combine",
    )(table, zero, values, sides)


def finish_kernel(hidden, near, arrived, gate, out):
    projected = near[...] + arrived[...].astype(jnp.float32)
    out[...] = (hidden[...].astype(jnp.float32) + gate[...] * projected).astype(jnp.bfloat16)


def finish(hidden, near, arrived, gate):
    part = hidden.shape[1]
    rows = pl.BlockSpec((ROWS // 2, part), lambda i: (i, 0))
    return pl.pallas_call(
        finish_kernel,
        grid=(2,),
        out_shape=jax.ShapeDtypeStruct(hidden.shape, jnp.bfloat16),
        in_specs=[rows, rows, rows, pl.BlockSpec((1, part), lambda i: (0, 0))],
        out_specs=rows,
        compiler_params=pltpu.CompilerParams(vmem_limit_bytes=SMALL_VMEM),
        name="finish",
    )(hidden, near, arrived, gate)


def pack_kernel(keys, values, pair):
    pair[:, :WIDTH] = keys[...]
    pair[:, WIDTH:] = values[...]


def pack(keys, values):
    return pl.pallas_call(
        pack_kernel,
        grid=(2,),
        out_shape=jax.ShapeDtypeStruct((ROWS, 2 * WIDTH), jnp.bfloat16),
        in_specs=[pl.BlockSpec((ROWS // 2, WIDTH), lambda i: (i, 0))] * 2,
        out_specs=pl.BlockSpec((ROWS // 2, 2 * WIDTH), lambda i: (i, 0)),
        compiler_params=pltpu.CompilerParams(vmem_limit_bytes=WHOLE_VMEM),
        name="pack",
    )(keys, values)


def copies_kernel(plan, ids, *refs):
    inputs, outs, sem = refs[: plan[0]], refs[plan[0] : -1], refs[-1]
    copies = []
    for n, (kind, source, target, number) in enumerate(plan[1]):
        src, dst = inputs[source], outs[target]
        if kind == "columns":
            width = dst.shape[1]
            src = src.at[:, pl.ds(pl.multiple_of(ids[number] * width, width), width)]
        else:
            dst = dst.at[number]
        copies.append(pltpu.make_async_copy(src, dst, sem.at[n]))
    for copy in copies:
        copy.start()
    for copy in copies:
        copy.wait()


def copied(name, ids, inputs, shapes, plan):
    anywhere = pl.BlockSpec(memory_space=pl.ANY)
    return pl.pallas_call(
        functools.partial(copies_kernel, (len(inputs), plan)),
        out_shape=[jax.ShapeDtypeStruct(shape, jnp.bfloat16) for shape in shapes],
        in_specs=[pl.BlockSpec(memory_space=pltpu.SMEM)] + [anywhere] * len(inputs),
        out_specs=[anywhere] * len(shapes),
        scratch_shapes=[pltpu.SemaphoreType.DMA((len(plan),))],
        compiler_params=pltpu.CompilerParams(vmem_limit_bytes=SMALL_VMEM),
        name=name,
    )(ids, *inputs)


def project_kernel(far, ids, *refs):
    rows, own, fetched, swapped, out, held, sem = refs[0:4], refs[4], refs[5], refs[6], refs[7], refs[8], refs[9]
    mine = ids[2] == (1 if far else 0)

    @pl.when(mine)
    def _():
        pltpu.make_async_copy(fetched, held, sem).start()

    @pl.when(jnp.logical_not(mine))
    def _():
        pltpu.make_async_copy(swapped, held, sem).start()

    pltpu.make_async_copy(fetched, held, sem).wait()
    block = out.shape[1] // 3

    def columns(n, unused):
        at = pl.ds(pl.multiple_of(n * block, block), block)
        total = jnp.dot(rows[0][...], own[:, at], preferred_element_type=jnp.float32)
        for k in range(3):
            total = total + jnp.dot(
                rows[k + 1][...], held[k, :, at], preferred_element_type=jnp.float32
            )
        out[:, at] = total.astype(out.dtype)
        return 0

    lax.fori_loop(0, 3, columns, 0)


def project(far, ids, rows, own, fetched, swapped):
    vmem = pl.BlockSpec(memory_space=pltpu.VMEM)
    anywhere = pl.BlockSpec(memory_space=pl.ANY)
    part = own.shape[1]
    return pl.pallas_call(
        functools.partial(project_kernel, far),
        out_shape=jax.ShapeDtypeStruct((ROWS, part), jnp.bfloat16 if far else jnp.float32),
        in_specs=[pl.BlockSpec(memory_space=pltpu.SMEM)] + [vmem] * 5 + [anywhere] * 2,
        out_specs=vmem,
        scratch_shapes=[pltpu.VMEM((3, WIDTH, part), jnp.bfloat16), pltpu.SemaphoreType.DMA],
        compiler_params=pltpu.CompilerParams(vmem_limit_bytes=SMALL_VMEM),
        cost_estimate=pl.CostEstimate(
            flops=8 * ROWS * WIDTH * part, bytes_accessed=5 * 10**6, transcendentals=0
        ),
        name="project",
    )(ids, *rows, own, fetched, swapped)


def around(value, axis, steps):
    count = lax.axis_size(axis)
    return lax.ppermute(value, axis, [(i, (i + steps) % count) for i in range(count)])


def together(*values):
    return lax.optimization_barrier(values)


def per_device(hidden, queries, key_rows, values, out_weight, level_table, noise_level, group_live):
    z, y, core = lax.axis_index("z"), lax.axis_index("y"), lax.axis_index("c")
    w, x = lax.axis_index("w"), lax.axis_index("x")
    slot = z * 8 + y * 2 + core
    home = lax.rem(slot + 1, 32) // 8
    block = jnp.where(core == 0, w, 1 - w) * 4
    owners = [block + lax.rem(x + step, 4) for step in (1, 2, 3)] + [w * 4 + x, (1 - w) * 4 + x]
    ids = jnp.stack([z, y, core, home, *owners]).astype(jnp.int32)
    column_block = (out_weight.shape[0], out_weight.shape[1] // 8)

    def to_level(value, d):
        return lax.ppermute(value, "z", [(i, i - d) for i in range(d, 4)])

    pair = pack(key_rows, values)
    *pieces, weight_near, weight_far = copied(
        "columns",
        ids,
        [out_weight],
        [column_block] * 5,
        tuple(("columns", 0, k, 4 + k) for k in range(5)),
    )
    next_one, next_three, below, above, pair_there, pair, queries, hidden, *pieces = together(
        to_level(queries, 1),
        to_level(queries, 3),
        around(pair, "y", 1),
        around(pair, "y", -1),
        around(pair, "c", 1),
        pair,
        queries,
        hidden,
        *pieces,
    )
    states = attend(
        "early",
        ids,
        group_live,
        noise_level,
        [next_one, next_three, queries],
        [pair, below, above, None, pair_there],
    )
    next_two, across, piece_one, piece_three, below_there, piece_two, above, *states = together(
        to_level(queries, 2),
        around(pair, "y", 2),
        around(pieces[0], "x", 1),
        around(pieces[2], "x", 3),
        around(below, "c", 1),
        pieces[1],
        above,
        *states,
    )
    above_there, across_there = around(above, "c", 1), around(across, "c", 1)
    pairs = [pair, below, above, across, pair_there, below_there, above_there, across_there]
    piece_two = around(piece_two, "x", 2)

    def back(share, d):
        pairs_back = [
            (8 * (i - d) + j, (8 * i + j - 1) % 32) for i in range(d, 4) for j in range(8)
        ]
        return lax.ppermute(share, SLOT, pairs_back)

    (two,) = attend("third", ids, group_live, noise_level, [next_two], pairs)
    back_two = back(two, 2)
    live_middle, two = together(group_live, two)
    one, three = attend(
        "middle", ids, live_middle, noise_level, [next_one, next_three], pairs, states[0:2]
    )
    back_one, back_three = back(one, 1), back(three, 3)
    live_late, one = together(group_live, one)
    (zero,) = attend("late", ids, live_late, noise_level, [queries], pairs, states[2:4])
    zero, back_two, piece_two = together(zero, back_two, piece_two)
    (fetched,) = copied(
        "stack",
        ids,
        [piece_one, piece_two, piece_three],
        [(3, *column_block)],
        tuple(("stack", k, 0, k) for k in range(3)),
    )
    swapped = around(fetched, "c", 1)
    values_later, sides_later = combine_later(ids, back_one, back_two, back_three)
    attended, gate_row = combine(level_table, back(zero, 0), values_later, sides_later)

    attended, hidden = together(attended, hidden)
    hidden_next = around(hidden, SLOT, -1)
    rows = [attended] + [around(attended, "x", step) for step in (1, 2, 3)]
    far_sum = project(True, ids, rows, weight_far, fetched, swapped)
    arrived = around(far_sum, "w", 1)
    near_sum = project(False, ids, rows, weight_near, fetched, swapped)
    return finish(hidden_next, near_sum, arrived, gate_row)


def solution(mesh):
    fine = Mesh(np.asarray(mesh.devices).reshape(4, 4, 2, 2, 4), ("z", "y", "c", "w", "x"))
    tp = ("w", "x")
    block = P(SLOT, tp)
    in_specs = (block, block, block, block, P(tp, None), P(None, tp), P(SLOT), P())
    return jax.shard_map(
        per_device, mesh=fine, in_specs=in_specs, out_specs=block, check_vma=False
    )
```
